128 devices in a mesh: rep: 8 (over x, core), ctx: 16 (over y, z).
Axes of the slice: x: 4, y: 4, z: 4, core: 2. Of those that a mesh axis runs over, the one named last changes fastest.
Arguments:
- queries: bfloat16 [8, 16384, 512], P('rep', 'ctx'), may hold values from -6 to 6
- key_states: bfloat16 [8, 16384, 512], P('rep', 'ctx'), may hold values from -6 to 6
- value_states: bfloat16 [8, 16384, 512], P('rep', 'ctx'), may hold values from -6 to 6
- grad_out: bfloat16 [8, 16384, 1024], P('rep', 'ctx'), may hold values from -6 to 6
- out_weight: bfloat16 [512, 1024], replicated, may hold values from -0.25 to 0.25
Outputs:
- outputs: bfloat16 [8, 16384, 1024], P('rep', 'ctx')
- grad_queries: bfloat16 [8, 16384, 512], P('rep', 'ctx')
- grad_keys: bfloat16 [8, 16384, 512], P('rep', 'ctx')
- grad_values: bfloat16 [8, 16384, 512], P('rep', 'ctx')
- grad_weight: float32 [512, 1024], P('ctx', 'rep')
The draws below stay inside these ranges and needn't reach their ends.
All inputs are finite; a program needn't handle non-finite values.
Results may differ from the reference program's by a relative error of at most 0.012.
Values may be sent and summed in bfloat16 or wider, within the bound.
No kernel may reach another device: no remote copies, remote signals or barrier semaphores. Data moves between devices by JAX's collectives and lax.ppermute only.
A program may use at most 320 MiB of HBM per device.

```python
from functools import reduce
import jax
import jax.numpy as jnp
from jax import lax

D = 1024
HEADS = 8
HDIM = 64
BLOCK = 1024
SEQ_LEN = 16384
SEQS = 8
LEVELS = 4


def draw_queries(key, part):
    key = jax.random.fold_in(key, 11)
    full_shape = (SEQS, SEQ_LEN, HEADS * HDIM)
    samples = jnp.clip(jax.random.normal(key, full_shape, jnp.float32), -6.0, 6.0)
    return samples.astype(jnp.bfloat16)


def draw_key_states(key, part):
    key = jax.random.fold_in(key, 12)
    full_shape = (SEQS, SEQ_LEN, HEADS * HDIM)
    samples = jnp.clip(jax.random.normal(key, full_shape, jnp.float32), -6.0, 6.0)
    return samples.astype(jnp.bfloat16)


def with_spikes(result, key, source, target, parts, factor):
    def block_of(axis_at):
        return (jnp.arange(result.shape[axis_at]) // (result.shape[axis_at] // parts)).reshape((-1,) + (1,) * (result.ndim - 1 - axis_at))

    one_side = jax.random.permutation(key, parts)[block_of(target)]
    far = (block_of(target) + parts // 2) % parts
    return jnp.where((block_of(source) == one_side) | (block_of(source) == far), factor * result, result)


def shard_levels(rng, extent, shards, low, largest):
    loudness, own = 1.0, jax.random.fold_in(rng, 6)
    for dim, shards_of in shards:
        heights = jnp.exp(jax.random.uniform(jax.random.fold_in(own, dim), (shards_of,), jnp.float32, low / len(shards), largest / len(shards)))
        loudness = loudness * jnp.repeat(heights, extent[dim] // shards_of).reshape([-1 if axis == dim else 1 for axis in range(len(extent))])
    return loudness


def centred(stream_key, shape, width, bound, shards=(), dtype=jnp.bfloat16):
    factor_of = shard_levels(stream_key, shape, shards, -0.22, 0.18) if shards else 1.0
    array = jax.random.normal(stream_key, shape, jnp.float32) * width * factor_of
    return jnp.minimum(jnp.maximum(array, -bound), bound).astype(dtype)


def noise_with(own_key, extent, deviation, reach, pieces, heavy, held_as=jnp.bfloat16):
    array = deviation * jax.random.normal(own_key, extent, jnp.float32)
    if pieces:
        array = array * shard_levels(own_key, extent, pieces, -0.22, 0.18)
    return jnp.clip(with_spikes(array, jax.random.fold_in(own_key, 3), *heavy), -reach, reach).astype(held_as)


def setup_inputs(seed: int = 0) -> dict:
    key_list = jax.random.split(jax.random.key(seed), 6)
    return {
        "queries": draw_queries(jax.random.fold_in(key_list[5], 71), 0),
        "key_states": draw_key_states(jax.random.fold_in(key_list[5], 71), 0),
        "value_states": centred(key_list[2], (SEQS, SEQ_LEN, HEADS * HDIM), 1.0, 6.0, ((0, 8), (1, 16))),
        "grad_out": noise_with(key_list[3], (SEQS, SEQ_LEN, D), 1.0, 6.0, ((0, 8), (1, 16)), (1, 2, 16, 2.0)),
        "out_weight": centred(key_list[4], (HEADS * HDIM, D), (HEADS * HDIM) ** -0.5, 0.25),
    }


SCALE = 0.125


def pool_pairs(matrix):
    paired = matrix.astype(jnp.float32).reshape(matrix.shape[0] // 2, 2, matrix.shape[1])
    return (0.5 * (paired[:, 0] + paired[:, 1])).astype(jnp.bfloat16)


def split_heads(matrix):
    return matrix.astype(jnp.float32).reshape(matrix.shape[0], HEADS, HDIM)


def rounded(matrix):
    return lax.optimization_barrier(matrix.astype(jnp.bfloat16)).astype(jnp.float32)


def block_forward(operands):
    query_rows, key_rows, value_rows = operands
    query_heads = split_heads(query_rows)
    key_heads = split_heads(key_rows)
    value_heads = split_heads(value_rows)
    scores = jnp.einsum("phd,rhd->hpr", query_heads, key_heads) * SCALE
    row_max = jnp.max(scores, axis=2)
    exponent = jnp.exp(scores - row_max[:, :, None])
    totals = jnp.sum(exponent, axis=2)
    weighted = jnp.einsum("hpr,rhd->hpd", rounded(exponent), value_heads)
    return row_max, totals, weighted


def block_backward(operands):
    query_rows, key_rows, value_rows, row_max, grad_rows, grad_scale = operands
    query_heads = split_heads(query_rows)
    key_heads = split_heads(key_rows)
    value_heads = split_heads(value_rows)
    grad_heads = split_heads(grad_rows)
    scores = jnp.einsum("phd,rhd->hpr", query_heads, key_heads) * SCALE
    exponent = jnp.exp(scores - row_max[:, :, None])
    soft_weights = rounded(exponent)
    grad_prob = jnp.einsum("phd,rhd->hpr", grad_heads, value_heads)
    grad_score = rounded(exponent * (grad_prob - grad_scale[:, :, None]))
    grad_query = SCALE * jnp.einsum("hpr,rhd->phd", grad_score, key_heads)
    grad_key = SCALE * jnp.einsum("hpr,phd->rhd", grad_score, query_heads)
    grad_value = jnp.einsum("hpr,phd->rhd", soft_weights, grad_heads)
    full_width = HEADS * HDIM
    return (grad_query.reshape(query_rows.shape[0], full_width),
            grad_key.reshape(key_rows.shape[0], full_width),
            grad_value.reshape(key_rows.shape[0], full_width))


def level_blocks(matrix, level_id):
    if level_id == 0:
        return matrix.reshape(-1, 2 * BLOCK, matrix.shape[1])
    return matrix.reshape(-1, BLOCK, matrix.shape[1])


def swap_blocks(blocks, level_id):
    if level_id == 0:
        return blocks
    return jnp.flip(blocks.reshape(-1, 2, BLOCK, blocks.shape[2]), 1).reshape(blocks.shape)


def heads_first(stat):
    return jnp.moveaxis(stat, 0, 1).reshape(HEADS, -1)


def heads_first_wide(stat):
    return jnp.moveaxis(stat, 0, 1).reshape(HEADS, -1, HDIM)


def one_sequence(query_seq, key_seq, value_seq, grad_seq, out_weight):
    query_pyr = [query_seq]
    key_pyr = [key_seq]
    value_pyr = [value_seq]
    for level_id in range(1, LEVELS):
        query_pyr.append(pool_pairs(query_pyr[-1]))
        key_pyr.append(pool_pairs(key_pyr[-1]))
        value_pyr.append(pool_pairs(value_pyr[-1]))
    fine_rows = query_seq.shape[0]
    full_width = HEADS * HDIM
    kept_blocks = []
    maxima = []
    row_totals = []
    products = []
    for level_id in range(LEVELS):
        repeat_by = 2 ** level_id
        query_blocks = level_blocks(query_pyr[level_id], level_id)
        key_blocks = swap_blocks(level_blocks(key_pyr[level_id], level_id), level_id)
        value_blocks = swap_blocks(level_blocks(value_pyr[level_id], level_id), level_id)
        row_max, totals, weighted = lax.map(block_forward, (query_blocks, key_blocks, value_blocks))
        kept_blocks.append((query_blocks, key_blocks, value_blocks, row_max))
        maxima.append(jnp.repeat(heads_first(row_max), repeat_by, axis=1))
        row_totals.append(jnp.repeat(heads_first(totals), repeat_by, axis=1))
        products.append(jnp.repeat(heads_first_wide(weighted), repeat_by, axis=1))
    joint_max = reduce(jnp.maximum, maxima)
    factors = [2.0 ** level_id * jnp.exp(maxima[level_id] - joint_max) for level_id in range(LEVELS)]
    totals_all = factors[0] * row_totals[0]
    combined = factors[0][:, :, None] * products[0]
    for level_id in range(1, LEVELS):
        totals_all = totals_all + factors[level_id] * row_totals[level_id]
        combined = combined + factors[level_id][:, :, None] * products[level_id]
    attn_heads = combined / totals_all[:, :, None]
    attention = jnp.moveaxis(attn_heads, 0, 1).reshape(fine_rows, full_width).astype(jnp.bfloat16)
    outputs = jnp.dot(attention, out_weight, preferred_element_type=jnp.float32).astype(jnp.bfloat16)
    grad_attn = jnp.dot(grad_seq, out_weight.T, preferred_element_type=jnp.float32).astype(jnp.bfloat16)
    grad_heads = split_heads(grad_attn)
    row_delta = jnp.sum(grad_heads * split_heads(attention), axis=2).T
    grad_query = jnp.zeros((fine_rows, full_width), jnp.float32)
    grad_key = jnp.zeros((fine_rows, full_width), jnp.float32)
    grad_value = jnp.zeros((fine_rows, full_width), jnp.float32)
    for level_id in range(LEVELS):
        repeat_by = 2 ** level_id
        coarse_rows = fine_rows // repeat_by
        row_share = factors[level_id] / totals_all
        grad_level = (row_share.T[:, :, None] * grad_heads).reshape(coarse_rows, repeat_by, HEADS, HDIM)
        grad_level = grad_level.sum(axis=1).reshape(coarse_rows, full_width).astype(jnp.bfloat16)
        grad_scale = (row_share * row_delta).reshape(HEADS, coarse_rows, repeat_by).sum(axis=2)
        query_blocks, key_blocks, value_blocks, row_max = kept_blocks[level_id]
        block_rows = query_blocks.shape[1]
        scale_blocks = jnp.moveaxis(grad_scale.reshape(HEADS, -1, block_rows), 1, 0)
        part_query, part_key, part_value = lax.map(
            block_backward,
            (query_blocks, key_blocks, value_blocks, row_max, level_blocks(grad_level, level_id), scale_blocks))
        part_query = part_query.reshape(coarse_rows, full_width)
        part_key = swap_blocks(part_key, level_id).reshape(coarse_rows, full_width)
        part_value = swap_blocks(part_value, level_id).reshape(coarse_rows, full_width)
        grad_query = grad_query + jnp.repeat(part_query, repeat_by, axis=0) / repeat_by
        grad_key = grad_key + jnp.repeat(part_key, repeat_by, axis=0) / repeat_by
        grad_value = grad_value + jnp.repeat(part_value, repeat_by, axis=0) / repeat_by
    weight_term = lax.dot_general(attention, grad_seq, (((0,), (0,)), ((), ())), preferred_element_type=jnp.float32)
    return (outputs, grad_query.astype(jnp.bfloat16), grad_key.astype(jnp.bfloat16),
            grad_value.astype(jnp.bfloat16), weight_term)


def reference(queries, key_states, value_states, grad_out, out_weight):
    def per_sequence(operands):
        return one_sequence(operands[0], operands[1], operands[2], operands[3], out_weight)

    outputs, grad_queries, grad_keys, grad_values, weight_terms = lax.map(
        per_sequence, (queries, key_states, value_states, grad_out))
    return outputs, grad_queries, grad_keys, grad_values, jnp.sum(weight_terms, axis=0)
```

```python
import functools

import jax
import jax.numpy as jnp
from jax import lax
from jax.experimental import pallas as pl
from jax.experimental.pallas import tpu as pltpu
from jax.sharding import PartitionSpec as P

F32=jnp.float32; BF=jnp.bfloat16
KEYS=1024; SLAB=128; TW=256
NT=(((1,),(1,)),((),()))
NN=(((1,),(0,)),((),()))
LOG2E=1.4426950408889634
TILES=23
BLK=[(0,0,8),(1,8,8),(2,16,4),(3,20,2),(4,22,1)]

def dot(a,b,dims=NN):
    return lax.dot_general(a,b,dims,preferred_element_type=F32)

def kernel(q_ref, ga_ref, kv0,kv1,kv2,kv3,kv4, attn_ref, dq_ref, g0,g1,g2,g3,g4,
           kk,va,kT,vT,qw,qk,gw,gk,p_ref,ds_ref,w_ref,st_ref,s_ref,dqt_ref):
    kvs=[kv0,kv1,kv2,kv3,kv4]
    gouts=[g0,g1,g2,g3,g4]
    ones3=(lax.broadcasted_iota(jnp.int32,(KEYS,64),1)<3).astype(F32).astype(BF)
    for b in range(5):
        k=kvs[b][:,0:128]; v=kvs[b][:,128:256]
        k0=k[:,0:64]; k1=k[:,64:128]; v0=v[:,0:64]; v1=v[:,64:128]
        kk[b]=jnp.concatenate([k0,k0,k1,k1],1)
        va[b]=jnp.concatenate([v0,ones3,v1,ones3],1)
        kT[b]=k.T
        vT[b,0:128]=v.T
        vT[b,128:144]=(lax.broadcasted_iota(jnp.int32,(16,KEYS),0)==0).astype(F32).astype(BF)
    zero=jnp.zeros((64,SLAB),BF)
    def put_q(t,q):
        qs=q.astype(F32)*(0.125*LOG2E)
        hi=qs.astype(BF); lo=(qs-hi.astype(F32)).astype(BF)
        qw[t,0:64,0:128]=hi[0:64]; qw[t,64:128,0:128]=lo[0:64]
        qw[t,128:192,0:128]=zero; qw[t,192:256,0:128]=zero
        qw[t,0:64,128:256]=zero; qw[t,64:128,128:256]=zero
        qw[t,128:192,128:256]=hi[64:128]; qw[t,192:256,128:256]=lo[64:128]
        qq=(q.astype(F32)*0.125).astype(BF)
        qk[0:64,t*TW:t*TW+128]=qq[0:64]; qk[64:128,t*TW:t*TW+128]=zero
        qk[0:64,t*TW+128:t*TW+256]=zero; qk[64:128,t*TW+128:t*TW+256]=qq[64:128]
    level=[q_ref[:,j*SLAB:(j+1)*SLAB] for j in range(8)]
    for j in range(8):
        put_q(j,level[j]);
    for l,first in ((1,16),(2,20),(3,22)):
        level=[(0.5*(level[2*c].astype(F32)+level[2*c+1].astype(F32))).astype(BF) for c in range(len(level)//2)]
        for c,x in enumerate(level): put_q(first+c,x)

    def fwd(t,b,tq):
        s=dot(kk[b],qw[tq])
        s_ref[...]=s
        m=jnp.max(s_ref[...],axis=0,keepdims=True)
        p=jnp.exp2(s_ref[...]-m).astype(BF)
        off=pl.multiple_of(t*TW,TW)
        p_ref[:,pl.ds(off,TW)]=p
        w=dot(vT[b],p)
        w_ref[t]=jnp.concatenate([w[0:64,0:128],w[64:128,128:256]],1)
        st_ref[t,0:1]=m
        st_ref[t,1:2]=w[128:129]
    for b,first,n in BLK:
        def body(i,c,b=b,first=first):
            fwd(first+i,b,i if b==1 else first+i)
            return c
        lax.fori_loop(0,n,body,0)

    gl=[None]*TILES; gs=[None]*TILES
    def acc(lst,i,x): lst[i]=x if lst[i] is None else lst[i]+x
    for j in range(8):
        ts=[j,8+j,16+j//2,20+j//4,22]
        ms=[st_ref[t,0:1] for t in ts]; tt=[st_ref[t,1:2] for t in ts]
        mx=functools.reduce(jnp.maximum,ms)
        fs=[jnp.exp2(m-mx)*w for m,w in zip(ms,(1.,1.,2.,4.,8.))]
        tot=functools.reduce(jnp.add,[f*x for f,x in zip(fs,tt)])
        inv=1.0/tot
        sh=[f*inv for f in fs]
        at=functools.reduce(jnp.add,[s*w_ref[t] for s,t in zip(sh,ts)])
        atb=at.astype(BF)
        attn_ref[0:64,j*SLAB:(j+1)*SLAB]=atb[:,0:128]
        attn_ref[64:128,j*SLAB:(j+1)*SLAB]=atb[:,128:256]
        ga=jnp.concatenate([ga_ref[0:64,j*SLAB:(j+1)*SLAB],ga_ref[64:128,j*SLAB:(j+1)*SLAB]],1).astype(F32)
        delta=jnp.sum(ga*atb.astype(F32),axis=0,keepdims=True)
        for s,t in zip(sh,ts):
            acc(gl,t,s*ga); acc(gs,t,s*delta)
    z64=jnp.zeros((64,SLAB),BF); z48=jnp.zeros((48,SLAB),BF)
    for t in range(TILES):
        g=gl[t].astype(BF)
        n=-gs[t]
        hi=n.astype(BF).astype(F32); r=n-hi; mid=r.astype(BF).astype(F32); lo=r-mid
        row=lax.broadcasted_iota(jnp.int32,(16,TW),0)
        gsb=jnp.where(row==0,hi,jnp.where(row==1,mid,jnp.where(row==2,lo,0.0))).astype(BF)
        gw[t,0:64,0:128]=g[:,0:128]; gw[t,64:80,0:128]=gsb[:,0:128]; gw[t,80:128,0:128]=z48
        gw[t,128:192,0:128]=z64; gw[t,192:256,0:128]=z64
        gw[t,0:64,128:256]=z64; gw[t,64:128,128:256]=z64
        gw[t,128:192,128:256]=g[:,128:256]; gw[t,192:208,128:256]=gsb[:,128:256]; gw[t,208:256,128:256]=z48
        gk[0:64,t*TW:t*TW+128]=g[:,0:128]; gk[64:128,t*TW:t*TW+128]=z64
        gk[0:64,t*TW+128:t*TW+256]=z64; gk[64:128,t*TW+128:t*TW+256]=g[:,128:256]

    for b,first,n in BLK:
        qoff=0 if b==1 else first
        def body(i,c,b=b,first=first):
            t=first+i
            off=pl.multiple_of(t*TW,TW)
            dp=dot(va[b],gw[t])
            ds=(p_ref[:,pl.ds(off,TW)].astype(F32)*dp).astype(BF)
            ds_ref[:,pl.ds(pl.multiple_of(i*TW,TW),TW)]=ds
            dq=dot(kT[b],ds)
            dqt_ref[t]=jnp.concatenate([dq[0:64,0:128],dq[64:128,128:256]],1)
            return c
        lax.fori_loop(0,n,body,0)
        def body2(i,c,b=b,first=first,n=n,qoff=qoff):
            rows=pl.ds(pl.multiple_of(i*256,256),256)
            dk=dot(ds_ref[rows,0:n*TW],qk[:,qoff*TW:(qoff+n)*TW],NT)
            dv=dot(p_ref[rows,first*TW:(first+n)*TW],gk[:,first*TW:(first+n)*TW],NT)
            gouts[b][rows,0:128]=dk.astype(gouts[b].dtype)
            gouts[b][rows,128:256]=dv.astype(gouts[b].dtype)
            return c
        lax.fori_loop(0,4,body2,0)
    for j in range(8):
        d=0.125*(dqt_ref[j]+dqt_ref[8+j]+0.5*dqt_ref[16+j//2]+0.25*dqt_ref[20+j//4]+0.125*dqt_ref[22])
        d=d.astype(BF)
        dq_ref[0:64,j*SLAB:(j+1)*SLAB]=d[:,0:128]
        dq_ref[64:128,j*SLAB:(j+1)*SLAB]=d[:,128:256]

def main(g,qT,gaT,kvs,gdt=F32):
    spec=lambda: pl.BlockSpec((KEYS,256),lambda i:(0,0))
    colspec=pl.BlockSpec((128,KEYS),lambda i:(g,0))
    return pl.pallas_call(kernel,grid=(1,),
        in_specs=[colspec,colspec]+[spec()]*5,
        out_specs=[pl.BlockSpec((128,KEYS),lambda i:(0,0))]*2+[spec()]*5,
        out_shape=[jax.ShapeDtypeStruct((128,KEYS),BF)]*2+[jax.ShapeDtypeStruct((KEYS,256),F32)]+[jax.ShapeDtypeStruct((KEYS,256),gdt)]*4,
        scratch_shapes=[pltpu.VMEM((5,KEYS,256),BF),pltpu.VMEM((5,KEYS,256),BF),pltpu.VMEM((5,128,KEYS),BF),pltpu.VMEM((5,144,KEYS),BF),
          pltpu.VMEM((TILES,256,TW),BF),pltpu.VMEM((128,TILES*TW),BF),pltpu.VMEM((TILES,256,TW),BF),pltpu.VMEM((128,TILES*TW),BF),
          pltpu.VMEM((KEYS,TILES*TW),BF),pltpu.VMEM((KEYS,8*TW),BF),pltpu.VMEM((TILES,64,TW),F32),pltpu.VMEM((TILES,8,TW),F32),
          pltpu.VMEM((KEYS,TW),F32),pltpu.VMEM((TILES,64,TW),F32)],
        compiler_params=pltpu.CompilerParams(vmem_limit_bytes=56*2**20),
        name="group")(qT,gaT,*kvs)


GROUPS = 4
MASKS = (1, 3, 4, 12)


def to_slabs(src, tmp, width):
    tmp[...] = src[...].astype(F32)
    return [tmp[pl.ds(b, SLAB, stride=8), 0:width] for b in range(8)]


def keys_kernel(k_ref, v_ref, o0, o1, o2, o3, tmp):
    outs = (o0, o1, o2, o3)
    for part, src in enumerate((k_ref, v_ref)):
        for g in range(GROUPS):
            tmp[...] = src[:, g * 128 : (g + 1) * 128].astype(F32)
            for b in range(8):
                outs[g][b * SLAB : (b + 1) * SLAB, part * 128 : (part + 1) * 128] = tmp[
                    pl.ds(b, SLAB, stride=8), :
                ].astype(BF)


def prep_keys(k, v):
    return pl.pallas_call(
        keys_kernel,
        out_shape=[jax.ShapeDtypeStruct((KEYS, 256), BF)] * GROUPS,
        scratch_shapes=[pltpu.VMEM((KEYS, 128), F32)],
        compiler_params=pltpu.CompilerParams(vmem_limit_bytes=32 * 2**20),
        name="prep_keys",
    )(k, v)


def rows_kernel(q_ref, go_ref, w_ref, qT_ref, gaT_ref, gp_ref, tmp):
    for g in range(GROUPS):
        tmp[...] = q_ref[:, g * 128 : (g + 1) * 128].astype(F32)
        for b in range(8):
            x = tmp[pl.ds(b, SLAB, stride=8), :]
            qT_ref[g * 128 : (g + 1) * 128, b * SLAB : (b + 1) * SLAB] = x.T.astype(BF)
    for c in range(8):
        tmp[...] = go_ref[:, c * 128 : (c + 1) * 128].astype(F32)
        for b in range(8):
            gp_ref[b * SLAB : (b + 1) * SLAB, c * 128 : (c + 1) * 128] = tmp[
                pl.ds(b, SLAB, stride=8), :
            ].astype(BF)
    for c in range(4):
        rows = pl.ds(c * 256, 256)
        gaT_ref[:, c * 256 : (c + 1) * 256] = dot(w_ref[...], gp_ref[rows, :], NT).astype(BF)


def prep_rows(q, go, w):
    return pl.pallas_call(
        rows_kernel,
        out_shape=[
            jax.ShapeDtypeStruct((512, KEYS), BF),
            jax.ShapeDtypeStruct((512, KEYS), BF),
            jax.ShapeDtypeStruct((KEYS, 1024), BF),
        ],
        scratch_shapes=[pltpu.VMEM((KEYS, 128), F32)],
        compiler_params=pltpu.CompilerParams(vmem_limit_bytes=40 * 2**20),
        name="prep_rows",
    )(q, go, w)


def project_kernel(a0, a1, a2, a3, gp_ref, w_ref, out_ref, gw_ref, at, tmp):
    attns = (a0, a1, a2, a3)
    for g in range(GROUPS):
        at[:, g * 128 : (g + 1) * 128] = attns[g][...].T
        gw_ref[g * 128 : (g + 1) * 128, :] = dot(attns[g][...], gp_ref[...])
    for c in range(8):
        for b in range(8):
            tmp[pl.ds(b, SLAB, stride=8), :] = dot(
                at[b * SLAB : (b + 1) * SLAB, :], w_ref[:, c * 128 : (c + 1) * 128]
            )
        out_ref[:, c * 128 : (c + 1) * 128] = tmp[...].astype(BF)


def project(attns, gp, w):
    return pl.pallas_call(
        project_kernel,
        out_shape=[
            jax.ShapeDtypeStruct((KEYS, 1024), BF),
            jax.ShapeDtypeStruct((512, 1024), F32),
        ],
        scratch_shapes=[pltpu.VMEM((KEYS, 512), BF), pltpu.VMEM((KEYS, 128), F32)],
        compiler_params=pltpu.CompilerParams(vmem_limit_bytes=40 * 2**20),
        name="project",
    )(*attns, gp, w)


def queries_kernel(d0, d1, d2, d3, out_ref, tmp):
    for g, d in enumerate((d0, d1, d2, d3)):
        for b in range(8):
            tmp[pl.ds(b, SLAB, stride=8), :] = d[:, b * SLAB : (b + 1) * SLAB].astype(F32).T
        out_ref[:, g * 128 : (g + 1) * 128] = tmp[...].astype(BF)


def finish_queries(dqs):
    return pl.pallas_call(
        queries_kernel,
        out_shape=jax.ShapeDtypeStruct((KEYS, 512), BF),
        scratch_shapes=[pltpu.VMEM((KEYS, 128), F32)],
        compiler_params=pltpu.CompilerParams(vmem_limit_bytes=32 * 2**20),
        name="finish_queries",
    )(*dqs)


def finish_kernel(*refs):
    parts, (dk_ref, dv_ref, tmp) = refs[: 3 * GROUPS], refs[3 * GROUPS :]
    for g in range(GROUPS):
        own, kept, got = parts[3 * g : 3 * g + 3]
        for part, out in enumerate((dk_ref, dv_ref)):
            cols = slice(part * 128, (part + 1) * 128)
            for b in range(8):
                rows = slice(b * SLAB, (b + 1) * SLAB)
                half = slice(b // 2 * SLAB, (b // 2 + 1) * SLAB)
                tmp[pl.ds(b, SLAB, stride=8), :] = (
                    own[rows, cols] + 0.5 * kept[half, cols] + got[rows, cols].astype(F32)
                )
            out[:, g * 128 : (g + 1) * 128] = tmp[...].astype(BF)


def finish_keys(parts):
    return pl.pallas_call(
        finish_kernel,
        out_shape=[jax.ShapeDtypeStruct((KEYS, 512), BF)] * 2,
        scratch_shapes=[pltpu.VMEM((KEYS, 128), F32)],
        compiler_params=pltpu.CompilerParams(vmem_limit_bytes=40 * 2**20),
        name="finish_keys",
    )(*[x for part in parts for x in part])


def partner(value, level):
    mask = MASKS[level]
    pairs = [(source, source ^ mask) for source in range(lax.axis_size("ctx"))]
    return lax.ppermute(value, "ctx", pairs)


def pool(x):
    y = x.astype(F32).reshape(4, 2, SLAB, 256)
    return (0.5 * (y[:, 0] + y[:, 1])).astype(BF).reshape(512, 256)


def spread(x):
    y = jnp.broadcast_to((0.5 * x).reshape(4, 1, SLAB, 256), (4, 2, SLAB, 256))
    return y.reshape(KEYS, 256)


def on_device(queries, key_states, value_states, grad_out, out_weight):
    held = list(prep_keys(key_states[0], value_states[0]))
    kvs = [[h] for h in held]
    for level in range(4):
        far = [partner(h, level) for h in held]
        for g in range(GROUPS):
            kvs[g].append(far[g])
        if level < 3:
            held = [jnp.concatenate([pool(h), pool(f)], 0) for h, f in zip(held, far)]
    qT, gaT, gp = prep_rows(queries[0], grad_out[0], out_weight)
    attns, dqs, parts = [], [], []
    for g in range(GROUPS):
        attn, dq, own, f0, f1, f2, f3 = main(g, qT, gaT, kvs[g], BF)
        attns.append(attn)
        dqs.append(dq)
        pending = partner(f3, 3).astype(F32)
        for level, f in ((2, f2), (1, f1), (0, f0)):
            outgoing = (f.astype(F32) + spread(pending[512:])).astype(BF)
            incoming = partner(outgoing, level)
            kept = pending[:512]
            if level:
                pending = spread(kept) + incoming.astype(F32)
        parts.append((own, kept, incoming))
    outputs, weight_part = project(attns, gp, out_weight)
    grad_queries = finish_queries(dqs)
    grad_keys, grad_values = finish_keys(parts)
    rows = lax.psum_scatter(weight_part, "ctx", scatter_dimension=0, tiled=True)
    grad_weight = lax.psum_scatter(rows, "rep", scatter_dimension=1, tiled=True)
    return outputs[None], grad_queries[None], grad_keys[None], grad_values[None], grad_weight


def solution(mesh):
    rows = P("rep", "ctx", None)
    return jax.shard_map(
        on_device,
        mesh=mesh,
        in_specs=(rows, rows, rows, rows, P()),
        out_specs=(rows, rows, rows, rows, P("ctx", "rep")),
        check_vma=False,
    )
```

```python
import functools

import jax
import jax.numpy as jnp
from jax import lax
from jax.experimental import pallas as pl
from jax.experimental.pallas import tpu as pltpu
from jax.sharding import PartitionSpec as P

F32 = jnp.float32
BF = jnp.bfloat16
KEYS = 1024
SLAB = 128
TW = 256
GROUPS = 4
MASKS = (1, 3, 4, 12)
NT = (((1,), (1,)), ((), ()))
NN = (((1,), (0,)), ((), ()))
LOG2E = 1.4426950408889634
CHUNK = 512


def dot(a, b, dims=NN):
    return lax.dot_general(a, b, dims, preferred_element_type=F32)


def cost(us):
    return pl.CostEstimate(flops=int(us * 1.15e9), bytes_accessed=2**20, transcendentals=0)


def params(mib=58):
    return pltpu.CompilerParams(vmem_limit_bytes=mib * 2**20)


def score_keys(kv):
    k0, k1 = kv[:, 0:64], kv[:, 64:128]
    return jnp.concatenate([k0, k0, k1, k1], 1)


def grad_values_operand(kv):
    ones3 = (lax.broadcasted_iota(jnp.int32, (KEYS, 64), 1) < 3).astype(F32).astype(BF)
    return jnp.concatenate([kv[:, 128:192], ones3, kv[:, 192:256], ones3], 1)


def put_value_rows(ref, kv):
    ref[0:128] = kv[:, 128:256].T
    ref[128:144] = (lax.broadcasted_iota(jnp.int32, (16, KEYS), 0) == 0).astype(F32).astype(BF)


def put_query(qw, t, q):
    zero = jnp.zeros((128, SLAB), BF)
    qs = q.astype(F32) * (0.125 * LOG2E)
    hi = qs.astype(BF)
    lo = (qs - hi.astype(F32)).astype(BF)
    qw[t, 0:64, 0:128] = hi[0:64]
    qw[t, 64:128, 0:128] = lo[0:64]
    qw[t, 128:256, 0:128] = zero
    qw[t, 0:128, 128:256] = zero
    qw[t, 128:192, 128:256] = hi[64:128]
    qw[t, 192:256, 128:256] = lo[64:128]


def put_pair(ref, t, first, second):
    zero = jnp.zeros((64, SLAB), BF)
    off = t * TW
    ref[0:64, off : off + 128] = first
    ref[64:128, off : off + 128] = zero
    ref[0:64, off + 128 : off + 256] = zero
    ref[64:128, off + 128 : off + 256] = second


def put_scaled(qk, t, q):
    qq = (q.astype(F32) * 0.125).astype(BF)
    put_pair(qk, t, qq[0:64], qq[64:128])


def put_grad(gw, gk, t, g, scale):
    n = -scale
    hi = n.astype(BF).astype(F32)
    rest = n - hi
    mid = rest.astype(BF).astype(F32)
    row = lax.broadcasted_iota(jnp.int32, (64, TW), 0)
    low = jnp.where(row == 0, hi, jnp.where(row == 1, mid, jnp.where(row == 2, rest - mid, 0.0)))
    low = low.astype(BF)
    zero = jnp.zeros((128, SLAB), BF)
    gw[t, 0:64, 0:128] = g[:, 0:128]
    gw[t, 64:128, 0:128] = low[:, 0:128]
    gw[t, 128:256, 0:128] = zero
    gw[t, 0:128, 128:256] = zero
    gw[t, 128:192, 128:256] = g[:, 128:256]
    gw[t, 192:256, 128:256] = low[:, 128:256]
    put_pair(gk, t, g[:, 0:128], g[:, 128:256])


def both_heads(x):
    return jnp.concatenate([x[0:64, 0:128], x[64:128, 128:256]], 1)


def forward_step(nxt, cur):
    if nxt is not None:
        keys, query, sn, mn = nxt
        top = None
    if cur is not None:
        values, p_ref, off, sc, mc, w_ref, st_ref, t = cur
        m = mc[0:1]
        w = None
    for c in range(KEYS // CHUNK):
        r = slice(c * CHUNK, (c + 1) * CHUNK)
        if nxt is not None:
            s = dot(keys(r), query())
            sn[r] = s
            x = jnp.max(s.reshape(CHUNK // 8, 8, TW), axis=0)
            top = x if top is None else jnp.maximum(top, x)
        if cur is not None:
            p = jnp.exp2(sc[r] - m).astype(BF)
            p_ref(r, off, p)
            y = dot(values(r), p)
            w = y if w is None else w + y
    if nxt is not None:
        mn[0:1] = jnp.max(top, axis=0, keepdims=True)
    if cur is not None:
        w_ref(t, both_heads(w))
        st_ref(t, m, w[128:129])


def forward_tiles(count, score, value, sa, sb, ma, mb):
    forward_step(score(jnp.int32(0), sa, ma), None)

    def body(i, c):
        t = 2 * i
        forward_step(score(t + 1, sb, mb), value(t, sa, ma))
        forward_step(score(t + 2, sa, ma), value(t + 1, sb, mb))
        return c

    steps = (count - 1) // 2
    lax.fori_loop(0, steps, body, 0)
    t = jnp.int32(2 * steps)
    if count % 2 == 0:
        forward_step(score(t + 1, sb, mb), value(t, sa, ma))
        forward_step(None, value(t + 1, sb, mb))
    else:
        forward_step(None, value(t, sa, ma))


def tile_cols(t):
    return pl.ds(pl.multiple_of(t * TW, TW), TW)


def select(refs, use):
    for i, ref in enumerate(refs):
        pl.when(pl.program_id(0) == i)(functools.partial(use, ref))


def block_forward_kernel(n, q_ref, *refs):
    kvs, (p_ref, w_ref, st_ref, kk, vT, qw, sa, sb, ma, mb) = refs[:n], refs[n:]

    def prepare(kv_ref):
        kv = kv_ref[...]
        kk[...] = score_keys(kv)
        put_value_rows(vT, kv)

    select(kvs, prepare)
    for j in range(8):
        put_query(qw, j, q_ref[:, j * SLAB : (j + 1) * SLAB])

    def put_p(r, t, p):
        p_ref[r, tile_cols(t)] = p

    def put_w(t, w):
        w_ref[t] = w

    def put_st(t, m, total):
        st_ref[t, 0:1] = m
        st_ref[t, 1:2] = total

    def score(t, s, m):
        return (lambda r: kk[r], lambda: qw[t], s, m)

    def value(t, s, m):
        return (lambda r: vT[:, r], put_p, t, s, m, put_w, put_st, t)

    forward_tiles(8, score, value, sa, sb, ma, mb)


WHOLE = pl.BlockSpec((KEYS, 256), lambda i: (0, 0))


def block_forward(first, qT, kvs):
    n = len(kvs)
    return pl.pallas_call(
        functools.partial(block_forward_kernel, n),
        grid=(n,),
        in_specs=[pl.BlockSpec((128, KEYS), lambda i: (first + i, 0))] + [WHOLE] * n,
        out_specs=[
            pl.BlockSpec((None, KEYS, 8 * TW), lambda i: (i, 0, 0)),
            pl.BlockSpec((None, 8, 64, TW), lambda i: (i, 0, 0, 0)),
            pl.BlockSpec((None, 8, 8, TW), lambda i: (i, 0, 0, 0)),
        ],
        out_shape=[
            jax.ShapeDtypeStruct((n, KEYS, 8 * TW), BF),
            jax.ShapeDtypeStruct((n, 8, 64, TW), F32),
            jax.ShapeDtypeStruct((n, 8, 8, TW), F32),
        ],
        scratch_shapes=[
            pltpu.VMEM((KEYS, 256), BF),
            pltpu.VMEM((144, KEYS), BF),
            pltpu.VMEM((8, 256, TW), BF),
            pltpu.VMEM((KEYS, TW), F32),
            pltpu.VMEM((KEYS, TW), F32),
            pltpu.VMEM((8, TW), F32),
            pltpu.VMEM((8, TW), F32),
        ],
        compiler_params=params(),
        cost_estimate=cost(5 * n),
        name="block_forward",
    )(qT, *kvs)


def backward_tile(va, gw_tile, p_tile, kT, put_ds):
    dq = None
    for c in range(KEYS // CHUNK):
        r = slice(c * CHUNK, (c + 1) * CHUNK)
        ds = (p_tile(r).astype(F32) * dot(va(r), gw_tile())).astype(BF)
        put_ds(r, ds)
        y = dot(kT(r), ds)
        dq = y if dq is None else dq + y
    return both_heads(dq)


FAR_TILES = 7
FAR_BLOCKS = ((0, 0, 4), (1, 4, 2), (2, 6, 1))


def far_block(t):
    one = lambda at: (t >= at).astype(jnp.int32)
    return one(4) + one(6)


def group_kernel(
    chained, q_ref, ga_ref, kv1, kv2, kv3, wa_ref, sta_ref, wb_ref, stb_ref, *refs
):
    if chained:
        refs = refs[1:]
    (
        attn_ref, dq_ref, g_ref, gs_ref, o1, o2, o3,
        kk, va, kT, vT, qw, qk, gw, gk, p_ref, ds_ref, w_ref, st_ref, dqt, sa, sb, ma, mb,
    ) = refs
    kvs, outs = (kv1, kv2, kv3), (o1, o2, o3)
    for b in range(3):
        kv = kvs[b][...]
        kk[b] = score_keys(kv)
        va[b] = grad_values_operand(kv)
        kT[b] = kv[:, 0:128].T
        put_value_rows(vT.at[b], kv)
    level = [q_ref[:, j * SLAB : (j + 1) * SLAB] for j in range(8)]
    first = 0
    for _ in range(3):
        level = [
            (0.5 * (level[2 * c].astype(F32) + level[2 * c + 1].astype(F32))).astype(BF)
            for c in range(len(level) // 2)
        ]
        for c, x in enumerate(level):
            put_query(qw, first + c, x)
            put_scaled(qk, first + c, x)
        first += len(level)

    def put_p(r, t, p):
        p_ref[r, tile_cols(t)] = p

    def put_w(t, w):
        w_ref[t] = w

    def put_st(t, m, total):
        st_ref[t, 0:1] = m
        st_ref[t, 1:2] = total

    def score(t, s, m):
        b = far_block(t)
        return (lambda r: kk[b, r], lambda: qw[t], s, m)

    def value(t, s, m):
        b = far_block(t)
        return (lambda r: vT[b, :, r], put_p, t, s, m, put_w, put_st, t)

    forward_tiles(FAR_TILES, score, value, sa, sb, ma, mb)

    gl, gs = [None] * FAR_TILES, [None] * FAR_TILES
    for j in range(8):
        ts = [j // 2, 4 + j // 4, 6]
        ms = [sta_ref[j, 0:1], stb_ref[j, 0:1]] + [st_ref[t, 0:1] for t in ts]
        totals = [sta_ref[j, 1:2], stb_ref[j, 1:2]] + [st_ref[t, 1:2] for t in ts]
        ws = [wa_ref[j], wb_ref[j]] + [w_ref[t] for t in ts]
        top = functools.reduce(jnp.maximum, ms)
        factors = [jnp.exp2(m - top) * c for m, c in zip(ms, (1.0, 1.0, 2.0, 4.0, 8.0))]
        inv = 1.0 / functools.reduce(jnp.add, [f * x for f, x in zip(factors, totals)])
        shares = [f * inv for f in factors]
        at = functools.reduce(jnp.add, [s * w for s, w in zip(shares, ws)]).astype(BF)
        cols = slice(j * SLAB, (j + 1) * SLAB)
        attn_ref[0:64, cols] = at[:, 0:128]
        attn_ref[64:128, cols] = at[:, 128:256]
        ga = jnp.concatenate([ga_ref[0:64, cols], ga_ref[64:128, cols]], 1).astype(F32)
        delta = jnp.sum(ga * at.astype(F32), axis=0, keepdims=True)
        for side in range(2):
            g_ref[side, j] = (shares[side] * ga).astype(BF)
            gs_ref[side, j, 0:1] = shares[side] * delta
        for s, t in zip(shares[2:], ts):
            x, y = s * ga, s * delta
            gl[t] = x if gl[t] is None else gl[t] + x
            gs[t] = y if gs[t] is None else gs[t] + y
    for t in range(FAR_TILES):
        put_grad(gw, gk, t, gl[t].astype(BF), gs[t])

    for b, first, n in reversed(FAR_BLOCKS):

        def body(i, c, b=b, first=first):
            t = first + i

            def put_ds(r, ds):
                ds_ref[r, tile_cols(i)] = ds

            dqt[t] = backward_tile(
                lambda r: va[b, r],
                lambda: gw[t],
                lambda r: p_ref[r, tile_cols(t)],
                lambda r: kT[b, :, r],
                put_ds,
            )
            return c

        lax.fori_loop(0, n, body, 0)

        def rows_body(i, c, b=b, first=first, n=n):
            rows = pl.ds(pl.multiple_of(i * 256, 256), 256)
            cols = slice(first * TW, (first + n) * TW)
            outs[b][rows, 0:128] = dot(ds_ref[rows, 0 : n * TW], qk[:, cols], NT).astype(BF)
            outs[b][rows, 128:256] = dot(p_ref[rows, cols], gk[:, cols], NT).astype(BF)
            return c

        lax.fori_loop(0, 4, rows_body, 0)
    for j in range(8):
        dq_ref[j] = 0.5 * dqt[j // 2] + 0.25 * dqt[4 + j // 4] + 0.125 * dqt[6]


def group(g, qT, gaT, kvs, own, far, attn):
    cols = pl.BlockSpec((128, KEYS), lambda i: (g, 0))
    tiles = lambda rows: pl.BlockSpec((2, 8, rows, TW), lambda i: (0, 0, 0, 0))
    at = lambda place, rows: pl.BlockSpec((None, 8, rows, TW), lambda i: (place, 0, 0, 0))
    chain = [] if attn is None else [attn]
    return pl.pallas_call(
        functools.partial(group_kernel, bool(chain)),
        grid=(1,),
        in_specs=[cols, cols]
        + [WHOLE] * 3
        + [at(own[2], 64), at(own[2], 8), at(far[2], 64), at(far[2], 8)]
        + [pl.BlockSpec(memory_space=pl.ANY) for _ in chain],
        out_specs=[cols, pl.BlockSpec((8, 64, TW), lambda i: (0, 0, 0)), tiles(64), tiles(8)]
        + [WHOLE] * 3,
        out_shape=[
            jax.ShapeDtypeStruct((512, KEYS), BF),
            jax.ShapeDtypeStruct((8, 64, TW), F32),
            jax.ShapeDtypeStruct((2, 8, 64, TW), BF),
            jax.ShapeDtypeStruct((2, 8, 8, TW), F32),
        ]
        + [jax.ShapeDtypeStruct((KEYS, 256), BF)] * 3,
        scratch_shapes=[
            pltpu.VMEM((3, KEYS, 256), BF),
            pltpu.VMEM((3, KEYS, 256), BF),
            pltpu.VMEM((3, 128, KEYS), BF),
            pltpu.VMEM((3, 144, KEYS), BF),
            pltpu.VMEM((FAR_TILES, 256, TW), BF),
            pltpu.VMEM((128, FAR_TILES * TW), BF),
            pltpu.VMEM((FAR_TILES, 256, TW), BF),
            pltpu.VMEM((128, FAR_TILES * TW), BF),
            pltpu.VMEM((KEYS, FAR_TILES * TW), BF),
            pltpu.VMEM((KEYS, 4 * TW), BF),
            pltpu.VMEM((FAR_TILES, 64, TW), F32),
            pltpu.VMEM((FAR_TILES, 8, TW), F32),
            pltpu.VMEM((FAR_TILES, 64, TW), F32),
            pltpu.VMEM((KEYS, TW), F32),
            pltpu.VMEM((KEYS, TW), F32),
            pltpu.VMEM((8, TW), F32),
            pltpu.VMEM((8, TW), F32),
        ],
        input_output_aliases={9: 0} if chain else {},
        compiler_params=params(),
        cost_estimate=cost(16),
        name="group",
    )(qT, gaT, *kvs, *own[:2], *far[:2], *chain)


def block_backward_kernel(n, last, chained, q_ref, p_ref, *refs):
    take = lambda: (refs[:n], refs[n:])
    kvs, refs = take()
    gls, refs = take()
    scales, refs = take()
    if last:
        upper, refs = take()
        other, refs = take()
    if chained:
        refs = refs[1:]
    dq_ref, o_ref, va, kT, qk, gw, gk, ds_ref, dqt, tmp = refs
    for i in range(n):

        @pl.when(pl.program_id(0) == i)
        def _(i=i):
            kv = kvs[i][...]
            va[...] = grad_values_operand(kv)
            kT[...] = kv[:, 0:128].T
            for j in range(8):
                put_grad(gw, gk, j, gls[i][j], scales[i][j, 0:1])

    for j in range(8):
        put_scaled(qk, j, q_ref[:, j * SLAB : (j + 1) * SLAB])

    def body(t, c):
        def put_ds(r, ds):
            ds_ref[r, tile_cols(t)] = ds

        dqt[t] = backward_tile(
            lambda r: va[r],
            lambda: gw[t],
            lambda r: p_ref[r, tile_cols(t)],
            lambda r: kT[:, r],
            put_ds,
        )
        return c

    lax.fori_loop(0, 8, body, 0)

    def rows_body(i, c):
        rows = pl.ds(pl.multiple_of(i * 256, 256), 256)
        o_ref[rows, 0:128] = dot(ds_ref[rows], qk[...], NT).astype(o_ref.dtype)
        o_ref[rows, 128:256] = dot(p_ref[rows], gk[...], NT).astype(o_ref.dtype)
        return c

    lax.fori_loop(0, 4, rows_body, 0)
    if not last:
        dq_ref[...] = dqt[...]
        return
    for i in range(n):

        @pl.when(pl.program_id(0) == i)
        def _(i=i):
            for j in range(8):
                dqt[j] = dqt[j] + upper[i][j] + other[i][j]

    for j in range(8):
        d = 0.125 * dqt[j]
        tmp[pl.ds(j, SLAB, stride=8), :] = jnp.concatenate([d[:, 0:128], d[:, 128:256]], 0).T
    dq_ref[...] = tmp[...].astype(BF)


def block_backward(first, qT, p, kvs, gls, scales, side, upper=None, other=None, dq=None):
    n = len(kvs)
    last = upper is not None
    chain = [] if dq is None else [dq]
    of_side = lambda rows: pl.BlockSpec((None, 8, rows, TW), lambda i: (side, 0, 0, 0))
    at = lambda place: pl.BlockSpec((None, 8, 64, TW), lambda i: (place, 0, 0, 0))
    in_specs = [
        pl.BlockSpec((128, KEYS), lambda i: (first + i, 0)),
        pl.BlockSpec((None, KEYS, 8 * TW), lambda i: (i, 0, 0)),
    ]
    in_specs += [WHOLE] * n + [of_side(64)] * n + [of_side(8)] * n
    args = [qT, p, *kvs, *gls, *scales]
    if last:
        in_specs += [pl.BlockSpec((8, 64, TW), lambda i: (0, 0, 0))] * n
        in_specs += [at(place) for _, place in other]
        args += [*upper, *[part for part, _ in other]]
        dq_spec = pl.BlockSpec((KEYS, 128), lambda i: (0, first + i))
        dq_shape = jax.ShapeDtypeStruct((KEYS, 512), BF)
    else:
        dq_spec = pl.BlockSpec((None, 8, 64, TW), lambda i: (i, 0, 0, 0))
        dq_shape = jax.ShapeDtypeStruct((n, 8, 64, TW), F32)
    in_specs += [pl.BlockSpec(memory_space=pl.ANY) for _ in chain]
    return pl.pallas_call(
        functools.partial(block_backward_kernel, n, last, bool(chain)),
        grid=(n,),
        in_specs=in_specs,
        out_specs=[dq_spec, pl.BlockSpec((None, KEYS, 256), lambda i: (i, 0, 0))],
        out_shape=[dq_shape, jax.ShapeDtypeStruct((n, KEYS, 256), F32 if last else BF)],
        scratch_shapes=[
            pltpu.VMEM((KEYS, 256), BF),
            pltpu.VMEM((128, KEYS), BF),
            pltpu.VMEM((128, 8 * TW), BF),
            pltpu.VMEM((8, 256, TW), BF),
            pltpu.VMEM((128, 8 * TW), BF),
            pltpu.VMEM((KEYS, 8 * TW), BF),
            pltpu.VMEM((8, 64, TW), F32),
            pltpu.VMEM((KEYS, 128), F32),
        ],
        input_output_aliases={len(args): 0} if chain else {},
        compiler_params=params(),
        cost_estimate=cost(10 * n),
        name="block_backward",
    )(*args, *chain)


def keys_kernel(k_ref, v_ref, o0, o1, o2, o3, tmp):
    outs = (o0, o1, o2, o3)
    for part, src in enumerate((k_ref, v_ref)):
        for g in range(GROUPS):
            tmp[...] = src[:, g * 128 : (g + 1) * 128].astype(F32)
            for b in range(8):
                outs[g][b * SLAB : (b + 1) * SLAB, part * 128 : (part + 1) * 128] = tmp[
                    pl.ds(b, SLAB, stride=8), :
                ].astype(BF)


def prep_keys(k, v):
    return pl.pallas_call(
        keys_kernel,
        out_shape=[jax.ShapeDtypeStruct((KEYS, 256), BF)] * GROUPS,
        scratch_shapes=[pltpu.VMEM((KEYS, 128), F32)],
        compiler_params=params(),
        cost_estimate=cost(3),
        name="prep_keys",
    )(k, v)


def rows_kernel(q_ref, go_ref, w_ref, qT_ref, gaT_ref, gp_ref, tmp):
    for g in range(GROUPS):
        tmp[...] = q_ref[:, g * 128 : (g + 1) * 128].astype(F32)
        for b in range(8):
            x = tmp[pl.ds(b, SLAB, stride=8), :]
            qT_ref[g * 128 : (g + 1) * 128, b * SLAB : (b + 1) * SLAB] = x.T.astype(BF)
    for c in range(8):
        tmp[...] = go_ref[:, c * 128 : (c + 1) * 128].astype(F32)
        for b in range(8):
            gp_ref[b * SLAB : (b + 1) * SLAB, c * 128 : (c + 1) * 128] = tmp[
                pl.ds(b, SLAB, stride=8), :
            ].astype(BF)
    for c in range(4):
        rows = pl.ds(c * 256, 256)
        gaT_ref[:, c * 256 : (c + 1) * 256] = dot(w_ref[...], gp_ref[rows, :], NT).astype(BF)


def prep_rows(q, go, w):
    return pl.pallas_call(
        rows_kernel,
        out_shape=[
            jax.ShapeDtypeStruct((512, KEYS), BF),
            jax.ShapeDtypeStruct((512, KEYS), BF),
            jax.ShapeDtypeStruct((KEYS, 1024), BF),
        ],
        scratch_shapes=[pltpu.VMEM((KEYS, 128), F32)],
        compiler_params=params(),
        cost_estimate=cost(6),
        name="prep_rows",
    )(q, go, w)


def project_kernel(attn_ref, gp_ref, w_ref, out_ref, gw_ref, at, tmp):
    for g in range(GROUPS):
        rows = slice(g * 128, (g + 1) * 128)
        at[:, rows] = attn_ref[rows, :].T
        gw_ref[rows, :] = dot(attn_ref[rows, :], gp_ref[...])
    for c in range(8):
        for b in range(8):
            tmp[pl.ds(b, SLAB, stride=8), :] = dot(
                at[b * SLAB : (b + 1) * SLAB, :], w_ref[:, c * 128 : (c + 1) * 128]
            )
        out_ref[:, c * 128 : (c + 1) * 128] = tmp[...].astype(BF)


def project(attn, gp, w):
    return pl.pallas_call(
        project_kernel,
        out_shape=[
            jax.ShapeDtypeStruct((KEYS, 1024), BF),
            jax.ShapeDtypeStruct((512, 1024), F32),
        ],
        scratch_shapes=[pltpu.VMEM((KEYS, 512), BF), pltpu.VMEM((KEYS, 128), F32)],
        compiler_params=params(),
        cost_estimate=cost(7),
        name="project",
    )(attn, gp, w)


def finish_kernel(*refs):
    parts, (dk_ref, dv_ref, tmp) = refs[: 3 * GROUPS], refs[3 * GROUPS :]
    for g in range(GROUPS):
        own, kept, got = parts[3 * g : 3 * g + 3]
        for part, out in enumerate((dk_ref, dv_ref)):
            cols = slice(part * 128, (part + 1) * 128)
            for b in range(8):
                rows = slice(b * SLAB, (b + 1) * SLAB)
                half = slice(b // 2 * SLAB, (b // 2 + 1) * SLAB)
                tmp[pl.ds(b, SLAB, stride=8), :] = (
                    own[rows, cols] + 0.5 * kept[half, cols] + got[rows, cols].astype(F32)
                )
            out[:, g * 128 : (g + 1) * 128] = tmp[...].astype(BF)


def finish_keys(owns, kept, got):
    in_specs, args = [], []
    for (own, place), x, y in zip(owns, kept, got):
        in_specs.append(pl.BlockSpec((None, KEYS, 256), lambda i, place=place: (place, 0, 0)))
        in_specs += [pl.BlockSpec((512, 256), lambda i: (0, 0)), WHOLE]
        args += [own, x, y]
    return pl.pallas_call(
        finish_kernel,
        grid=(1,),
        in_specs=in_specs,
        out_specs=[pl.BlockSpec((KEYS, 512), lambda i: (0, 0))] * 2,
        out_shape=[jax.ShapeDtypeStruct((KEYS, 512), BF)] * 2,
        scratch_shapes=[pltpu.VMEM((KEYS, 128), F32)],
        compiler_params=params(),
        cost_estimate=cost(5),
        name="finish_keys",
    )(*args)


def partner(value, level):
    mask = MASKS[level]
    pairs = [(source, source ^ mask) for source in range(lax.axis_size("ctx"))]
    return lax.ppermute(value, "ctx", pairs)


def pool(x):
    y = x.astype(F32).reshape(4, 2, SLAB, 256)
    return (0.5 * (y[:, 0] + y[:, 1])).astype(BF).reshape(512, 256)


def spread(x):
    y = jnp.broadcast_to((0.5 * x).reshape(4, 1, SLAB, 256), (4, 2, SLAB, 256))
    return y.reshape(KEYS, 256)


def after(values, done):
    out = lax.optimization_barrier((*values, *done))
    return list(out[: len(values)])


def on_device(queries, key_states, value_states, grad_out, out_weight):
    held = [[x] for x in prep_keys(key_states[0], value_states[0])]
    far = [[] for _ in held]

    def send(g):
        far[g].append(partner(held[g][-1], len(far[g])))

    def pool_and_send(which, done):
        for g, x in zip(which, after([far[g][-1] for g in which], done)):
            far[g][-1] = x
            held[g].append(jnp.concatenate([pool(held[g][-1]), pool(x)], 0))
        made = [held[g][-1] for g in which]
        for g in which:
            send(g)
        return made

    own = [h[0] for h in held]
    for g in range(GROUPS):
        send(g)
    qT, gaT, gp = prep_rows(queries[0], grad_out[0], out_weight)

    p_own0, w_own0, st_own0 = block_forward(0, qT, own[:1])
    made = pool_and_send([0], [st_own0])
    (qT,) = after([qT], made)
    p_own1, w_own1, st_own1 = block_forward(1, qT, own[1:])
    made = pool_and_send([0, 1], [st_own1])
    (qT,) = after([qT], made)
    p_far0, w_far0, st_far0 = block_forward(0, qT, [far[0][0], far[1][0]])
    made = pool_and_send([0, 1, 2], [st_far0])
    (qT,) = after([qT], made)
    p_far2, w_far2, st_far2 = block_forward(2, qT, [far[2][0]])
    made = pool_and_send([1, 2, 3], [st_far2])
    (qT,) = after([qT], made)

    owns = [(w_own0, st_own0, 0)] + [(w_own1, st_own1, i) for i in range(3)]
    fars = [(w_far0, st_far0, 0), (w_far0, st_far0, 1), (w_far2, st_far2, 0)]
    attn = None
    dqs, gls, scales, grads, pending, sent = [], [], [], [], [], []

    def level_3_to_1(g):
        nonlocal attn
        attn, dq, gl, gs, f1, f2, f3 = group(g, qT, gaT, far[g][1:], owns[g], fars[g], attn)
        dqs.append(dq)
        gls.append(gl)
        scales.append(gs)
        grads.append([None, f1, f2, f3])
        sent.append(partner(f3, 3))
        pending.append(None)

    def pass_on(steps, done):
        made = []
        for (g, level), x in zip(steps, after([sent[g] for g, _ in steps], done)):
            x = x.astype(F32)
            full = x if pending[g] is None else spread(pending[g]) + x
            pending[g] = full[:512]
            outgoing = (grads[g][level].astype(F32) + spread(full[512:])).astype(BF)
            made.append(outgoing)
            sent[g] = partner(outgoing, level)
        return made

    level_3_to_1(0)
    made = pool_and_send([2, 3], [dqs[0]])
    (qT,) = after([qT], made)
    p_far3, w_far3, st_far3 = block_forward(3, qT, [far[3][0]])
    fars.append((w_far3, st_far3, 0))
    (qT,) = after([qT], [st_far3])
    level_3_to_1(1)
    made = pool_and_send([3], [dqs[1]]) + pass_on([(0, 2)], [dqs[1]])
    (qT,) = after([qT], made)
    level_3_to_1(2)
    made = pass_on([(0, 1), (1, 2)], [dqs[2]])
    (qT,) = after([qT], made)
    level_3_to_1(3)
    made = pass_on([(1, 1), (2, 2)], [dqs[3]])
    (attn,) = after([attn], made)
    outputs, weight_part = project(attn, gp, out_weight)
    (qT,) = after([qT], [outputs])

    def far_backward(first, p, n):
        which = range(first, first + n)
        dq, o = block_backward(
            first, qT, p, [far[g][0] for g in which], [gls[g] for g in which],
            [scales[g] for g in which], 1,
        )
        for i, g in enumerate(which):
            grads[g][0] = o[i]
        return dq

    dq_far0 = far_backward(0, p_far0, 2)
    made = pass_on([(0, 0), (1, 0), (2, 1), (3, 2)], [dq_far0])
    (qT,) = after([qT], made)
    dq_far2 = far_backward(2, p_far2, 1)
    made = pass_on([(2, 0), (3, 1)], [dq_far2])
    (qT,) = after([qT], made)
    dq_far3 = far_backward(3, p_far3, 1)
    (qT,) = after([qT], [dq_far3])
    other = [(dq_far0, 0), (dq_far0, 1), (dq_far2, 0), (dq_far3, 0)]
    dq, o_own0 = block_backward(
        0, qT, p_own0, own[:1], gls[:1], scales[:1], 0, dqs[:1], other[:1]
    )
    made = pass_on([(3, 0)], [o_own0])
    (qT,) = after([qT], made)
    dq, o_own1 = block_backward(
        1, qT, p_own1, own[1:], gls[1:], scales[1:], 0, dqs[1:], other[1:], dq
    )
    got = after(sent, [o_own1])
    grad_keys, grad_values = finish_keys(
        [(o_own0, 0)] + [(o_own1, i) for i in range(3)], pending, got
    )
    rows = lax.psum_scatter(weight_part, "ctx", scatter_dimension=0, tiled=True)
    grad_weight = lax.psum_scatter(rows, "rep", scatter_dimension=1, tiled=True)
    return outputs[None], dq[None], grad_keys[None], grad_values[None], grad_weight


def solution(mesh):
    rows = P("rep", "ctx", None)
    return jax.shard_map(
        on_device,
        mesh=mesh,
        in_specs=(rows, rows, rows, rows, P()),
        out_specs=(rows, rows, rows, rows, P("ctx", "rep")),
        check_vma=False,
    )
```

```python
import functools

import jax
import jax.numpy as jnp
from jax import lax
from jax.experimental import pallas as pl
from jax.experimental.pallas import tpu as pltpu
from jax.sharding import PartitionSpec as P

F32 = jnp.float32
BF = jnp.bfloat16
KEYS = 1024
SLAB = 128
TW = 256
GROUPS = 4
MASKS = (1, 3, 4, 12)
NT = (((1,), (1,)), ((), ()))
NN = (((1,), (0,)), ((), ()))
LOG2E = 1.4426950408889634
CHUNK = 512
BACK = 256


def dot(a, b, dims=NN):
    return lax.dot_general(a, b, dims, preferred_element_type=F32)


def cost(us):
    return pl.CostEstimate(flops=int(us * 1.15e9), bytes_accessed=2**20, transcendentals=0)


def params(mib=58):
    return pltpu.CompilerParams(vmem_limit_bytes=mib * 2**20)


def score_keys(kv):
    k0, k1 = kv[:, 0:64], kv[:, 64:128]
    return jnp.concatenate([k0, k0, k1, k1], 1)


def grad_values_operand(kv):
    ones3 = (lax.broadcasted_iota(jnp.int32, (KEYS, 64), 1) < 3).astype(F32).astype(BF)
    return jnp.concatenate([kv[:, 128:192], ones3, kv[:, 192:256], ones3], 1)


def put_value_rows(ref, kv):
    ref[0:128] = kv[:, 128:256].T
    ref[128:144] = (lax.broadcasted_iota(jnp.int32, (16, KEYS), 0) == 0).astype(F32).astype(BF)


def put_query(qw, t, q):
    zero = jnp.zeros((128, SLAB), BF)
    qs = q.astype(F32) * (0.125 * LOG2E)
    hi = qs.astype(BF)
    lo = (qs - hi.astype(F32)).astype(BF)
    qw[t, 0:64, 0:128] = hi[0:64]
    qw[t, 64:128, 0:128] = lo[0:64]
    qw[t, 128:256, 0:128] = zero
    qw[t, 0:128, 128:256] = zero
    qw[t, 128:192, 128:256] = hi[64:128]
    qw[t, 192:256, 128:256] = lo[64:128]


def put_pair(ref, t, first, second):
    zero = jnp.zeros((64, SLAB), BF)
    off = t * TW
    ref[0:64, off : off + 128] = first
    ref[64:128, off : off + 128] = zero
    ref[0:64, off + 128 : off + 256] = zero
    ref[64:128, off + 128 : off + 256] = second


def put_scaled(qk, t, q):
    qq = (q.astype(F32) * 0.125).astype(BF)
    put_pair(qk, t, qq[0:64], qq[64:128])


def put_grad(gw, gk, t, g, scale):
    n = -scale
    hi = n.astype(BF).astype(F32)
    rest = n - hi
    mid = rest.astype(BF).astype(F32)
    row = lax.broadcasted_iota(jnp.int32, (64, TW), 0)
    low = jnp.where(row == 0, hi, jnp.where(row == 1, mid, jnp.where(row == 2, rest - mid, 0.0)))
    low = low.astype(BF)
    zero = jnp.zeros((128, SLAB), BF)
    gw[t, 0:64, 0:128] = g[:, 0:128]
    gw[t, 64:128, 0:128] = low[:, 0:128]
    gw[t, 128:256, 0:128] = zero
    gw[t, 0:128, 128:256] = zero
    gw[t, 128:192, 128:256] = g[:, 128:256]
    gw[t, 192:256, 128:256] = low[:, 128:256]
    put_pair(gk, t, g[:, 0:128], g[:, 128:256])


def both_heads(x):
    return jnp.concatenate([x[0:64, 0:128], x[64:128, 128:256]], 1)


def forward_step(nxt, cur):
    if nxt is not None:
        keys, query, sn, mn = nxt
        top = None
    if cur is not None:
        values, p_ref, off, sc, mc, w_ref, st_ref, t = cur
        m = mc[0:1]
        w = None
    for c in range(KEYS // CHUNK):
        r = slice(c * CHUNK, (c + 1) * CHUNK)
        if nxt is not None:
            s = dot(keys(r), query())
            sn[r] = s
            x = jnp.max(s.reshape(CHUNK // 8, 8, TW), axis=0)
            top = x if top is None else jnp.maximum(top, x)
        if cur is not None:
            p = jnp.exp2(sc[r] - m).astype(BF)
            p_ref(r, off, p)
            y = dot(values(r), p)
            w = y if w is None else w + y
    if nxt is not None:
        mn[0:1] = jnp.max(top, axis=0, keepdims=True)
    if cur is not None:
        w_ref(t, both_heads(w))
        st_ref(t, m, w[128:129])


def forward_tiles(count, score, value, sa, sb, ma, mb):
    forward_step(score(jnp.int32(0), sa, ma), None)

    def body(i, c):
        t = 2 * i
        forward_step(score(t + 1, sb, mb), value(t, sa, ma))
        forward_step(score(t + 2, sa, ma), value(t + 1, sb, mb))
        return c

    steps = (count - 1) // 2
    lax.fori_loop(0, steps, body, 0)
    t = jnp.int32(2 * steps)
    if count % 2 == 0:
        forward_step(score(t + 1, sb, mb), value(t, sa, ma))
        forward_step(None, value(t + 1, sb, mb))
    else:
        forward_step(None, value(t, sa, ma))


def tile_cols(t):
    if isinstance(t, int):
        return slice(t * TW, (t + 1) * TW)
    return pl.ds(pl.multiple_of(t * TW, TW), TW)


def select(refs, use):
    for i, ref in enumerate(refs):
        pl.when(pl.program_id(0) == i)(functools.partial(use, ref))


def block_forward_kernel(n, q_ref, *refs):
    kvs, (p_ref, w_ref, st_ref, kk, vT, qw, sa, sb, ma, mb) = refs[:n], refs[n:]

    def prepare(kv_ref):
        kv = kv_ref[...]
        kk[...] = score_keys(kv)
        put_value_rows(vT, kv)

    select(kvs, prepare)
    for j in range(8):
        put_query(qw, j, q_ref[:, j * SLAB : (j + 1) * SLAB])

    def put_p(r, t, p):
        p_ref[r, tile_cols(t)] = p

    def put_w(t, w):
        w_ref[t] = w

    def put_st(t, m, total):
        st_ref[t, 0:1] = m
        st_ref[t, 1:2] = total

    def score(t, s, m):
        return (lambda r: kk[r], lambda: qw[t], s, m)

    def value(t, s, m):
        return (lambda r: vT[:, r], put_p, t, s, m, put_w, put_st, t)

    forward_tiles(8, score, value, sa, sb, ma, mb)


WHOLE = pl.BlockSpec((KEYS, 256), lambda i: (0, 0))


def block_forward(first, qT, kvs):
    n = len(kvs)
    return pl.pallas_call(
        functools.partial(block_forward_kernel, n),
        grid=(n,),
        in_specs=[pl.BlockSpec((128, KEYS), lambda i: (first + i, 0))] + [WHOLE] * n,
        out_specs=[
            pl.BlockSpec((None, KEYS, 8 * TW), lambda i: (i, 0, 0)),
            pl.BlockSpec((None, 8, 64, TW), lambda i: (i, 0, 0, 0)),
            pl.BlockSpec((None, 8, 8, TW), lambda i: (i, 0, 0, 0)),
        ],
        out_shape=[
            jax.ShapeDtypeStruct((n, KEYS, 8 * TW), BF),
            jax.ShapeDtypeStruct((n, 8, 64, TW), F32),
            jax.ShapeDtypeStruct((n, 8, 8, TW), F32),
        ],
        scratch_shapes=[
            pltpu.VMEM((KEYS, 256), BF),
            pltpu.VMEM((144, KEYS), BF),
            pltpu.VMEM((8, 256, TW), BF),
            pltpu.VMEM((KEYS, TW), F32),
            pltpu.VMEM((KEYS, TW), F32),
            pltpu.VMEM((8, TW), F32),
            pltpu.VMEM((8, TW), F32),
        ],
        compiler_params=params(),
        cost_estimate=cost(5 * n),
        name="block_forward",
    )(qT, *kvs)


def backward_tiles(blocks, va, kT, qk, gw, gk, p_ref, ds_ref, dqt, outs, pieces):
    rows_of = KEYS // BACK
    items = [(b, t, c) for b, first, n in blocks for t in range(first, first + n) for c in range(rows_of)]
    ends = {first + n - 1: (b, first, n) for b, first, n in blocks}
    grads, scores, dqs, fill = {}, {}, {}, []

    def sums(b, first, n, left, right, lanes, count):
        cols = slice(first * TW, (first + n) * TW)

        def piece(rows):
            outs[b][rows, lanes] = dot(left[rows, cols], right[:, cols], NT).astype(outs[b].dtype)

        step = KEYS // count
        return [functools.partial(piece, slice(i * step, (i + 1) * step)) for i in range(count)]

    def issue(n):
        if n < len(items):
            b, t, c = items[n]
            grads[n] = dot(va(b, slice(c * BACK, (c + 1) * BACK)), gw[t])

    for block in blocks:
        fill += sums(*block, p_ref, gk, slice(128, 256), pieces)
    issue(0)
    issue(1)
    for n, (b, t, c) in enumerate(items):
        issue(n + 2)
        r = slice(c * BACK, (c + 1) * BACK)
        ds = (p_ref[r, tile_cols(t)].astype(F32) * grads.pop(n)).astype(BF)
        ds_ref[r, tile_cols(t)] = ds
        if c == 0 and fill:
            fill.pop(0)()
        y = dot(kT(b, r), ds)
        dqs[t] = y if c == 0 else dqs[t] + y
        if c == rows_of - 1:
            dqt[t] = both_heads(dqs.pop(t))
            if t in ends:
                last = t == items[-1][1]
                fill += sums(*ends[t], ds_ref, qk, slice(0, 128), 1 if last else pieces)
    while fill:
        fill.pop(0)()


FAR_TILES = 7
FAR_BLOCKS = ((0, 0, 4), (1, 4, 2), (2, 6, 1))


def far_block(t):
    one = lambda at: (t >= at).astype(jnp.int32)
    return one(4) + one(6)


def group_kernel(
    chained, q_ref, ga_ref, kv1, kv2, kv3, wa_ref, sta_ref, wb_ref, stb_ref, *refs
):
    if chained:
        refs = refs[1:]
    (
        attn_ref, dq_ref, g_ref, gs_ref, o1, o2, o3,
        kk, va, kT, vT, qw, qk, gw, gk, p_ref, ds_ref, w_ref, st_ref, dqt, sa, sb, ma, mb,
    ) = refs
    kvs, outs = (kv1, kv2, kv3), (o1, o2, o3)
    for b in range(3):
        kv = kvs[b][...]
        kk[b] = score_keys(kv)
        va[b] = grad_values_operand(kv)
        kT[b] = kv[:, 0:128].T
        put_value_rows(vT.at[b], kv)
    level = [q_ref[:, j * SLAB : (j + 1) * SLAB] for j in range(8)]
    first = 0
    for _ in range(3):
        level = [
            (0.5 * (level[2 * c].astype(F32) + level[2 * c + 1].astype(F32))).astype(BF)
            for c in range(len(level) // 2)
        ]
        for c, x in enumerate(level):
            put_query(qw, first + c, x)
            put_scaled(qk, first + c, x)
        first += len(level)

    def put_p(r, t, p):
        p_ref[r, tile_cols(t)] = p

    def put_w(t, w):
        w_ref[t] = w

    def put_st(t, m, total):
        st_ref[t, 0:1] = m
        st_ref[t, 1:2] = total

    def score(t, s, m):
        b = far_block(t)
        return (lambda r: kk[b, r], lambda: qw[t], s, m)

    def value(t, s, m):
        b = far_block(t)
        return (lambda r: vT[b, :, r], put_p, t, s, m, put_w, put_st, t)

    forward_tiles(FAR_TILES, score, value, sa, sb, ma, mb)

    gl, gs = [None] * FAR_TILES, [None] * FAR_TILES
    for j in range(8):
        ts = [j // 2, 4 + j // 4, 6]
        ms = [sta_ref[j, 0:1], stb_ref[j, 0:1]] + [st_ref[t, 0:1] for t in ts]
        totals = [sta_ref[j, 1:2], stb_ref[j, 1:2]] + [st_ref[t, 1:2] for t in ts]
        ws = [wa_ref[j], wb_ref[j]] + [w_ref[t] for t in ts]
        top = functools.reduce(jnp.maximum, ms)
        factors = [jnp.exp2(m - top) * c for m, c in zip(ms, (1.0, 1.0, 2.0, 4.0, 8.0))]
        inv = 1.0 / functools.reduce(jnp.add, [f * x for f, x in zip(factors, totals)])
        shares = [f * inv for f in factors]
        at = functools.reduce(jnp.add, [s * w for s, w in zip(shares, ws)]).astype(BF)
        cols = slice(j * SLAB, (j + 1) * SLAB)
        attn_ref[0:64, cols] = at[:, 0:128]
        attn_ref[64:128, cols] = at[:, 128:256]
        ga = jnp.concatenate([ga_ref[0:64, cols], ga_ref[64:128, cols]], 1).astype(F32)
        delta = jnp.sum(ga * at.astype(F32), axis=0, keepdims=True)
        for side in range(2):
            g_ref[side, j] = (shares[side] * ga).astype(BF)
            gs_ref[side, j, 0:1] = shares[side] * delta
        for s, t in zip(shares[2:], ts):
            x, y = s * ga, s * delta
            gl[t] = x if gl[t] is None else gl[t] + x
            gs[t] = y if gs[t] is None else gs[t] + y
    for t in range(FAR_TILES):
        put_grad(gw, gk, t, gl[t].astype(BF), gs[t])

    backward_tiles(
        FAR_BLOCKS, lambda b, r: va[b, r], lambda b, r: kT[b, :, r],
        qk, gw, gk, p_ref, ds_ref, dqt, outs, 4,
    )
    for j in range(8):
        dq_ref[j] = 0.5 * dqt[j // 2] + 0.25 * dqt[4 + j // 4] + 0.125 * dqt[6]


def group(g, qT, gaT, kvs, own, far, attn):
    cols = pl.BlockSpec((128, KEYS), lambda i: (g, 0))
    tiles = lambda rows: pl.BlockSpec((2, 8, rows, TW), lambda i: (0, 0, 0, 0))
    at = lambda place, rows: pl.BlockSpec((None, 8, rows, TW), lambda i: (place, 0, 0, 0))
    chain = [] if attn is None else [attn]
    return pl.pallas_call(
        functools.partial(group_kernel, bool(chain)),
        grid=(1,),
        in_specs=[cols, cols]
        + [WHOLE] * 3
        + [at(own[2], 64), at(own[2], 8), at(far[2], 64), at(far[2], 8)]
        + [pl.BlockSpec(memory_space=pl.ANY) for _ in chain],
        out_specs=[cols, pl.BlockSpec((8, 64, TW), lambda i: (0, 0, 0)), tiles(64), tiles(8)]
        + [WHOLE] * 3,
        out_shape=[
            jax.ShapeDtypeStruct((512, KEYS), BF),
            jax.ShapeDtypeStruct((8, 64, TW), F32),
            jax.ShapeDtypeStruct((2, 8, 64, TW), BF),
            jax.ShapeDtypeStruct((2, 8, 8, TW), F32),
        ]
        + [jax.ShapeDtypeStruct((KEYS, 256), BF)] * 3,
        scratch_shapes=[
            pltpu.VMEM((3, KEYS, 256), BF),
            pltpu.VMEM((3, KEYS, 256), BF),
            pltpu.VMEM((3, 128, KEYS), BF),
            pltpu.VMEM((3, 144, KEYS), BF),
            pltpu.VMEM((FAR_TILES, 256, TW), BF),
            pltpu.VMEM((128, FAR_TILES * TW), BF),
            pltpu.VMEM((FAR_TILES, 256, TW), BF),
            pltpu.VMEM((128, FAR_TILES * TW), BF),
            pltpu.VMEM((KEYS, FAR_TILES * TW), BF),
            pltpu.VMEM((KEYS, FAR_TILES * TW), BF),
            pltpu.VMEM((FAR_TILES, 64, TW), F32),
            pltpu.VMEM((FAR_TILES, 8, TW), F32),
            pltpu.VMEM((FAR_TILES, 64, TW), F32),
            pltpu.VMEM((KEYS, TW), F32),
            pltpu.VMEM((KEYS, TW), F32),
            pltpu.VMEM((8, TW), F32),
            pltpu.VMEM((8, TW), F32),
        ],
        input_output_aliases={9: 0} if chain else {},
        compiler_params=params(),
        cost_estimate=cost(16),
        name="group",
    )(qT, gaT, *kvs, *own[:2], *far[:2], *chain)


def block_backward_kernel(n, last, chained, q_ref, p_ref, *refs):
    take = lambda: (refs[:n], refs[n:])
    kvs, refs = take()
    gls, refs = take()
    scales, refs = take()
    if last:
        upper, refs = take()
        other, refs = take()
    if chained:
        refs = refs[1:]
    dq_ref, o_ref, va, kT, qk, gw, gk, ds_ref, dqt, tmp = refs
    for i in range(n):

        @pl.when(pl.program_id(0) == i)
        def _(i=i):
            kv = kvs[i][...]
            va[...] = grad_values_operand(kv)
            kT[...] = kv[:, 0:128].T
            for j in range(8):
                put_grad(gw, gk, j, gls[i][j], scales[i][j, 0:1])

    for j in range(8):
        put_scaled(qk, j, q_ref[:, j * SLAB : (j + 1) * SLAB])

    backward_tiles(
        ((0, 0, 8),), lambda b, r: va[r], lambda b, r: kT[:, r],
        qk, gw, gk, p_ref, ds_ref, dqt, (o_ref,), 8,
    )
    if not last:
        dq_ref[...] = dqt[...]
        return
    for i in range(n):

        @pl.when(pl.program_id(0) == i)
        def _(i=i):
            for j in range(8):
                dqt[j] = dqt[j] + upper[i][j] + other[i][j]

    for j in range(8):
        d = 0.125 * dqt[j]
        tmp[pl.ds(j, SLAB, stride=8), :] = jnp.concatenate([d[:, 0:128], d[:, 128:256]], 0).T
    dq_ref[...] = tmp[...].astype(BF)


def block_backward(first, qT, p, kvs, gls, scales, side, upper=None, other=None, dq=None):
    n = len(kvs)
    last = upper is not None
    chain = [] if dq is None else [dq]
    of_side = lambda rows: pl.BlockSpec((None, 8, rows, TW), lambda i: (side, 0, 0, 0))
    at = lambda place: pl.BlockSpec((None, 8, 64, TW), lambda i: (place, 0, 0, 0))
    in_specs = [
        pl.BlockSpec((128, KEYS), lambda i: (first + i, 0)),
        pl.BlockSpec((None, KEYS, 8 * TW), lambda i: (i, 0, 0)),
    ]
    in_specs += [WHOLE] * n + [of_side(64)] * n + [of_side(8)] * n
    args = [qT, p, *kvs, *gls, *scales]
    if last:
        in_specs += [pl.BlockSpec((8, 64, TW), lambda i: (0, 0, 0))] * n
        in_specs += [at(place) for _, place in other]
        args += [*upper, *[part for part, _ in other]]
        dq_spec = pl.BlockSpec((KEYS, 128), lambda i: (0, first + i))
        dq_shape = jax.ShapeDtypeStruct((KEYS, 512), BF)
    else:
        dq_spec = pl.BlockSpec((None, 8, 64, TW), lambda i: (i, 0, 0, 0))
        dq_shape = jax.ShapeDtypeStruct((n, 8, 64, TW), F32)
    in_specs += [pl.BlockSpec(memory_space=pl.ANY) for _ in chain]
    return pl.pallas_call(
        functools.partial(block_backward_kernel, n, last, bool(chain)),
        grid=(n,),
        in_specs=in_specs,
        out_specs=[dq_spec, pl.BlockSpec((None, KEYS, 256), lambda i: (i, 0, 0))],
        out_shape=[dq_shape, jax.ShapeDtypeStruct((n, KEYS, 256), F32 if last else BF)],
        scratch_shapes=[
            pltpu.VMEM((KEYS, 256), BF),
            pltpu.VMEM((128, KEYS), BF),
            pltpu.VMEM((128, 8 * TW), BF),
            pltpu.VMEM((8, 256, TW), BF),
            pltpu.VMEM((128, 8 * TW), BF),
            pltpu.VMEM((KEYS, 8 * TW), BF),
            pltpu.VMEM((8, 64, TW), F32),
            pltpu.VMEM((KEYS, 128), F32),
        ],
        input_output_aliases={len(args): 0} if chain else {},
        compiler_params=params(),
        cost_estimate=cost(10 * n),
        name="block_backward",
    )(*args, *chain)


def keys_kernel(k_ref, v_ref, o0, o1, o2, o3, tmp):
    outs = (o0, o1, o2, o3)
    for part, src in enumerate((k_ref, v_ref)):
        for g in range(GROUPS):
            tmp[...] = src[:, g * 128 : (g + 1) * 128].astype(F32)
            for b in range(8):
                outs[g][b * SLAB : (b + 1) * SLAB, part * 128 : (part + 1) * 128] = tmp[
                    pl.ds(b, SLAB, stride=8), :
                ].astype(BF)


def prep_keys(k, v):
    return pl.pallas_call(
        keys_kernel,
        out_shape=[jax.ShapeDtypeStruct((KEYS, 256), BF)] * GROUPS,
        scratch_shapes=[pltpu.VMEM((KEYS, 128), F32)],
        compiler_params=params(),
        cost_estimate=cost(3),
        name="prep_keys",
    )(k, v)


def rows_kernel(q_ref, go_ref, w_ref, qT_ref, gaT_ref, gp_ref, tmp):
    for g in range(GROUPS):
        tmp[...] = q_ref[:, g * 128 : (g + 1) * 128].astype(F32)
        for b in range(8):
            x = tmp[pl.ds(b, SLAB, stride=8), :]
            qT_ref[g * 128 : (g + 1) * 128, b * SLAB : (b + 1) * SLAB] = x.T.astype(BF)
    for c in range(8):
        tmp[...] = go_ref[:, c * 128 : (c + 1) * 128].astype(F32)
        for b in range(8):
            gp_ref[b * SLAB : (b + 1) * SLAB, c * 128 : (c + 1) * 128] = tmp[
                pl.ds(b, SLAB, stride=8), :
            ].astype(BF)
    for c in range(4):
        rows = pl.ds(c * 256, 256)
        gaT_ref[:, c * 256 : (c + 1) * 256] = dot(w_ref[...], gp_ref[rows, :], NT).astype(BF)


def prep_rows(q, go, w):
    return pl.pallas_call(
        rows_kernel,
        out_shape=[
            jax.ShapeDtypeStruct((512, KEYS), BF),
            jax.ShapeDtypeStruct((512, KEYS), BF),
            jax.ShapeDtypeStruct((KEYS, 1024), BF),
        ],
        scratch_shapes=[pltpu.VMEM((KEYS, 128), F32)],
        compiler_params=params(),
        cost_estimate=cost(6),
        name="prep_rows",
    )(q, go, w)


def project_kernel(attn_ref, gp_ref, w_ref, out_ref, gw_ref, at, tmp):
    for g in range(GROUPS):
        rows = slice(g * 128, (g + 1) * 128)
        at[:, rows] = attn_ref[rows, :].T
        gw_ref[rows, :] = dot(attn_ref[rows, :], gp_ref[...])
    for c in range(8):
        for b in range(8):
            tmp[pl.ds(b, SLAB, stride=8), :] = dot(
                at[b * SLAB : (b + 1) * SLAB, :], w_ref[:, c * 128 : (c + 1) * 128]
            )
        out_ref[:, c * 128 : (c + 1) * 128] = tmp[...].astype(BF)


def project(attn, gp, w):
    return pl.pallas_call(
        project_kernel,
        out_shape=[
            jax.ShapeDtypeStruct((KEYS, 1024), BF),
            jax.ShapeDtypeStruct((512, 1024), F32),
        ],
        scratch_shapes=[pltpu.VMEM((KEYS, 512), BF), pltpu.VMEM((KEYS, 128), F32)],
        compiler_params=params(),
        cost_estimate=cost(7),
        name="project",
    )(attn, gp, w)


def finish_kernel(*refs):
    parts, (dk_ref, dv_ref, tmp) = refs[: 3 * GROUPS], refs[3 * GROUPS :]
    for g in range(GROUPS):
        own, kept, got = parts[3 * g : 3 * g + 3]
        for part, out in enumerate((dk_ref, dv_ref)):
            cols = slice(part * 128, (part + 1) * 128)
            for b in range(8):
                rows = slice(b * SLAB, (b + 1) * SLAB)
                half = slice(b // 2 * SLAB, (b // 2 + 1) * SLAB)
                tmp[pl.ds(b, SLAB, stride=8), :] = (
                    own[rows, cols] + 0.5 * kept[half, cols] + got[rows, cols].astype(F32)
                )
            out[:, g * 128 : (g + 1) * 128] = tmp[...].astype(BF)


def finish_keys(owns, kept, got):
    in_specs, args = [], []
    for (own, place), x, y in zip(owns, kept, got):
        in_specs.append(pl.BlockSpec((None, KEYS, 256), lambda i, place=place: (place, 0, 0)))
        in_specs += [pl.BlockSpec((512, 256), lambda i: (0, 0)), WHOLE]
        args += [own, x, y]
    return pl.pallas_call(
        finish_kernel,
        grid=(1,),
        in_specs=in_specs,
        out_specs=[pl.BlockSpec((KEYS, 512), lambda i: (0, 0))] * 2,
        out_shape=[jax.ShapeDtypeStruct((KEYS, 512), BF)] * 2,
        scratch_shapes=[pltpu.VMEM((KEYS, 128), F32)],
        compiler_params=params(),
        cost_estimate=cost(5),
        name="finish_keys",
    )(*args)


def partner(value, level):
    mask = MASKS[level]
    pairs = [(source, source ^ mask) for source in range(lax.axis_size("ctx"))]
    return lax.ppermute(value, "ctx", pairs)


def pool(x):
    y = x.astype(F32).reshape(4, 2, SLAB, 256)
    return (0.5 * (y[:, 0] + y[:, 1])).astype(BF).reshape(512, 256)


def spread(x):
    y = jnp.broadcast_to((0.5 * x).reshape(4, 1, SLAB, 256), (4, 2, SLAB, 256))
    return y.reshape(KEYS, 256)


def after(values, done):
    out = lax.optimization_barrier((*values, *done))
    return list(out[: len(values)])


def on_device(queries, key_states, value_states, grad_out, out_weight):
    held = [[x] for x in prep_keys(key_states[0], value_states[0])]
    far = [[] for _ in held]

    def send(g):
        far[g].append(partner(held[g][-1], len(far[g])))

    def pool_and_send(which, done):
        for g, x in zip(which, after([far[g][-1] for g in which], done)):
            far[g][-1] = x
            held[g].append(jnp.concatenate([pool(held[g][-1]), pool(x)], 0))
        made = [held[g][-1] for g in which]
        for g in which:
            send(g)
        return made

    own = [h[0] for h in held]
    for g in range(GROUPS):
        send(g)
    qT, gaT, gp = prep_rows(queries[0], grad_out[0], out_weight)

    p_own0, w_own0, st_own0 = block_forward(0, qT, own[:1])
    made = pool_and_send([0], [st_own0])
    (qT,) = after([qT], made)
    p_own1, w_own1, st_own1 = block_forward(1, qT, own[1:])
    made = pool_and_send([0, 1], [st_own1])
    (qT,) = after([qT], made)
    p_far0, w_far0, st_far0 = block_forward(0, qT, [far[0][0], far[1][0]])
    made = pool_and_send([0, 1, 2], [st_far0])
    (qT,) = after([qT], made)
    p_far2, w_far2, st_far2 = block_forward(2, qT, [far[2][0]])
    made = pool_and_send([1, 2, 3], [st_far2])
    (qT,) = after([qT], made)

    owns = [(w_own0, st_own0, 0)] + [(w_own1, st_own1, i) for i in range(3)]
    fars = [(w_far0, st_far0, 0), (w_far0, st_far0, 1), (w_far2, st_far2, 0)]
    attn = None
    dqs, gls, scales, grads, pending, sent = [], [], [], [], [], []

    def level_3_to_1(g):
        nonlocal attn
        attn, dq, gl, gs, f1, f2, f3 = group(g, qT, gaT, far[g][1:], owns[g], fars[g], attn)
        dqs.append(dq)
        gls.append(gl)
        scales.append(gs)
        grads.append([None, f1, f2, f3])
        sent.append(partner(f3, 3))
        pending.append(None)

    def pass_on(steps, done):
        made = []
        for (g, level), x in zip(steps, after([sent[g] for g, _ in steps], done)):
            x = x.astype(F32)
            full = x if pending[g] is None else spread(pending[g]) + x
            pending[g] = full[:512]
            outgoing = (grads[g][level].astype(F32) + spread(full[512:])).astype(BF)
            made.append(outgoing)
            sent[g] = partner(outgoing, level)
        return made

    level_3_to_1(0)
    made = pool_and_send([2, 3], [dqs[0]])
    (qT,) = after([qT], made)
    p_far3, w_far3, st_far3 = block_forward(3, qT, [far[3][0]])
    fars.append((w_far3, st_far3, 0))
    (qT,) = after([qT], [st_far3])
    level_3_to_1(1)
    made = pool_and_send([3], [dqs[1]]) + pass_on([(0, 2)], [dqs[1]])
    (qT,) = after([qT], made)
    level_3_to_1(2)
    made = pass_on([(0, 1), (1, 2)], [dqs[2]])
    (qT,) = after([qT], made)
    level_3_to_1(3)
    made = pass_on([(1, 1), (2, 2)], [dqs[3]])
    (attn,) = after([attn], made)
    outputs, weight_part = project(attn, gp, out_weight)
    (qT,) = after([qT], [outputs])

    def far_backward(first, p, n):
        which = range(first, first + n)
        dq, o = block_backward(
            first, qT, p, [far[g][0] for g in which], [gls[g] for g in which],
            [scales[g] for g in which], 1,
        )
        for i, g in enumerate(which):
            grads[g][0] = o[i]
        return dq

    dq_far0 = far_backward(0, p_far0, 2)
    made = pass_on([(0, 0), (1, 0), (2, 1), (3, 2)], [dq_far0])
    (qT,) = after([qT], made)
    dq_far2 = far_backward(2, p_far2, 1)
    made = pass_on([(2, 0), (3, 1)], [dq_far2])
    (qT,) = after([qT], made)
    dq_far3 = far_backward(3, p_far3, 1)
    (qT,) = after([qT], [dq_far3])
    other = [(dq_far0, 0), (dq_far0, 1), (dq_far2, 0), (dq_far3, 0)]
    dq, o_own0 = block_backward(
        0, qT, p_own0, own[:1], gls[:1], scales[:1], 0, dqs[:1], other[:1]
    )
    made = pass_on([(3, 0)], [o_own0])
    (qT,) = after([qT], made)
    rows = lax.psum_scatter(weight_part, "ctx", scatter_dimension=0, tiled=True)
    (qT,) = after([qT], [rows])
    dq, o_own1 = block_backward(
        1, qT, p_own1, own[1:], gls[1:], scales[1:], 0, dqs[1:], other[1:], dq
    )
    got = after(sent, [o_own1])
    grad_keys, grad_values = finish_keys(
        [(o_own0, 0)] + [(o_own1, i) for i in range(3)], pending, got
    )
    grad_weight = lax.psum_scatter(rows, "rep", scatter_dimension=1, tiled=True)
    return outputs[None], dq[None], grad_keys[None], grad_values[None], grad_weight


def solution(mesh):
    rows = P("rep", "ctx", None)
    return jax.shard_map(
        on_device,
        mesh=mesh,
        in_specs=(rows, rows, rows, rows, P()),
        out_specs=(rows, rows, rows, rows, P("ctx", "rep")),
        check_vma=False,
    )
```

```python
import functools

import jax
import jax.numpy as jnp
from jax import lax
from jax.experimental import pallas as pl
from jax.experimental.pallas import tpu as pltpu
from jax.sharding import PartitionSpec as P

F32 = jnp.float32
BF = jnp.bfloat16
KEYS = 1024
SLAB = 128
TW = 256
GROUPS = 4
MASKS = (1, 3, 4, 12)
NT = (((1,), (1,)), ((), ()))
NN = (((1,), (0,)), ((), ()))
LOG2E = 1.4426950408889634
CHUNK = 512
BACK = 256


def dot(a, b, dims=NN):
    return lax.dot_general(a, b, dims, preferred_element_type=F32)


def cost(us):
    return pl.CostEstimate(flops=int(us * 1.15e9), bytes_accessed=2**20, transcendentals=0)


def params(mib=58):
    return pltpu.CompilerParams(vmem_limit_bytes=mib * 2**20)


def score_keys(kv):
    k0, k1 = kv[:, 0:64], kv[:, 64:128]
    return jnp.concatenate([k0, k0, k1, k1], 1)


def grad_values_operand(kv):
    ones3 = (lax.broadcasted_iota(jnp.int32, (KEYS, 64), 1) < 3).astype(F32).astype(BF)
    return jnp.concatenate([kv[:, 128:192], ones3, kv[:, 192:256], ones3], 1)


def put_value_rows(ref, kv):
    ref[0:128] = kv[:, 128:256].T
    ref[128:144] = (lax.broadcasted_iota(jnp.int32, (16, KEYS), 0) == 0).astype(F32).astype(BF)


def put_query(qw, t, q):
    zero = jnp.zeros((128, SLAB), BF)
    qs = q.astype(F32) * (0.125 * LOG2E)
    hi = qs.astype(BF)
    lo = (qs - hi.astype(F32)).astype(BF)
    qw[t, 0:64, 0:128] = hi[0:64]
    qw[t, 64:128, 0:128] = lo[0:64]
    qw[t, 128:256, 0:128] = zero
    qw[t, 0:128, 128:256] = zero
    qw[t, 128:192, 128:256] = hi[64:128]
    qw[t, 192:256, 128:256] = lo[64:128]


def put_pair(ref, t, first, second):
    zero = jnp.zeros((64, SLAB), BF)
    off = t * TW
    ref[0:64, off : off + 128] = first
    ref[64:128, off : off + 128] = zero
    ref[0:64, off + 128 : off + 256] = zero
    ref[64:128, off + 128 : off + 256] = second


def put_scaled(qk, t, q):
    qq = (q.astype(F32) * 0.125).astype(BF)
    put_pair(qk, t, qq[0:64], qq[64:128])


def put_grad(gw, gk, t, g, scale):
    n = -scale
    hi = n.astype(BF).astype(F32)
    rest = n - hi
    mid = rest.astype(BF).astype(F32)
    row = lax.broadcasted_iota(jnp.int32, (64, TW), 0)
    low = jnp.where(row == 0, hi, jnp.where(row == 1, mid, jnp.where(row == 2, rest - mid, 0.0)))
    low = low.astype(BF)
    zero = jnp.zeros((128, SLAB), BF)
    gw[t, 0:64, 0:128] = g[:, 0:128]
    gw[t, 64:128, 0:128] = low[:, 0:128]
    gw[t, 128:256, 0:128] = zero
    gw[t, 0:128, 128:256] = zero
    gw[t, 128:192, 128:256] = g[:, 128:256]
    gw[t, 192:256, 128:256] = low[:, 128:256]
    put_pair(gk, t, g[:, 0:128], g[:, 128:256])


def both_heads(x):
    return jnp.concatenate([x[0:64, 0:128], x[64:128, 128:256]], 1)


def forward_step(nxt, cur):
    if nxt is not None:
        keys, query, sn, mn = nxt
        top = None
    if cur is not None:
        values, p_ref, off, sc, mc, w_ref, st_ref, t = cur
        m = mc[0:1]
        w = None
    for c in range(KEYS // CHUNK):
        r = slice(c * CHUNK, (c + 1) * CHUNK)
        if nxt is not None:
            s = dot(keys(r), query())
            sn[r] = s
            x = jnp.max(s.reshape(CHUNK // 8, 8, TW), axis=0)
            top = x if top is None else jnp.maximum(top, x)
        if cur is not None:
            p = jnp.exp2(sc[r] - m).astype(BF)
            p_ref(r, off, p)
            y = dot(values(r), p)
            w = y if w is None else w + y
    if nxt is not None:
        mn[0:1] = jnp.max(top, axis=0, keepdims=True)
    if cur is not None:
        w_ref(t, both_heads(w))
        st_ref(t, m, w[128:129])


def forward_tiles(count, score, value, sa, sb, ma, mb):
    forward_step(score(jnp.int32(0), sa, ma), None)

    def body(i, c):
        t = 2 * i
        forward_step(score(t + 1, sb, mb), value(t, sa, ma))
        forward_step(score(t + 2, sa, ma), value(t + 1, sb, mb))
        return c

    steps = (count - 1) // 2
    lax.fori_loop(0, steps, body, 0)
    t = jnp.int32(2 * steps)
    if count % 2 == 0:
        forward_step(score(t + 1, sb, mb), value(t, sa, ma))
        forward_step(None, value(t + 1, sb, mb))
    else:
        forward_step(None, value(t, sa, ma))


def tile_cols(t):
    if isinstance(t, int):
        return slice(t * TW, (t + 1) * TW)
    return pl.ds(pl.multiple_of(t * TW, TW), TW)


def select(refs, use):
    for i, ref in enumerate(refs):
        pl.when(pl.program_id(0) == i)(functools.partial(use, ref))


def block_forward_kernel(n, q_ref, *refs):
    kvs, (p_ref, w_ref, st_ref, kk, vT, qw, sa, sb, ma, mb) = refs[:n], refs[n:]

    def prepare(kv_ref):
        kv = kv_ref[...]
        kk[...] = score_keys(kv)
        put_value_rows(vT, kv)

    select(kvs, prepare)
    for j in range(8):
        put_query(qw, j, q_ref[:, j * SLAB : (j + 1) * SLAB])

    def put_p(r, t, p):
        p_ref[r, tile_cols(t)] = p

    def put_w(t, w):
        w_ref[t] = w

    def put_st(t, m, total):
        st_ref[t, 0:1] = m
        st_ref[t, 1:2] = total

    def score(t, s, m):
        return (lambda r: kk[r], lambda: qw[t], s, m)

    def value(t, s, m):
        return (lambda r: vT[:, r], put_p, t, s, m, put_w, put_st, t)

    forward_tiles(8, score, value, sa, sb, ma, mb)


WHOLE = pl.BlockSpec((KEYS, 256), lambda i: (0, 0))


def block_forward(first, qT, kvs):
    n = len(kvs)
    return pl.pallas_call(
        functools.partial(block_forward_kernel, n),
        grid=(n,),
        in_specs=[pl.BlockSpec((128, KEYS), lambda i: (first + i, 0))] + [WHOLE] * n,
        out_specs=[
            pl.BlockSpec((None, KEYS, 8 * TW), lambda i: (i, 0, 0)),
            pl.BlockSpec((None, 8, 64, TW), lambda i: (i, 0, 0, 0)),
            pl.BlockSpec((None, 8, 8, TW), lambda i: (i, 0, 0, 0)),
        ],
        out_shape=[
            jax.ShapeDtypeStruct((n, KEYS, 8 * TW), BF),
            jax.ShapeDtypeStruct((n, 8, 64, TW), F32),
            jax.ShapeDtypeStruct((n, 8, 8, TW), F32),
        ],
        scratch_shapes=[
            pltpu.VMEM((KEYS, 256), BF),
            pltpu.VMEM((144, KEYS), BF),
            pltpu.VMEM((8, 256, TW), BF),
            pltpu.VMEM((KEYS, TW), F32),
            pltpu.VMEM((KEYS, TW), F32),
            pltpu.VMEM((8, TW), F32),
            pltpu.VMEM((8, TW), F32),
        ],
        compiler_params=params(),
        cost_estimate=cost(5 * n),
        name="block_forward",
    )(qT, *kvs)


def backward_tiles(blocks, va, kT, qk, gw, gk, p_ref, ds_ref, dqt, outs, pieces):
    rows_of = KEYS // BACK
    items = [(b, t, c) for b, first, n in blocks for t in range(first, first + n) for c in range(rows_of)]
    ends = {first + n - 1: (b, first, n) for b, first, n in blocks}
    grads, scores, dqs, fill = {}, {}, {}, []

    def sums(b, first, n, left, right, lanes, count):
        cols = slice(first * TW, (first + n) * TW)

        def piece(rows):
            outs[b][rows, lanes] = dot(left[rows, cols], right[:, cols], NT).astype(outs[b].dtype)

        step = KEYS // count
        return [functools.partial(piece, slice(i * step, (i + 1) * step)) for i in range(count)]

    def issue(n):
        if n < len(items):
            b, t, c = items[n]
            grads[n] = dot(va(b, slice(c * BACK, (c + 1) * BACK)), gw[t])

    for block in blocks:
        fill += sums(*block, p_ref, gk, slice(128, 256), pieces)
    issue(0)
    issue(1)
    for n, (b, t, c) in enumerate(items):
        issue(n + 2)
        r = slice(c * BACK, (c + 1) * BACK)
        ds = (p_ref[r, tile_cols(t)].astype(F32) * grads.pop(n)).astype(BF)
        ds_ref[r, tile_cols(t)] = ds
        if c == 0 and fill:
            fill.pop(0)()
        y = dot(kT(b, r), ds)
        dqs[t] = y if c == 0 else dqs[t] + y
        if c == rows_of - 1:
            dqt[t] = both_heads(dqs.pop(t))
            if t in ends:
                last = t == items[-1][1]
                fill += sums(*ends[t], ds_ref, qk, slice(0, 128), 1 if last else pieces)
    while fill:
        fill.pop(0)()


FAR_TILES = 7
FAR_BLOCKS = ((0, 0, 4), (1, 4, 2), (2, 6, 1))


def far_block(t):
    one = lambda at: (t >= at).astype(jnp.int32)
    return one(4) + one(6)


def group_kernel(
    chained, q_ref, ga_ref, kv1, kv2, kv3, wa_ref, sta_ref, wb_ref, stb_ref, *refs
):
    if chained:
        refs = refs[1:]
    (
        attn_ref, dq_ref, g_ref, gs_ref, o1, o2, o3,
        kk, va, kT, vT, qw, qk, gw, gk, p_ref, ds_ref, w_ref, st_ref, dqt, sa, sb, ma, mb,
    ) = refs
    kvs, outs = (kv1, kv2, kv3), (o1, o2, o3)
    for b in range(3):
        kv = kvs[b][...]
        kk[b] = score_keys(kv)
        va[b] = grad_values_operand(kv)
        kT[b] = kv[:, 0:128].T
        put_value_rows(vT.at[b], kv)
    level = [q_ref[:, j * SLAB : (j + 1) * SLAB] for j in range(8)]
    first = 0
    for _ in range(3):
        level = [
            (0.5 * (level[2 * c].astype(F32) + level[2 * c + 1].astype(F32))).astype(BF)
            for c in range(len(level) // 2)
        ]
        for c, x in enumerate(level):
            put_query(qw, first + c, x)
            put_scaled(qk, first + c, x)
        first += len(level)

    def put_p(r, t, p):
        p_ref[r, tile_cols(t)] = p

    def put_w(t, w):
        w_ref[t] = w

    def put_st(t, m, total):
        st_ref[t, 0:1] = m
        st_ref[t, 1:2] = total

    def score(t, s, m):
        b = far_block(t)
        return (lambda r: kk[b, r], lambda: qw[t], s, m)

    def value(t, s, m):
        b = far_block(t)
        return (lambda r: vT[b, :, r], put_p, t, s, m, put_w, put_st, t)

    forward_tiles(FAR_TILES, score, value, sa, sb, ma, mb)

    gl, gs = [None] * FAR_TILES, [None] * FAR_TILES
    for j in range(8):
        ts = [j // 2, 4 + j // 4, 6]
        ms = [sta_ref[j, 0:1], stb_ref[j, 0:1]] + [st_ref[t, 0:1] for t in ts]
        totals = [sta_ref[j, 1:2], stb_ref[j, 1:2]] + [st_ref[t, 1:2] for t in ts]
        ws = [wa_ref[j], wb_ref[j]] + [w_ref[t] for t in ts]
        top = functools.reduce(jnp.maximum, ms)
        factors = [jnp.exp2(m - top) * c for m, c in zip(ms, (1.0, 1.0, 2.0, 4.0, 8.0))]
        inv = 1.0 / functools.reduce(jnp.add, [f * x for f, x in zip(factors, totals)])
        shares = [f * inv for f in factors]
        at = functools.reduce(jnp.add, [s * w for s, w in zip(shares, ws)]).astype(BF)
        cols = slice(j * SLAB, (j + 1) * SLAB)
        attn_ref[0:64, cols] = at[:, 0:128]
        attn_ref[64:128, cols] = at[:, 128:256]
        ga = jnp.concatenate([ga_ref[0:64, cols], ga_ref[64:128, cols]], 1).astype(F32)
        delta = jnp.sum(ga * at.astype(F32), axis=0, keepdims=True)
        for side in range(2):
            g_ref[side, j] = (shares[side] * ga).astype(BF)
            gs_ref[side, j, 0:1] = shares[side] * delta
        for s, t in zip(shares[2:], ts):
            x, y = s * ga, s * delta
            gl[t] = x if gl[t] is None else gl[t] + x
            gs[t] = y if gs[t] is None else gs[t] + y
    for t in range(FAR_TILES):
        put_grad(gw, gk, t, gl[t].astype(BF), gs[t])

    backward_tiles(
        FAR_BLOCKS, lambda b, r: va[b, r], lambda b, r: kT[b, :, r],
        qk, gw, gk, p_ref, ds_ref, dqt, outs, 4,
    )
    for j in range(8):
        dq_ref[j] = 0.5 * dqt[j // 2] + 0.25 * dqt[4 + j // 4] + 0.125 * dqt[6]


def group(g, qT, gaT, kvs, own, far, attn):
    cols = pl.BlockSpec((128, KEYS), lambda i: (g, 0))
    tiles = lambda rows: pl.BlockSpec((2, 8, rows, TW), lambda i: (0, 0, 0, 0))
    at = lambda place, rows: pl.BlockSpec((None, 8, rows, TW), lambda i: (place, 0, 0, 0))
    chain = [] if attn is None else [attn]
    return pl.pallas_call(
        functools.partial(group_kernel, bool(chain)),
        grid=(1,),
        in_specs=[cols, cols]
        + [WHOLE] * 3
        + [at(own[2], 64), at(own[2], 8), at(far[2], 64), at(far[2], 8)]
        + [pl.BlockSpec(memory_space=pl.ANY) for _ in chain],
        out_specs=[cols, pl.BlockSpec((8, 64, TW), lambda i: (0, 0, 0)), tiles(64), tiles(8)]
        + [WHOLE] * 3,
        out_shape=[
            jax.ShapeDtypeStruct((512, KEYS), BF),
            jax.ShapeDtypeStruct((8, 64, TW), F32),
            jax.ShapeDtypeStruct((2, 8, 64, TW), BF),
            jax.ShapeDtypeStruct((2, 8, 8, TW), F32),
        ]
        + [jax.ShapeDtypeStruct((KEYS, 256), BF)] * 3,
        scratch_shapes=[
            pltpu.VMEM((3, KEYS, 256), BF),
            pltpu.VMEM((3, KEYS, 256), BF),
            pltpu.VMEM((3, 128, KEYS), BF),
            pltpu.VMEM((3, 144, KEYS), BF),
            pltpu.VMEM((FAR_TILES, 256, TW), BF),
            pltpu.VMEM((128, FAR_TILES * TW), BF),
            pltpu.VMEM((FAR_TILES, 256, TW), BF),
            pltpu.VMEM((128, FAR_TILES * TW), BF),
            pltpu.VMEM((KEYS, FAR_TILES * TW), BF),
            pltpu.VMEM((KEYS, FAR_TILES * TW), BF),
            pltpu.VMEM((FAR_TILES, 64, TW), F32),
            pltpu.VMEM((FAR_TILES, 8, TW), F32),
            pltpu.VMEM((FAR_TILES, 64, TW), F32),
            pltpu.VMEM((KEYS, TW), F32),
            pltpu.VMEM((KEYS, TW), F32),
            pltpu.VMEM((8, TW), F32),
            pltpu.VMEM((8, TW), F32),
        ],
        input_output_aliases={9: 0} if chain else {},
        compiler_params=params(),
        cost_estimate=cost(16),
        name="group",
    )(qT, gaT, *kvs, *own[:2], *far[:2], *chain)


def block_backward_kernel(n, last, chained, q_ref, p_ref, *refs):
    take = lambda: (refs[:n], refs[n:])
    kvs, refs = take()
    gls, refs = take()
    scales, refs = take()
    if last:
        upper, refs = take()
        other, refs = take()
    if chained:
        refs = refs[1:]
    dq_ref, o_ref, va, kT, qk, gw, gk, ds_ref, dqt, tmp = refs
    for i in range(n):

        @pl.when(pl.program_id(0) == i)
        def _(i=i):
            kv = kvs[i][...]
            va[...] = grad_values_operand(kv)
            kT[...] = kv[:, 0:128].T
            for j in range(8):
                put_grad(gw, gk, j, gls[i][j], scales[i][j, 0:1])

    for j in range(8):
        put_scaled(qk, j, q_ref[:, j * SLAB : (j + 1) * SLAB])

    backward_tiles(
        ((0, 0, 8),), lambda b, r: va[r], lambda b, r: kT[:, r],
        qk, gw, gk, p_ref, ds_ref, dqt, (o_ref,), 8,
    )
    if not last:
        dq_ref[...] = dqt[...]
        return
    for i in range(n):

        @pl.when(pl.program_id(0) == i)
        def _(i=i):
            for j in range(8):
                dqt[j] = dqt[j] + upper[i][j] + other[i][j]

    for j in range(8):
        d = 0.125 * dqt[j]
        tmp[pl.ds(j, SLAB, stride=8), :] = jnp.concatenate([d[:, 0:128], d[:, 128:256]], 0).T
    dq_ref[...] = tmp[...].astype(BF)


def block_backward(first, qT, p, kvs, gls, scales, side, upper=None, other=None, dq=None):
    n = len(kvs)
    last = upper is not None
    chain = [] if dq is None else [dq]
    of_side = lambda rows: pl.BlockSpec((None, 8, rows, TW), lambda i: (side, 0, 0, 0))
    at = lambda place: pl.BlockSpec((None, 8, 64, TW), lambda i: (place, 0, 0, 0))
    in_specs = [
        pl.BlockSpec((128, KEYS), lambda i: (first + i, 0)),
        pl.BlockSpec((None, KEYS, 8 * TW), lambda i: (i, 0, 0)),
    ]
    in_specs += [WHOLE] * n + [of_side(64)] * n + [of_side(8)] * n
    args = [qT, p, *kvs, *gls, *scales]
    if last:
        in_specs += [pl.BlockSpec((8, 64, TW), lambda i: (0, 0, 0))] * n
        in_specs += [at(place) for _, place in other]
        args += [*upper, *[part for part, _ in other]]
        dq_spec = pl.BlockSpec((KEYS, 128), lambda i: (0, first + i))
        dq_shape = jax.ShapeDtypeStruct((KEYS, 512), BF)
    else:
        dq_spec = pl.BlockSpec((None, 8, 64, TW), lambda i: (i, 0, 0, 0))
        dq_shape = jax.ShapeDtypeStruct((n, 8, 64, TW), F32)
    in_specs += [pl.BlockSpec(memory_space=pl.ANY) for _ in chain]
    return pl.pallas_call(
        functools.partial(block_backward_kernel, n, last, bool(chain)),
        grid=(n,),
        in_specs=in_specs,
        out_specs=[dq_spec, pl.BlockSpec((None, KEYS, 256), lambda i: (i, 0, 0))],
        out_shape=[dq_shape, jax.ShapeDtypeStruct((n, KEYS, 256), F32 if last else BF)],
        scratch_shapes=[
            pltpu.VMEM((KEYS, 256), BF),
            pltpu.VMEM((128, KEYS), BF),
            pltpu.VMEM((128, 8 * TW), BF),
            pltpu.VMEM((8, 256, TW), BF),
            pltpu.VMEM((128, 8 * TW), BF),
            pltpu.VMEM((KEYS, 8 * TW), BF),
            pltpu.VMEM((8, 64, TW), F32),
            pltpu.VMEM((KEYS, 128), F32),
        ],
        input_output_aliases={len(args): 0} if chain else {},
        compiler_params=params(),
        cost_estimate=cost(10 * n),
        name="block_backward",
    )(*args, *chain)


def keys_kernel(k_ref, v_ref, o0, o1, o2, o3, tmp):
    outs = (o0, o1, o2, o3)
    for part, src in enumerate((k_ref, v_ref)):
        for g in range(GROUPS):
            tmp[...] = src[:, g * 128 : (g + 1) * 128].astype(F32)
            for b in range(8):
                outs[g][b * SLAB : (b + 1) * SLAB, part * 128 : (part + 1) * 128] = tmp[
                    pl.ds(b, SLAB, stride=8), :
                ].astype(BF)


def prep_keys(k, v):
    return pl.pallas_call(
        keys_kernel,
        out_shape=[jax.ShapeDtypeStruct((KEYS, 256), BF)] * GROUPS,
        scratch_shapes=[pltpu.VMEM((KEYS, 128), F32)],
        compiler_params=params(),
        cost_estimate=cost(3),
        name="prep_keys",
    )(k, v)


def rows_kernel(q_ref, go_ref, w_ref, qT_ref, gaT_ref, gp_ref, tmp):
    for g in range(GROUPS):
        tmp[...] = q_ref[:, g * 128 : (g + 1) * 128].astype(F32)
        for b in range(8):
            x = tmp[pl.ds(b, SLAB, stride=8), :]
            qT_ref[g * 128 : (g + 1) * 128, b * SLAB : (b + 1) * SLAB] = x.T.astype(BF)
    for c in range(8):
        tmp[...] = go_ref[:, c * 128 : (c + 1) * 128].astype(F32)
        for b in range(8):
            gp_ref[b * SLAB : (b + 1) * SLAB, c * 128 : (c + 1) * 128] = tmp[
                pl.ds(b, SLAB, stride=8), :
            ].astype(BF)
    for c in range(4):
        rows = pl.ds(c * 256, 256)
        gaT_ref[:, c * 256 : (c + 1) * 256] = dot(w_ref[...], gp_ref[rows, :], NT).astype(BF)


def prep_rows(q, go, w):
    return pl.pallas_call(
        rows_kernel,
        out_shape=[
            jax.ShapeDtypeStruct((512, KEYS), BF),
            jax.ShapeDtypeStruct((512, KEYS), BF),
            jax.ShapeDtypeStruct((KEYS, 1024), BF),
        ],
        scratch_shapes=[pltpu.VMEM((KEYS, 128), F32)],
        compiler_params=params(),
        cost_estimate=cost(6),
        name="prep_rows",
    )(q, go, w)


def project_kernel(attn_ref, gp_ref, w_ref, out_ref, gw_ref, at, tmp):
    for g in range(GROUPS):
        rows = slice(g * 128, (g + 1) * 128)
        at[:, rows] = attn_ref[rows, :].T
        for c in range(4):
            x = dot(attn_ref[rows, :], gp_ref[:, c * 256 : (c + 1) * 256])
            gw_ref[2 * c, rows, :] = x[:, 0:128]
            gw_ref[2 * c + 1, rows, :] = x[:, 128:256]
    for c in range(8):
        for b in range(8):
            tmp[pl.ds(b, SLAB, stride=8), :] = dot(
                at[b * SLAB : (b + 1) * SLAB, :], w_ref[:, c * 128 : (c + 1) * 128]
            )
        out_ref[:, c * 128 : (c + 1) * 128] = tmp[...].astype(BF)


def project(attn, gp, w):
    return pl.pallas_call(
        project_kernel,
        out_shape=[
            jax.ShapeDtypeStruct((KEYS, 1024), BF),
            jax.ShapeDtypeStruct((8, 512, 128), F32),
        ],
        scratch_shapes=[pltpu.VMEM((KEYS, 512), BF), pltpu.VMEM((KEYS, 128), F32)],
        compiler_params=params(),
        cost_estimate=cost(7),
        name="project",
    )(attn, gp, w)


def finish_kernel(*refs):
    parts, (dk_ref, dv_ref, tmp) = refs[: 3 * GROUPS], refs[3 * GROUPS :]
    for g in range(GROUPS):
        own, kept, got = parts[3 * g : 3 * g + 3]
        for part, out in enumerate((dk_ref, dv_ref)):
            cols = slice(part * 128, (part + 1) * 128)
            for b in range(8):
                rows = slice(b * SLAB, (b + 1) * SLAB)
                half = slice(b // 2 * SLAB, (b // 2 + 1) * SLAB)
                tmp[pl.ds(b, SLAB, stride=8), :] = (
                    own[rows, cols] + 0.5 * kept[half, cols] + got[rows, cols].astype(F32)
                )
            out[:, g * 128 : (g + 1) * 128] = tmp[...].astype(BF)


def finish_keys(owns, kept, got):
    in_specs, args = [], []
    for (own, place), x, y in zip(owns, kept, got):
        in_specs.append(pl.BlockSpec((None, KEYS, 256), lambda i, place=place: (place, 0, 0)))
        in_specs += [pl.BlockSpec((512, 256), lambda i: (0, 0)), WHOLE]
        args += [own, x, y]
    return pl.pallas_call(
        finish_kernel,
        grid=(1,),
        in_specs=in_specs,
        out_specs=[pl.BlockSpec((KEYS, 512), lambda i: (0, 0))] * 2,
        out_shape=[jax.ShapeDtypeStruct((KEYS, 512), BF)] * 2,
        scratch_shapes=[pltpu.VMEM((KEYS, 128), F32)],
        compiler_params=params(),
        cost_estimate=cost(5),
        name="finish_keys",
    )(*args)


def partner(value, level):
    mask = MASKS[level]
    pairs = [(source, source ^ mask) for source in range(lax.axis_size("ctx"))]
    return lax.ppermute(value, "ctx", pairs)


def pool(x):
    y = x.astype(F32).reshape(4, 2, SLAB, 256)
    return (0.5 * (y[:, 0] + y[:, 1])).astype(BF).reshape(512, 256)


def spread(x):
    n = x.shape[0] // SLAB
    y = jnp.broadcast_to((0.5 * x).reshape(n, 1, SLAB, 256), (n, 2, SLAB, 256))
    return y.reshape(2 * x.shape[0], 256)


def after(values, done):
    out = lax.optimization_barrier((*values, *done))
    return list(out[: len(values)])


def on_device(queries, key_states, value_states, grad_out, out_weight):
    held = [[x] for x in prep_keys(key_states[0], value_states[0])]
    far = [[] for _ in held]

    def send(g):
        far[g].append(partner(held[g][-1], len(far[g])))

    def pool_and_send(which, done):
        for g, x in zip(which, after([far[g][-1] for g in which], done)):
            far[g][-1] = x
            held[g].append(jnp.concatenate([pool(held[g][-1]), pool(x)], 0))
        made = [held[g][-1] for g in which]
        for g in which:
            send(g)
        return made

    own = [h[0] for h in held]
    for g in range(GROUPS):
        send(g)
    qT, gaT, gp = prep_rows(queries[0], grad_out[0], out_weight)

    p_own0, w_own0, st_own0 = block_forward(0, qT, own[:1])
    made = pool_and_send([0], [st_own0])
    (qT,) = after([qT], made)
    p_own1, w_own1, st_own1 = block_forward(1, qT, own[1:])
    made = pool_and_send([0, 1], [st_own1])
    (qT,) = after([qT], made)
    p_far0, w_far0, st_far0 = block_forward(0, qT, [far[0][0], far[1][0]])
    made = pool_and_send([0, 1, 2], [st_far0])
    (qT,) = after([qT], made)
    p_far2, w_far2, st_far2 = block_forward(2, qT, [far[2][0]])
    made = pool_and_send([1, 2, 3], [st_far2])
    (qT,) = after([qT], made)

    owns = [(w_own0, st_own0, 0)] + [(w_own1, st_own1, i) for i in range(3)]
    fars = [(w_far0, st_far0, 0), (w_far0, st_far0, 1), (w_far2, st_far2, 0)]
    attn = None
    dqs, gls, scales, grads, pending, sent = [], [], [], [], [], []

    def level_3_to_1(g):
        nonlocal attn
        attn, dq, gl, gs, f1, f2, f3 = group(g, qT, gaT, far[g][1:], owns[g], fars[g], attn)
        dqs.append(dq)
        gls.append(gl)
        scales.append(gs)
        grads.append([None, f1, f2, f3])
        sent.append(partner(f3, 3))
        pending.append(None)

    def pass_on(steps, done):
        made = []
        for (g, level), x in zip(steps, after([sent[g] for g, _ in steps], done)):
            x = x.astype(F32)
            low, high = x[:512], x[512:]
            if pending[g] is not None:
                low = spread(pending[g][:256]) + low
                high = spread(pending[g][256:]) + high
            pending[g] = low
            outgoing = (grads[g][level].astype(F32) + spread(high)).astype(BF)
            made.append(outgoing)
            sent[g] = partner(outgoing, level)
        return made

    level_3_to_1(0)
    made = pool_and_send([2, 3], [dqs[0]])
    (qT,) = after([qT], made)
    p_far3, w_far3, st_far3 = block_forward(3, qT, [far[3][0]])
    fars.append((w_far3, st_far3, 0))
    (qT,) = after([qT], [st_far3])
    level_3_to_1(1)
    made = pool_and_send([3], [dqs[1]]) + pass_on([(0, 2)], [dqs[1]])
    (qT,) = after([qT], made)
    level_3_to_1(2)
    made = pass_on([(0, 1), (1, 2)], [dqs[2]])
    (qT,) = after([qT], made)
    level_3_to_1(3)
    made = pass_on([(1, 1), (2, 2)], [dqs[3]])
    (attn,) = after([attn], made)
    outputs, weight_part = project(attn, gp, out_weight)
    (qT,) = after([qT], [outputs])

    def far_backward(first, p, n):
        which = range(first, first + n)
        dq, o = block_backward(
            first, qT, p, [far[g][0] for g in which], [gls[g] for g in which],
            [scales[g] for g in which], 1,
        )
        for i, g in enumerate(which):
            grads[g][0] = o[i]
        return dq

    dq_far0 = far_backward(0, p_far0, 2)
    made = pass_on([(0, 0), (1, 0), (2, 1), (3, 2)], [dq_far0])
    (qT,) = after([qT], made)
    dq_far2 = far_backward(2, p_far2, 1)
    made = pass_on([(2, 0), (3, 1)], [dq_far2])
    (qT,) = after([qT], made)
    dq_far3 = far_backward(3, p_far3, 1)
    (qT,) = after([qT], [dq_far3])
    other = [(dq_far0, 0), (dq_far0, 1), (dq_far2, 0), (dq_far3, 0)]
    dq, o_own0 = block_backward(
        0, qT, p_own0, own[:1], gls[:1], scales[:1], 0, dqs[:1], other[:1]
    )
    made = pass_on([(3, 0)], [o_own0])
    (qT,) = after([qT], made)
    dq, o_own1 = block_backward(
        1, qT, p_own1, own[1:], gls[1:], scales[1:], 0, dqs[1:], other[1:], dq
    )
    got = after(sent, [o_own1])
    grad_keys, grad_values = finish_keys(
        [(o_own0, 0)] + [(o_own1, i) for i in range(3)], pending, got
    )
    grad_weight = lax.psum_scatter(
        weight_part.reshape(KEYS * 4, 128), ("rep", "ctx"), scatter_dimension=0, tiled=True
    )
    return outputs[None], dq[None], grad_keys[None], grad_values[None], grad_weight


def solution(mesh):
    rows = P("rep", "ctx", None)
    return jax.shard_map(
        on_device,
        mesh=mesh,
        in_specs=(rows, rows, rows, rows, P()),
        out_specs=(rows, rows, rows, rows, P("ctx", "rep")),
        check_vma=False,
    )
```

```python
import functools

import jax
import jax.numpy as jnp
from jax import lax
from jax.experimental import pallas as pl
from jax.experimental.pallas import tpu as pltpu
from jax.sharding import PartitionSpec as P

F32 = jnp.float32
BF = jnp.bfloat16
KEYS = 1024
SLAB = 128
TW = 256
GROUPS = 4
MASKS = (1, 3, 4, 12)
NT = (((1,), (1,)), ((), ()))
NN = (((1,), (0,)), ((), ()))
LOG2E = 1.4426950408889634
CHUNK = 512
BACK = 256


def dot(a, b, dims=NN):
    return lax.dot_general(a, b, dims, preferred_element_type=F32)


def cost(us):
    return pl.CostEstimate(flops=int(us * 1.15e9), bytes_accessed=2**20, transcendentals=0)


def params(mib=58):
    return pltpu.CompilerParams(vmem_limit_bytes=mib * 2**20)


def score_keys(kv):
    k0, k1 = kv[:, 0:64], kv[:, 64:128]
    return jnp.concatenate([k0, k0, k1, k1], 1)


def grad_values_operand(kv):
    ones3 = (lax.broadcasted_iota(jnp.int32, (KEYS, 64), 1) < 3).astype(F32).astype(BF)
    return jnp.concatenate([kv[:, 128:192], ones3, kv[:, 192:256], ones3], 1)


def put_value_rows(ref, kv):
    ref[0:128] = kv[:, 128:256].T
    ref[128:144] = (lax.broadcasted_iota(jnp.int32, (16, KEYS), 0) == 0).astype(F32).astype(BF)


def put_query(qw, t, q):
    zero = jnp.zeros((128, SLAB), BF)
    qs = q.astype(F32) * (0.125 * LOG2E)
    hi = qs.astype(BF)
    lo = (qs - hi.astype(F32)).astype(BF)
    qw[t, 0:64, 0:128] = hi[0:64]
    qw[t, 64:128, 0:128] = lo[0:64]
    qw[t, 128:256, 0:128] = zero
    qw[t, 0:128, 128:256] = zero
    qw[t, 128:192, 128:256] = hi[64:128]
    qw[t, 192:256, 128:256] = lo[64:128]


def put_pair(ref, t, first, second):
    zero = jnp.zeros((64, SLAB), BF)
    off = t * TW
    ref[0:64, off : off + 128] = first
    ref[64:128, off : off + 128] = zero
    ref[0:64, off + 128 : off + 256] = zero
    ref[64:128, off + 128 : off + 256] = second


def put_scaled(qk, t, q):
    qq = (q.astype(F32) * 0.125).astype(BF)
    put_pair(qk, t, qq[0:64], qq[64:128])


def put_grad(gw, gk, t, g, scale):
    n = -scale
    hi = n.astype(BF).astype(F32)
    rest = n - hi
    mid = rest.astype(BF).astype(F32)
    row = lax.broadcasted_iota(jnp.int32, (64, TW), 0)
    low = jnp.where(row == 0, hi, jnp.where(row == 1, mid, jnp.where(row == 2, rest - mid, 0.0)))
    low = low.astype(BF)
    zero = jnp.zeros((128, SLAB), BF)
    gw[t, 0:64, 0:128] = g[:, 0:128]
    gw[t, 64:128, 0:128] = low[:, 0:128]
    gw[t, 128:256, 0:128] = zero
    gw[t, 0:128, 128:256] = zero
    gw[t, 128:192, 128:256] = g[:, 128:256]
    gw[t, 192:256, 128:256] = low[:, 128:256]
    put_pair(gk, t, g[:, 0:128], g[:, 128:256])


def both_heads(x):
    return jnp.concatenate([x[0:64, 0:128], x[64:128, 128:256]], 1)


def forward_step(nxt, cur):
    if nxt is not None:
        keys, query, sn, mn = nxt
        top = None
    if cur is not None:
        values, p_ref, off, sc, mc, w_ref, st_ref, t = cur
        m = mc[0:1]
        w = None
    for c in range(KEYS // CHUNK):
        r = slice(c * CHUNK, (c + 1) * CHUNK)
        if nxt is not None:
            s = dot(keys(r), query())
            sn[r] = s
            x = jnp.max(s.reshape(CHUNK // 8, 8, TW), axis=0)
            top = x if top is None else jnp.maximum(top, x)
        if cur is not None:
            p = jnp.exp2(sc[r] - m).astype(BF)
            p_ref(r, off, p)
            y = dot(values(r), p)
            w = y if w is None else w + y
    if nxt is not None:
        mn[0:1] = jnp.max(top, axis=0, keepdims=True)
    if cur is not None:
        w_ref(t, both_heads(w))
        st_ref(t, m, w[128:129])


def forward_tiles(count, score, value, sa, sb, ma, mb):
    forward_step(score(jnp.int32(0), sa, ma), None)

    def body(i, c):
        t = 2 * i
        forward_step(score(t + 1, sb, mb), value(t, sa, ma))
        forward_step(score(t + 2, sa, ma), value(t + 1, sb, mb))
        return c

    steps = (count - 1) // 2
    lax.fori_loop(0, steps, body, 0)
    t = jnp.int32(2 * steps)
    if count % 2 == 0:
        forward_step(score(t + 1, sb, mb), value(t, sa, ma))
        forward_step(None, value(t + 1, sb, mb))
    else:
        forward_step(None, value(t, sa, ma))


def tile_cols(t):
    if isinstance(t, int):
        return slice(t * TW, (t + 1) * TW)
    return pl.ds(pl.multiple_of(t * TW, TW), TW)


def select(refs, use):
    for i, ref in enumerate(refs):
        pl.when(pl.program_id(0) == i)(functools.partial(use, ref))


def block_forward_kernel(n, q_ref, *refs):
    kvs, (p_ref, w_ref, st_ref, kk, vT, qw, sa, sb, ma, mb) = refs[:n], refs[n:]

    def prepare(kv_ref):
        kv = kv_ref[...]
        kk[...] = score_keys(kv)
        put_value_rows(vT, kv)

    select(kvs, prepare)
    for j in range(8):
        put_query(qw, j, q_ref[:, j * SLAB : (j + 1) * SLAB])

    def put_p(r, t, p):
        p_ref[r, tile_cols(t)] = p

    def put_w(t, w):
        w_ref[t] = w

    def put_st(t, m, total):
        st_ref[t, 0:1] = m
        st_ref[t, 1:2] = total

    def score(t, s, m):
        return (lambda r: kk[r], lambda: qw[t], s, m)

    def value(t, s, m):
        return (lambda r: vT[:, r], put_p, t, s, m, put_w, put_st, t)

    forward_tiles(8, score, value, sa, sb, ma, mb)


WHOLE = pl.BlockSpec((KEYS, 256), lambda i: (0, 0))


def block_forward(first, qT, kvs):
    n = len(kvs)
    return pl.pallas_call(
        functools.partial(block_forward_kernel, n),
        grid=(n,),
        in_specs=[pl.BlockSpec((128, KEYS), lambda i: (first + i, 0))] + [WHOLE] * n,
        out_specs=[
            pl.BlockSpec((None, KEYS, 8 * TW), lambda i: (i, 0, 0)),
            pl.BlockSpec((None, 8, 64, TW), lambda i: (i, 0, 0, 0)),
            pl.BlockSpec((None, 8, 8, TW), lambda i: (i, 0, 0, 0)),
        ],
        out_shape=[
            jax.ShapeDtypeStruct((n, KEYS, 8 * TW), BF),
            jax.ShapeDtypeStruct((n, 8, 64, TW), F32),
            jax.ShapeDtypeStruct((n, 8, 8, TW), F32),
        ],
        scratch_shapes=[
            pltpu.VMEM((KEYS, 256), BF),
            pltpu.VMEM((144, KEYS), BF),
            pltpu.VMEM((8, 256, TW), BF),
            pltpu.VMEM((KEYS, TW), F32),
            pltpu.VMEM((KEYS, TW), F32),
            pltpu.VMEM((8, TW), F32),
            pltpu.VMEM((8, TW), F32),
        ],
        compiler_params=params(),
        cost_estimate=cost(5 * n),
        name="block_forward",
    )(qT, *kvs)


def backward_tiles(blocks, va, kT, qk, gw, gk, p_ref, ds_ref, dqt, outs, pieces):
    rows_of = KEYS // BACK
    items = [(b, t, c) for b, first, n in blocks for t in range(first, first + n) for c in range(rows_of)]
    ends = {first + n - 1: (b, first, n) for b, first, n in blocks}
    grads, scores, dqs, fill = {}, {}, {}, []

    def sums(b, first, n, left, right, lanes, count):
        cols = slice(first * TW, (first + n) * TW)

        def piece(rows):
            outs[b][rows, lanes] = dot(left[rows, cols], right[:, cols], NT).astype(outs[b].dtype)

        step = KEYS // count
        return [functools.partial(piece, slice(i * step, (i + 1) * step)) for i in range(count)]

    def issue(n):
        if n < len(items):
            b, t, c = items[n]
            grads[n] = dot(va(b, slice(c * BACK, (c + 1) * BACK)), gw[t])

    for block in blocks:
        fill += sums(*block, p_ref, gk, slice(128, 256), pieces)
    issue(0)
    issue(1)
    for n, (b, t, c) in enumerate(items):
        issue(n + 2)
        r = slice(c * BACK, (c + 1) * BACK)
        ds = (p_ref[r, tile_cols(t)].astype(F32) * grads.pop(n)).astype(BF)
        ds_ref[r, tile_cols(t)] = ds
        if c == 0 and fill:
            fill.pop(0)()
        y = dot(kT(b, r), ds)
        dqs[t] = y if c == 0 else dqs[t] + y
        if c == rows_of - 1:
            dqt[t] = both_heads(dqs.pop(t))
            if t in ends:
                last = t == items[-1][1]
                fill += sums(*ends[t], ds_ref, qk, slice(0, 128), 1 if last else pieces)
    while fill:
        fill.pop(0)()


FAR_TILES = 7
FAR_BLOCKS = ((0, 0, 4), (1, 4, 2), (2, 6, 1))


def far_block(t):
    one = lambda at: (t >= at).astype(jnp.int32)
    return one(4) + one(6)


def group_kernel(
    chained, q_ref, ga_ref, kv1, kv2, kv3, wa_ref, sta_ref, wb_ref, stb_ref, *refs
):
    if chained:
        refs = refs[1:]
    (
        attn_ref, dq_ref, g_ref, gs_ref, o1, o2, o3,
        kk, va, kT, vT, qw, qk, gw, gk, p_ref, ds_ref, w_ref, st_ref, dqt, sa, sb, ma, mb,
    ) = refs
    kvs, outs = (kv1, kv2, kv3), (o1, o2, o3)
    for b in range(3):
        kv = kvs[b][...]
        kk[b] = score_keys(kv)
        va[b] = grad_values_operand(kv)
        kT[b] = kv[:, 0:128].T
        put_value_rows(vT.at[b], kv)
    level = [q_ref[:, j * SLAB : (j + 1) * SLAB] for j in range(8)]
    first = 0
    for _ in range(3):
        level = [
            (0.5 * (level[2 * c].astype(F32) + level[2 * c + 1].astype(F32))).astype(BF)
            for c in range(len(level) // 2)
        ]
        for c, x in enumerate(level):
            put_query(qw, first + c, x)
            put_scaled(qk, first + c, x)
        first += len(level)

    def put_p(r, t, p):
        p_ref[r, tile_cols(t)] = p

    def put_w(t, w):
        w_ref[t] = w

    def put_st(t, m, total):
        st_ref[t, 0:1] = m
        st_ref[t, 1:2] = total

    def score(t, s, m):
        b = far_block(t)
        return (lambda r: kk[b, r], lambda: qw[t], s, m)

    def value(t, s, m):
        b = far_block(t)
        return (lambda r: vT[b, :, r], put_p, t, s, m, put_w, put_st, t)

    forward_tiles(FAR_TILES, score, value, sa, sb, ma, mb)

    gl, gs = [None] * FAR_TILES, [None] * FAR_TILES
    for j in range(8):
        ts = [j // 2, 4 + j // 4, 6]
        ms = [sta_ref[j, 0:1], stb_ref[j, 0:1]] + [st_ref[t, 0:1] for t in ts]
        totals = [sta_ref[j, 1:2], stb_ref[j, 1:2]] + [st_ref[t, 1:2] for t in ts]
        ws = [wa_ref[j], wb_ref[j]] + [w_ref[t] for t in ts]
        top = functools.reduce(jnp.maximum, ms)
        factors = [jnp.exp2(m - top) * c for m, c in zip(ms, (1.0, 1.0, 2.0, 4.0, 8.0))]
        inv = 1.0 / functools.reduce(jnp.add, [f * x for f, x in zip(factors, totals)])
        shares = [f * inv for f in factors]
        at = functools.reduce(jnp.add, [s * w for s, w in zip(shares, ws)]).astype(BF)
        cols = slice(j * SLAB, (j + 1) * SLAB)
        attn_ref[0:64, cols] = at[:, 0:128]
        attn_ref[64:128, cols] = at[:, 128:256]
        ga = jnp.concatenate([ga_ref[0:64, cols], ga_ref[64:128, cols]], 1).astype(F32)
        delta = jnp.sum(ga * at.astype(F32), axis=0, keepdims=True)
        for side in range(2):
            g_ref[side, j] = (shares[side] * ga).astype(BF)
            gs_ref[side, j, 0:1] = shares[side] * delta
        for s, t in zip(shares[2:], ts):
            x, y = s * ga, s * delta
            gl[t] = x if gl[t] is None else gl[t] + x
            gs[t] = y if gs[t] is None else gs[t] + y
    for t in range(FAR_TILES):
        put_grad(gw, gk, t, gl[t].astype(BF), gs[t])

    backward_tiles(
        FAR_BLOCKS, lambda b, r: va[b, r], lambda b, r: kT[b, :, r],
        qk, gw, gk, p_ref, ds_ref, dqt, outs, 4,
    )
    for j in range(8):
        dq_ref[j] = 0.5 * dqt[j // 2] + 0.25 * dqt[4 + j // 4] + 0.125 * dqt[6]


def group(g, qT, gaT, kvs, own, far, attn):
    cols = pl.BlockSpec((128, KEYS), lambda i: (g, 0))
    tiles = lambda rows: pl.BlockSpec((2, 8, rows, TW), lambda i: (0, 0, 0, 0))
    at = lambda place, rows: pl.BlockSpec((None, 8, rows, TW), lambda i: (place, 0, 0, 0))
    chain = [] if attn is None else [attn]
    return pl.pallas_call(
        functools.partial(group_kernel, bool(chain)),
        grid=(1,),
        in_specs=[cols, cols]
        + [WHOLE] * 3
        + [at(own[2], 64), at(own[2], 8), at(far[2], 64), at(far[2], 8)]
        + [pl.BlockSpec(memory_space=pl.ANY) for _ in chain],
        out_specs=[cols, pl.BlockSpec((8, 64, TW), lambda i: (0, 0, 0)), tiles(64), tiles(8)]
        + [WHOLE] * 3,
        out_shape=[
            jax.ShapeDtypeStruct((512, KEYS), BF),
            jax.ShapeDtypeStruct((8, 64, TW), F32),
            jax.ShapeDtypeStruct((2, 8, 64, TW), BF),
            jax.ShapeDtypeStruct((2, 8, 8, TW), F32),
        ]
        + [jax.ShapeDtypeStruct((KEYS, 256), BF)] * 3,
        scratch_shapes=[
            pltpu.VMEM((3, KEYS, 256), BF),
            pltpu.VMEM((3, KEYS, 256), BF),
            pltpu.VMEM((3, 128, KEYS), BF),
            pltpu.VMEM((3, 144, KEYS), BF),
            pltpu.VMEM((FAR_TILES, 256, TW), BF),
            pltpu.VMEM((128, FAR_TILES * TW), BF),
            pltpu.VMEM((FAR_TILES, 256, TW), BF),
            pltpu.VMEM((128, FAR_TILES * TW), BF),
            pltpu.VMEM((KEYS, FAR_TILES * TW), BF),
            pltpu.VMEM((KEYS, FAR_TILES * TW), BF),
            pltpu.VMEM((FAR_TILES, 64, TW), F32),
            pltpu.VMEM((FAR_TILES, 8, TW), F32),
            pltpu.VMEM((FAR_TILES, 64, TW), F32),
            pltpu.VMEM((KEYS, TW), F32),
            pltpu.VMEM((KEYS, TW), F32),
            pltpu.VMEM((8, TW), F32),
            pltpu.VMEM((8, TW), F32),
        ],
        input_output_aliases={9: 0} if chain else {},
        compiler_params=params(),
        cost_estimate=cost(16),
        name="group",
    )(qT, gaT, *kvs, *own[:2], *far[:2], *chain)


def block_backward_kernel(n, last, chained, q_ref, p_ref, *refs):
    take = lambda: (refs[:n], refs[n:])
    kvs, refs = take()
    gls, refs = take()
    scales, refs = take()
    if last:
        upper, refs = take()
        other, refs = take()
    if chained:
        refs = refs[1:]
    dq_ref, o_ref, va, kT, qk, gw, gk, ds_ref, dqt, tmp = refs
    for i in range(n):

        @pl.when(pl.program_id(0) == i)
        def _(i=i):
            kv = kvs[i][...]
            va[...] = grad_values_operand(kv)
            kT[...] = kv[:, 0:128].T
            for j in range(8):
                put_grad(gw, gk, j, gls[i][j], scales[i][j, 0:1])

    for j in range(8):
        put_scaled(qk, j, q_ref[:, j * SLAB : (j + 1) * SLAB])

    backward_tiles(
        ((0, 0, 8),), lambda b, r: va[r], lambda b, r: kT[:, r],
        qk, gw, gk, p_ref, ds_ref, dqt, (o_ref,), 8,
    )
    if not last:
        dq_ref[...] = dqt[...]
        return
    for i in range(n):

        @pl.when(pl.program_id(0) == i)
        def _(i=i):
            for j in range(8):
                dqt[j] = dqt[j] + upper[i][j] + other[i][j]

    for j in range(8):
        d = 0.125 * dqt[j]
        tmp[pl.ds(j, SLAB, stride=8), :] = jnp.concatenate([d[:, 0:128], d[:, 128:256]], 0).T
    dq_ref[...] = tmp[...].astype(BF)


def block_backward(first, qT, p, kvs, gls, scales, side, upper=None, other=None, dq=None):
    n = len(kvs)
    last = upper is not None
    chain = [] if dq is None else [dq]
    of_side = lambda rows: pl.BlockSpec((None, 8, rows, TW), lambda i: (side, 0, 0, 0))
    at = lambda place: pl.BlockSpec((None, 8, 64, TW), lambda i: (place, 0, 0, 0))
    in_specs = [
        pl.BlockSpec((128, KEYS), lambda i: (first + i, 0)),
        pl.BlockSpec((None, KEYS, 8 * TW), lambda i: (i, 0, 0)),
    ]
    in_specs += [WHOLE] * n + [of_side(64)] * n + [of_side(8)] * n
    args = [qT, p, *kvs, *gls, *scales]
    if last:
        in_specs += [pl.BlockSpec((8, 64, TW), lambda i: (0, 0, 0))] * n
        in_specs += [at(place) for _, place in other]
        args += [*upper, *[part for part, _ in other]]
        dq_spec = pl.BlockSpec((KEYS, 128), lambda i: (0, first + i))
        dq_shape = jax.ShapeDtypeStruct((KEYS, 512), BF)
    else:
        dq_spec = pl.BlockSpec((None, 8, 64, TW), lambda i: (i, 0, 0, 0))
        dq_shape = jax.ShapeDtypeStruct((n, 8, 64, TW), F32)
    in_specs += [pl.BlockSpec(memory_space=pl.ANY) for _ in chain]
    return pl.pallas_call(
        functools.partial(block_backward_kernel, n, last, bool(chain)),
        grid=(n,),
        in_specs=in_specs,
        out_specs=[dq_spec, pl.BlockSpec((None, KEYS, 256), lambda i: (i, 0, 0))],
        out_shape=[dq_shape, jax.ShapeDtypeStruct((n, KEYS, 256), F32 if last else BF)],
        scratch_shapes=[
            pltpu.VMEM((KEYS, 256), BF),
            pltpu.VMEM((128, KEYS), BF),
            pltpu.VMEM((128, 8 * TW), BF),
            pltpu.VMEM((8, 256, TW), BF),
            pltpu.VMEM((128, 8 * TW), BF),
            pltpu.VMEM((KEYS, 8 * TW), BF),
            pltpu.VMEM((8, 64, TW), F32),
            pltpu.VMEM((KEYS, 128), F32),
        ],
        input_output_aliases={len(args): 0} if chain else {},
        compiler_params=params(),
        cost_estimate=cost(10 * n),
        name="block_backward",
    )(*args, *chain)


def keys_kernel(k_ref, v_ref, o0, o1, o2, o3, tmp):
    outs = (o0, o1, o2, o3)
    for part, src in enumerate((k_ref, v_ref)):
        for g in range(GROUPS):
            tmp[...] = src[:, g * 128 : (g + 1) * 128].astype(F32)
            for b in range(8):
                outs[g][b * SLAB : (b + 1) * SLAB, part * 128 : (part + 1) * 128] = tmp[
                    pl.ds(b, SLAB, stride=8), :
                ].astype(BF)


def prep_keys(k, v):
    return pl.pallas_call(
        keys_kernel,
        out_shape=[jax.ShapeDtypeStruct((KEYS, 256), BF)] * GROUPS,
        scratch_shapes=[pltpu.VMEM((KEYS, 128), F32)],
        compiler_params=params(),
        cost_estimate=cost(3),
        name="prep_keys",
    )(k, v)


def rows_kernel(q_ref, go_ref, w_ref, qT_ref, gaT_ref, gp_ref, tmp):
    for g in range(GROUPS):
        tmp[...] = q_ref[:, g * 128 : (g + 1) * 128].astype(F32)
        for b in range(8):
            x = tmp[pl.ds(b, SLAB, stride=8), :]
            qT_ref[g * 128 : (g + 1) * 128, b * SLAB : (b + 1) * SLAB] = x.T.astype(BF)
    for c in range(8):
        tmp[...] = go_ref[:, c * 128 : (c + 1) * 128].astype(F32)
        for b in range(8):
            gp_ref[b * SLAB : (b + 1) * SLAB, c * 128 : (c + 1) * 128] = tmp[
                pl.ds(b, SLAB, stride=8), :
            ].astype(BF)
    for c in range(4):
        rows = pl.ds(c * 256, 256)
        gaT_ref[:, c * 256 : (c + 1) * 256] = dot(w_ref[...], gp_ref[rows, :], NT).astype(BF)


def prep_rows(q, go, w):
    return pl.pallas_call(
        rows_kernel,
        out_shape=[
            jax.ShapeDtypeStruct((512, KEYS), BF),
            jax.ShapeDtypeStruct((512, KEYS), BF),
            jax.ShapeDtypeStruct((KEYS, 1024), BF),
        ],
        scratch_shapes=[pltpu.VMEM((KEYS, 128), F32)],
        compiler_params=params(),
        cost_estimate=cost(6),
        name="prep_rows",
    )(q, go, w)


def project_kernel(attn_ref, gp_ref, w_ref, out_ref, gw_ref, at, tmp):
    for g in range(GROUPS):
        rows = slice(g * 128, (g + 1) * 128)
        at[:, rows] = attn_ref[rows, :].T
        gw_ref[rows, :] = dot(attn_ref[rows, :], gp_ref[...])
    for c in range(8):
        for b in range(8):
            tmp[pl.ds(b, SLAB, stride=8), :] = dot(
                at[b * SLAB : (b + 1) * SLAB, :], w_ref[:, c * 128 : (c + 1) * 128]
            )
        out_ref[:, c * 128 : (c + 1) * 128] = tmp[...].astype(BF)


def project(attn, gp, w):
    return pl.pallas_call(
        project_kernel,
        out_shape=[
            jax.ShapeDtypeStruct((KEYS, 1024), BF),
            jax.ShapeDtypeStruct((512, 1024), F32),
        ],
        scratch_shapes=[pltpu.VMEM((KEYS, 512), BF), pltpu.VMEM((KEYS, 128), F32)],
        compiler_params=params(),
        cost_estimate=cost(7),
        name="project",
    )(attn, gp, w)


def finish_kernel(*refs):
    parts, (dk_ref, dv_ref, tmp) = refs[: 3 * GROUPS], refs[3 * GROUPS :]
    for g in range(GROUPS):
        own, kept, got = parts[3 * g : 3 * g + 3]
        for part, out in enumerate((dk_ref, dv_ref)):
            cols = slice(part * 128, (part + 1) * 128)
            for b in range(8):
                rows = slice(b * SLAB, (b + 1) * SLAB)
                half = slice(b // 2 * SLAB, (b // 2 + 1) * SLAB)
                tmp[pl.ds(b, SLAB, stride=8), :] = (
                    own[rows, cols] + 0.5 * kept[half, cols] + got[rows, cols].astype(F32)
                )
            out[:, g * 128 : (g + 1) * 128] = tmp[...].astype(BF)


def finish_keys(owns, kept, got):
    in_specs, args = [], []
    for (own, place), x, y in zip(owns, kept, got):
        in_specs.append(pl.BlockSpec((None, KEYS, 256), lambda i, place=place: (place, 0, 0)))
        in_specs += [pl.BlockSpec((512, 256), lambda i: (0, 0)), WHOLE]
        args += [own, x, y]
    return pl.pallas_call(
        finish_kernel,
        grid=(1,),
        in_specs=in_specs,
        out_specs=[pl.BlockSpec((KEYS, 512), lambda i: (0, 0))] * 2,
        out_shape=[jax.ShapeDtypeStruct((KEYS, 512), BF)] * 2,
        scratch_shapes=[pltpu.VMEM((KEYS, 128), F32)],
        compiler_params=params(),
        cost_estimate=cost(5),
        name="finish_keys",
    )(*args)


def partner(value, level):
    mask = MASKS[level]
    pairs = [(source, source ^ mask) for source in range(lax.axis_size("ctx"))]
    return lax.ppermute(value, "ctx", pairs)


def pool(x):
    y = x.astype(F32).reshape(4, 2, SLAB, 256)
    return (0.5 * (y[:, 0] + y[:, 1])).astype(BF).reshape(512, 256)


def spread(x):
    n = x.shape[0] // SLAB
    y = jnp.broadcast_to((0.5 * x).reshape(n, 1, SLAB, 256), (n, 2, SLAB, 256))
    return y.reshape(2 * x.shape[0], 256)


def after(values, done):
    out = lax.optimization_barrier((*values, *done))
    return list(out[: len(values)])


def on_device(queries, key_states, value_states, grad_out, out_weight):
    held = [[x] for x in prep_keys(key_states[0], value_states[0])]
    far = [[] for _ in held]

    def send(g):
        far[g].append(partner(held[g][-1], len(far[g])))

    def pool_and_send(which, done):
        for g, x in zip(which, after([far[g][-1] for g in which], done)):
            far[g][-1] = x
            held[g].append(jnp.concatenate([pool(held[g][-1]), pool(x)], 0))
        made = [held[g][-1] for g in which]
        for g in which:
            send(g)
        return made

    own = [h[0] for h in held]
    for g in range(GROUPS):
        send(g)
    qT, gaT, gp = prep_rows(queries[0], grad_out[0], out_weight)

    p_own0, w_own0, st_own0 = block_forward(0, qT, own[:1])
    made = pool_and_send([0], [st_own0])
    (qT,) = after([qT], made)
    p_own1, w_own1, st_own1 = block_forward(1, qT, own[1:])
    made = pool_and_send([0, 1], [st_own1])
    (qT,) = after([qT], made)
    p_far0, w_far0, st_far0 = block_forward(0, qT, [far[0][0], far[1][0]])
    made = pool_and_send([0, 1, 2], [st_far0])
    (qT,) = after([qT], made)
    p_far2, w_far2, st_far2 = block_forward(2, qT, [far[2][0]])
    made = pool_and_send([1, 2, 3], [st_far2])
    (qT,) = after([qT], made)

    owns = [(w_own0, st_own0, 0)] + [(w_own1, st_own1, i) for i in range(3)]
    fars = [(w_far0, st_far0, 0), (w_far0, st_far0, 1), (w_far2, st_far2, 0)]
    attn = None
    dqs, gls, scales, grads, pending, sent = [], [], [], [], [], []

    def level_3_to_1(g):
        nonlocal attn
        attn, dq, gl, gs, f1, f2, f3 = group(g, qT, gaT, far[g][1:], owns[g], fars[g], attn)
        dqs.append(dq)
        gls.append(gl)
        scales.append(gs)
        grads.append([None, f1, f2, f3])
        sent.append(partner(f3, 3))
        pending.append(None)

    def pass_on(steps, done):
        made = []
        for (g, level), x in zip(steps, after([sent[g] for g, _ in steps], done)):
            x = x.astype(F32)
            low, high = x[:512], x[512:]
            if pending[g] is not None:
                low = spread(pending[g][:256]) + low
                high = spread(pending[g][256:]) + high
            pending[g] = low
            outgoing = (grads[g][level].astype(F32) + spread(high)).astype(BF)
            made.append(outgoing)
            sent[g] = partner(outgoing, level)
        return made

    level_3_to_1(0)
    made = pool_and_send([2, 3], [dqs[0]])
    (qT,) = after([qT], made)
    p_far3, w_far3, st_far3 = block_forward(3, qT, [far[3][0]])
    fars.append((w_far3, st_far3, 0))
    (qT,) = after([qT], [st_far3])
    level_3_to_1(1)
    made = pool_and_send([3], [dqs[1]]) + pass_on([(0, 2)], [dqs[1]])
    (qT,) = after([qT], made)
    level_3_to_1(2)
    made = pass_on([(0, 1), (1, 2)], [dqs[2]])
    (qT,) = after([qT], made)
    level_3_to_1(3)
    made = pass_on([(1, 1), (2, 2)], [dqs[3]])
    (attn,) = after([attn], made)
    outputs, weight_part = project(attn, gp, out_weight)
    (qT,) = after([qT], [outputs])

    def far_backward(first, p, n):
        which = range(first, first + n)
        dq, o = block_backward(
            first, qT, p, [far[g][0] for g in which], [gls[g] for g in which],
            [scales[g] for g in which], 1,
        )
        for i, g in enumerate(which):
            grads[g][0] = o[i]
        return dq

    dq_far0 = far_backward(0, p_far0, 2)
    made = pass_on([(0, 0), (1, 0), (2, 1), (3, 2)], [dq_far0])
    (qT,) = after([qT], made)
    dq_far2 = far_backward(2, p_far2, 1)
    made = pass_on([(2, 0), (3, 1)], [dq_far2])
    (qT,) = after([qT], made)
    dq_far3 = far_backward(3, p_far3, 1)
    weight_cols = lax.psum_scatter(weight_part, "rep", scatter_dimension=1, tiled=True)
    (qT,) = after([qT], [dq_far3, weight_cols])
    other = [(dq_far0, 0), (dq_far0, 1), (dq_far2, 0), (dq_far3, 0)]
    dq, o_own0 = block_backward(
        0, qT, p_own0, own[:1], gls[:1], scales[:1], 0, dqs[:1], other[:1]
    )
    made = pass_on([(3, 0)], [o_own0])
    (qT,) = after([qT], made)
    dq, o_own1 = block_backward(
        1, qT, p_own1, own[1:], gls[1:], scales[1:], 0, dqs[1:], other[1:], dq
    )
    grad_weight = lax.psum_scatter(weight_cols, "ctx", scatter_dimension=0, tiled=True)
    got = after(sent, [o_own1, grad_weight])
    grad_keys, grad_values = finish_keys(
        [(o_own0, 0)] + [(o_own1, i) for i in range(3)], pending, got
    )
    return outputs[None], dq[None], grad_keys[None], grad_values[None], grad_weight


def solution(mesh):
    rows = P("rep", "ctx", None)
    return jax.shard_map(
        on_device,
        mesh=mesh,
        in_specs=(rows, rows, rows, rows, P()),
        out_specs=(rows, rows, rows, rows, P("ctx", "rep")),
        check_vma=False,
    )
```

```python
import functools

import jax
import jax.numpy as jnp
from jax import lax
from jax.experimental import pallas as pl
from jax.experimental.pallas import tpu as pltpu
from jax.sharding import PartitionSpec as P

F32 = jnp.float32
BF = jnp.bfloat16
KEYS = 1024
SLAB = 128
TW = 256
GROUPS = 4
MASKS = (1, 3, 4, 12)
NT = (((1,), (1,)), ((), ()))
NN = (((1,), (0,)), ((), ()))
LOG2E = 1.4426950408889634
CHUNK = 512
BACK = 256


def dot(a, b, dims=NN):
    return lax.dot_general(a, b, dims, preferred_element_type=F32)


def cost(us):
    return pl.CostEstimate(flops=int(us * 1.15e9), bytes_accessed=2**20, transcendentals=0)


def params(mib=58):
    return pltpu.CompilerParams(vmem_limit_bytes=mib * 2**20)


def score_keys(kv):
    k0, k1 = kv[:, 0:64], kv[:, 64:128]
    return jnp.concatenate([k0, k0, k1, k1], 1)


def grad_values_operand(kv):
    ones3 = (lax.broadcasted_iota(jnp.int32, (KEYS, 64), 1) < 3).astype(F32).astype(BF)
    return jnp.concatenate([kv[:, 128:192], ones3, kv[:, 192:256], ones3], 1)


def put_value_rows(ref, kv):
    ref[0:128] = kv[:, 128:256].T
    ref[128:144] = (lax.broadcasted_iota(jnp.int32, (16, KEYS), 0) == 0).astype(F32).astype(BF)


def put_query(qw, t, q):
    zero = jnp.zeros((128, SLAB), BF)
    qs = q.astype(F32) * (0.125 * LOG2E)
    hi = qs.astype(BF)
    lo = (qs - hi.astype(F32)).astype(BF)
    qw[t, 0:64, 0:128] = hi[0:64]
    qw[t, 64:128, 0:128] = lo[0:64]
    qw[t, 128:256, 0:128] = zero
    qw[t, 0:128, 128:256] = zero
    qw[t, 128:192, 128:256] = hi[64:128]
    qw[t, 192:256, 128:256] = lo[64:128]


def put_pair(ref, t, first, second):
    zero = jnp.zeros((64, SLAB), BF)
    off = t * TW
    ref[0:64, off : off + 128] = first
    ref[64:128, off : off + 128] = zero
    ref[0:64, off + 128 : off + 256] = zero
    ref[64:128, off + 128 : off + 256] = second


def put_scaled(qk, t, q):
    qq = (q.astype(F32) * 0.125).astype(BF)
    put_pair(qk, t, qq[0:64], qq[64:128])


def put_grad(gw, gk, t, g, scale):
    n = -scale
    hi = n.astype(BF).astype(F32)
    rest = n - hi
    mid = rest.astype(BF).astype(F32)
    row = lax.broadcasted_iota(jnp.int32, (64, TW), 0)
    low = jnp.where(row == 0, hi, jnp.where(row == 1, mid, jnp.where(row == 2, rest - mid, 0.0)))
    low = low.astype(BF)
    zero = jnp.zeros((128, SLAB), BF)
    gw[t, 0:64, 0:128] = g[:, 0:128]
    gw[t, 64:128, 0:128] = low[:, 0:128]
    gw[t, 128:256, 0:128] = zero
    gw[t, 0:128, 128:256] = zero
    gw[t, 128:192, 128:256] = g[:, 128:256]
    gw[t, 192:256, 128:256] = low[:, 128:256]
    put_pair(gk, t, g[:, 0:128], g[:, 128:256])


def both_heads(x):
    return jnp.concatenate([x[0:64, 0:128], x[64:128, 128:256]], 1)


def forward_step(nxt, cur):
    if nxt is not None:
        keys, query, sn, mn = nxt
        top = None
    if cur is not None:
        values, p_ref, off, sc, mc, w_ref, st_ref, t = cur
        m = mc[0:1]
        w = None
    for c in range(KEYS // CHUNK):
        r = slice(c * CHUNK, (c + 1) * CHUNK)
        if nxt is not None:
            s = dot(keys(r), query())
            sn[r] = s
            x = jnp.max(s.reshape(CHUNK // 8, 8, TW), axis=0)
            top = x if top is None else jnp.maximum(top, x)
        if cur is not None:
            p = jnp.exp2(sc[r] - m).astype(BF)
            p_ref(r, off, p)
            y = dot(values(r), p)
            w = y if w is None else w + y
    if nxt is not None:
        mn[0:1] = jnp.max(top, axis=0, keepdims=True)
    if cur is not None:
        w_ref(t, both_heads(w))
        st_ref(t, m, w[128:129])


def forward_tiles(count, score, value, sa, sb, ma, mb):
    forward_step(score(jnp.int32(0), sa, ma), None)

    def body(i, c):
        t = 2 * i
        forward_step(score(t + 1, sb, mb), value(t, sa, ma))
        forward_step(score(t + 2, sa, ma), value(t + 1, sb, mb))
        return c

    steps = (count - 1) // 2
    lax.fori_loop(0, steps, body, 0)
    t = jnp.int32(2 * steps)
    if count % 2 == 0:
        forward_step(score(t + 1, sb, mb), value(t, sa, ma))
        forward_step(None, value(t + 1, sb, mb))
    else:
        forward_step(None, value(t, sa, ma))


def tile_cols(t):
    if isinstance(t, int):
        return slice(t * TW, (t + 1) * TW)
    return pl.ds(pl.multiple_of(t * TW, TW), TW)


def select(refs, use):
    for i, ref in enumerate(refs):
        pl.when(pl.program_id(0) == i)(functools.partial(use, ref))


def block_forward_kernel(n, q_ref, *refs):
    kvs, (p_ref, w_ref, st_ref, kk, vT, qw, sa, sb, ma, mb) = refs[:n], refs[n:]

    def prepare(kv_ref):
        kv = kv_ref[...]
        kk[...] = score_keys(kv)
        put_value_rows(vT, kv)

    select(kvs, prepare)
    for j in range(8):
        put_query(qw, j, q_ref[:, j * SLAB : (j + 1) * SLAB])

    def put_p(r, t, p):
        p_ref[r, tile_cols(t)] = p

    def put_w(t, w):
        w_ref[t] = w

    def put_st(t, m, total):
        st_ref[t, 0:1] = m
        st_ref[t, 1:2] = total

    def score(t, s, m):
        return (lambda r: kk[r], lambda: qw[t], s, m)

    def value(t, s, m):
        return (lambda r: vT[:, r], put_p, t, s, m, put_w, put_st, t)

    forward_tiles(8, score, value, sa, sb, ma, mb)


WHOLE = pl.BlockSpec((KEYS, 256), lambda i: (0, 0))


def block_forward(first, qT, kvs):
    n = len(kvs)
    return pl.pallas_call(
        functools.partial(block_forward_kernel, n),
        grid=(n,),
        in_specs=[pl.BlockSpec((128, KEYS), lambda i: (first + i, 0))] + [WHOLE] * n,
        out_specs=[
            pl.BlockSpec((None, KEYS, 8 * TW), lambda i: (i, 0, 0)),
            pl.BlockSpec((None, 8, 64, TW), lambda i: (i, 0, 0, 0)),
            pl.BlockSpec((None, 8, 8, TW), lambda i: (i, 0, 0, 0)),
        ],
        out_shape=[
            jax.ShapeDtypeStruct((n, KEYS, 8 * TW), BF),
            jax.ShapeDtypeStruct((n, 8, 64, TW), F32),
            jax.ShapeDtypeStruct((n, 8, 8, TW), F32),
        ],
        scratch_shapes=[
            pltpu.VMEM((KEYS, 256), BF),
            pltpu.VMEM((144, KEYS), BF),
            pltpu.VMEM((8, 256, TW), BF),
            pltpu.VMEM((KEYS, TW), F32),
            pltpu.VMEM((KEYS, TW), F32),
            pltpu.VMEM((8, TW), F32),
            pltpu.VMEM((8, TW), F32),
        ],
        compiler_params=params(),
        cost_estimate=cost(5 * n),
        name="block_forward",
    )(qT, *kvs)


def backward_tiles(blocks, va, kT, qk, gw, gk, p_ref, ds_ref, dqt, outs, pieces):
    rows_of = KEYS // BACK
    items = [(b, t, c) for b, first, n in blocks for t in range(first, first + n) for c in range(rows_of)]
    ends = {first + n - 1: (b, first, n) for b, first, n in blocks}
    grads, scores, dqs, fill = {}, {}, {}, []

    def sums(b, first, n, left, right, lanes, count):
        cols = slice(first * TW, (first + n) * TW)

        def piece(rows):
            outs[b][rows, lanes] = dot(left[rows, cols], right[:, cols], NT).astype(outs[b].dtype)

        step = KEYS // count
        return [functools.partial(piece, slice(i * step, (i + 1) * step)) for i in range(count)]

    def issue(n):
        if n < len(items):
            b, t, c = items[n]
            grads[n] = dot(va(b, slice(c * BACK, (c + 1) * BACK)), gw[t])

    for block in blocks:
        fill += sums(*block, p_ref, gk, slice(128, 256), pieces)
    issue(0)
    issue(1)
    for n, (b, t, c) in enumerate(items):
        issue(n + 2)
        r = slice(c * BACK, (c + 1) * BACK)
        ds = (p_ref[r, tile_cols(t)].astype(F32) * grads.pop(n)).astype(BF)
        ds_ref[r, tile_cols(t)] = ds
        if c == 0 and fill:
            fill.pop(0)()
        y = dot(kT(b, r), ds)
        dqs[t] = y if c == 0 else dqs[t] + y
        if c == rows_of - 1:
            dqt[t] = both_heads(dqs.pop(t))
            if t in ends:
                last = t == items[-1][1]
                fill += sums(*ends[t], ds_ref, qk, slice(0, 128), 1 if last else pieces)
    while fill:
        fill.pop(0)()


FAR_TILES = 7
FAR_BLOCKS = ((0, 0, 4), (1, 4, 2), (2, 6, 1))


def far_block(t):
    one = lambda at: (t >= at).astype(jnp.int32)
    return one(4) + one(6)


def group_kernel(
    chained, q_ref, ga_ref, kv1, kv2, kv3, wa_ref, sta_ref, wb_ref, stb_ref, *refs
):
    if chained:
        refs = refs[1:]
    (
        attn_ref, dq_ref, g_ref, gs_ref, o1, o2, o3,
        kk, va, kT, vT, qw, qk, gw, gk, p_ref, ds_ref, w_ref, st_ref, dqt, sa, sb, ma, mb,
    ) = refs
    kvs, outs = (kv1, kv2, kv3), (o1, o2, o3)
    for b in range(3):
        kv = kvs[b][...]
        kk[b] = score_keys(kv)
        va[b] = grad_values_operand(kv)
        kT[b] = kv[:, 0:128].T
        put_value_rows(vT.at[b], kv)
    level = [q_ref[:, j * SLAB : (j + 1) * SLAB] for j in range(8)]
    first = 0
    for _ in range(3):
        level = [
            (0.5 * (level[2 * c].astype(F32) + level[2 * c + 1].astype(F32))).astype(BF)
            for c in range(len(level) // 2)
        ]
        for c, x in enumerate(level):
            put_query(qw, first + c, x)
            put_scaled(qk, first + c, x)
        first += len(level)

    def put_p(r, t, p):
        p_ref[r, tile_cols(t)] = p

    def put_w(t, w):
        w_ref[t] = w

    def put_st(t, m, total):
        st_ref[t, 0:1] = m
        st_ref[t, 1:2] = total

    def score(t, s, m):
        b = far_block(t)
        return (lambda r: kk[b, r], lambda: qw[t], s, m)

    def value(t, s, m):
        b = far_block(t)
        return (lambda r: vT[b, :, r], put_p, t, s, m, put_w, put_st, t)

    forward_tiles(FAR_TILES, score, value, sa, sb, ma, mb)

    gl, gs = [None] * FAR_TILES, [None] * FAR_TILES
    for j in range(8):
        ts = [j // 2, 4 + j // 4, 6]
        ms = [sta_ref[j, 0:1], stb_ref[j, 0:1]] + [st_ref[t, 0:1] for t in ts]
        totals = [sta_ref[j, 1:2], stb_ref[j, 1:2]] + [st_ref[t, 1:2] for t in ts]
        ws = [wa_ref[j], wb_ref[j]] + [w_ref[t] for t in ts]
        top = functools.reduce(jnp.maximum, ms)
        factors = [jnp.exp2(m - top) * c for m, c in zip(ms, (1.0, 1.0, 2.0, 4.0, 8.0))]
        inv = 1.0 / functools.reduce(jnp.add, [f * x for f, x in zip(factors, totals)])
        shares = [f * inv for f in factors]
        at = functools.reduce(jnp.add, [s * w for s, w in zip(shares, ws)]).astype(BF)
        cols = slice(j * SLAB, (j + 1) * SLAB)
        attn_ref[0:64, cols] = at[:, 0:128]
        attn_ref[64:128, cols] = at[:, 128:256]
        ga = jnp.concatenate([ga_ref[0:64, cols], ga_ref[64:128, cols]], 1).astype(F32)
        delta = jnp.sum(ga * at.astype(F32), axis=0, keepdims=True)
        for side in range(2):
            g_ref[side, j] = (shares[side] * ga).astype(BF)
            gs_ref[side, j, 0:1] = shares[side] * delta
        for s, t in zip(shares[2:], ts):
            x, y = s * ga, s * delta
            gl[t] = x if gl[t] is None else gl[t] + x
            gs[t] = y if gs[t] is None else gs[t] + y
    for t in range(FAR_TILES):
        put_grad(gw, gk, t, gl[t].astype(BF), gs[t])

    backward_tiles(
        FAR_BLOCKS, lambda b, r: va[b, r], lambda b, r: kT[b, :, r],
        qk, gw, gk, p_ref, ds_ref, dqt, outs, 4,
    )
    for j in range(8):
        dq_ref[j] = 0.5 * dqt[j // 2] + 0.25 * dqt[4 + j // 4] + 0.125 * dqt[6]


def group(g, qT, gaT, kvs, own, far, attn):
    cols = pl.BlockSpec((128, KEYS), lambda i: (g, 0))
    tiles = lambda rows: pl.BlockSpec((2, 8, rows, TW), lambda i: (0, 0, 0, 0))
    at = lambda place, rows: pl.BlockSpec((None, 8, rows, TW), lambda i: (place, 0, 0, 0))
    chain = [] if attn is None else [attn]
    return pl.pallas_call(
        functools.partial(group_kernel, bool(chain)),
        grid=(1,),
        in_specs=[cols, cols]
        + [WHOLE] * 3
        + [at(own[2], 64), at(own[2], 8), at(far[2], 64), at(far[2], 8)]
        + [pl.BlockSpec(memory_space=pl.ANY) for _ in chain],
        out_specs=[cols, pl.BlockSpec((8, 64, TW), lambda i: (0, 0, 0)), tiles(64), tiles(8)]
        + [WHOLE] * 3,
        out_shape=[
            jax.ShapeDtypeStruct((512, KEYS), BF),
            jax.ShapeDtypeStruct((8, 64, TW), F32),
            jax.ShapeDtypeStruct((2, 8, 64, TW), BF),
            jax.ShapeDtypeStruct((2, 8, 8, TW), F32),
        ]
        + [jax.ShapeDtypeStruct((KEYS, 256), BF)] * 3,
        scratch_shapes=[
            pltpu.VMEM((3, KEYS, 256), BF),
            pltpu.VMEM((3, KEYS, 256), BF),
            pltpu.VMEM((3, 128, KEYS), BF),
            pltpu.VMEM((3, 144, KEYS), BF),
            pltpu.VMEM((FAR_TILES, 256, TW), BF),
            pltpu.VMEM((128, FAR_TILES * TW), BF),
            pltpu.VMEM((FAR_TILES, 256, TW), BF),
            pltpu.VMEM((128, FAR_TILES * TW), BF),
            pltpu.VMEM((KEYS, FAR_TILES * TW), BF),
            pltpu.VMEM((KEYS, FAR_TILES * TW), BF),
            pltpu.VMEM((FAR_TILES, 64, TW), F32),
            pltpu.VMEM((FAR_TILES, 8, TW), F32),
            pltpu.VMEM((FAR_TILES, 64, TW), F32),
            pltpu.VMEM((KEYS, TW), F32),
            pltpu.VMEM((KEYS, TW), F32),
            pltpu.VMEM((8, TW), F32),
            pltpu.VMEM((8, TW), F32),
        ],
        input_output_aliases={9: 0} if chain else {},
        compiler_params=params(),
        cost_estimate=cost(16),
        name="group",
    )(qT, gaT, *kvs, *own[:2], *far[:2], *chain)


def block_backward_kernel(n, last, chained, q_ref, p_ref, *refs):
    take = lambda: (refs[:n], refs[n:])
    kvs, refs = take()
    gls, refs = take()
    scales, refs = take()
    if last:
        upper, refs = take()
        other, refs = take()
    if chained:
        refs = refs[1:]
    dq_ref, o_ref, va, kT, qk, gw, gk, ds_ref, dqt, tmp = refs
    for i in range(n):

        @pl.when(pl.program_id(0) == i)
        def _(i=i):
            kv = kvs[i][...]
            va[...] = grad_values_operand(kv)
            kT[...] = kv[:, 0:128].T
            for j in range(8):
                put_grad(gw, gk, j, gls[i][j], scales[i][j, 0:1])

    for j in range(8):
        put_scaled(qk, j, q_ref[:, j * SLAB : (j + 1) * SLAB])

    backward_tiles(
        ((0, 0, 8),), lambda b, r: va[r], lambda b, r: kT[:, r],
        qk, gw, gk, p_ref, ds_ref, dqt, (o_ref,), 8,
    )
    if not last:
        dq_ref[...] = dqt[...]
        return
    for i in range(n):

        @pl.when(pl.program_id(0) == i)
        def _(i=i):
            for j in range(8):
                dqt[j] = dqt[j] + upper[i][j] + other[i][j]

    for j in range(8):
        d = 0.125 * dqt[j]
        tmp[pl.ds(j, SLAB, stride=8), :] = jnp.concatenate([d[:, 0:128], d[:, 128:256]], 0).T
    dq_ref[...] = tmp[...].astype(BF)


def block_backward(first, qT, p, kvs, gls, scales, side, upper=None, other=None, dq=None):
    n = len(kvs)
    last = upper is not None
    chain = [] if dq is None else [dq]
    of_side = lambda rows: pl.BlockSpec((None, 8, rows, TW), lambda i: (side, 0, 0, 0))
    at = lambda place: pl.BlockSpec((None, 8, 64, TW), lambda i: (place, 0, 0, 0))
    in_specs = [
        pl.BlockSpec((128, KEYS), lambda i: (first + i, 0)),
        pl.BlockSpec((None, KEYS, 8 * TW), lambda i: (i, 0, 0)),
    ]
    in_specs += [WHOLE] * n + [of_side(64)] * n + [of_side(8)] * n
    args = [qT, p, *kvs, *gls, *scales]
    if last:
        in_specs += [pl.BlockSpec((8, 64, TW), lambda i: (0, 0, 0))] * n
        in_specs += [at(place) for _, place in other]
        args += [*upper, *[part for part, _ in other]]
        dq_spec = pl.BlockSpec((KEYS, 128), lambda i: (0, first + i))
        dq_shape = jax.ShapeDtypeStruct((KEYS, 512), BF)
    else:
        dq_spec = pl.BlockSpec((None, 8, 64, TW), lambda i: (i, 0, 0, 0))
        dq_shape = jax.ShapeDtypeStruct((n, 8, 64, TW), F32)
    in_specs += [pl.BlockSpec(memory_space=pl.ANY) for _ in chain]
    return pl.pallas_call(
        functools.partial(block_backward_kernel, n, last, bool(chain)),
        grid=(n,),
        in_specs=in_specs,
        out_specs=[dq_spec, pl.BlockSpec((None, KEYS, 256), lambda i: (i, 0, 0))],
        out_shape=[dq_shape, jax.ShapeDtypeStruct((n, KEYS, 256), F32 if last else BF)],
        scratch_shapes=[
            pltpu.VMEM((KEYS, 256), BF),
            pltpu.VMEM((128, KEYS), BF),
            pltpu.VMEM((128, 8 * TW), BF),
            pltpu.VMEM((8, 256, TW), BF),
            pltpu.VMEM((128, 8 * TW), BF),
            pltpu.VMEM((KEYS, 8 * TW), BF),
            pltpu.VMEM((8, 64, TW), F32),
            pltpu.VMEM((KEYS, 128), F32),
        ],
        input_output_aliases={len(args): 0} if chain else {},
        compiler_params=params(),
        cost_estimate=cost(10 * n),
        name="block_backward",
    )(*args, *chain)


def keys_kernel(k_ref, v_ref, o0, o1, o2, o3, tmp):
    outs = (o0, o1, o2, o3)
    for part, src in enumerate((k_ref, v_ref)):
        for g in range(GROUPS):
            tmp[...] = src[:, g * 128 : (g + 1) * 128].astype(F32)
            for b in range(8):
                outs[g][b * SLAB : (b + 1) * SLAB, part * 128 : (part + 1) * 128] = tmp[
                    pl.ds(b, SLAB, stride=8), :
                ].astype(BF)


def prep_keys(k, v):
    return pl.pallas_call(
        keys_kernel,
        out_shape=[jax.ShapeDtypeStruct((KEYS, 256), BF)] * GROUPS,
        scratch_shapes=[pltpu.VMEM((KEYS, 128), F32)],
        compiler_params=params(),
        cost_estimate=cost(3),
        name="prep_keys",
    )(k, v)


def rows_kernel(q_ref, go_ref, w_ref, qT_ref, gaT_ref, gp_ref, tmp):
    for g in range(GROUPS):
        tmp[...] = q_ref[:, g * 128 : (g + 1) * 128].astype(F32)
        for b in range(8):
            x = tmp[pl.ds(b, SLAB, stride=8), :]
            qT_ref[g * 128 : (g + 1) * 128, b * SLAB : (b + 1) * SLAB] = x.T.astype(BF)
    for c in range(8):
        tmp[...] = go_ref[:, c * 128 : (c + 1) * 128].astype(F32)
        for b in range(8):
            gp_ref[b * SLAB : (b + 1) * SLAB, c * 128 : (c + 1) * 128] = tmp[
                pl.ds(b, SLAB, stride=8), :
            ].astype(BF)
    for c in range(4):
        rows = pl.ds(c * 256, 256)
        gaT_ref[:, c * 256 : (c + 1) * 256] = dot(w_ref[...], gp_ref[rows, :], NT).astype(BF)


def prep_rows(q, go, w):
    return pl.pallas_call(
        rows_kernel,
        out_shape=[
            jax.ShapeDtypeStruct((512, KEYS), BF),
            jax.ShapeDtypeStruct((512, KEYS), BF),
            jax.ShapeDtypeStruct((KEYS, 1024), BF),
        ],
        scratch_shapes=[pltpu.VMEM((KEYS, 128), F32)],
        compiler_params=params(),
        cost_estimate=cost(6),
        name="prep_rows",
    )(q, go, w)


def project_kernel(attn_ref, gp_ref, w_ref, out_ref, gw_ref, at, tmp):
    for g in range(GROUPS):
        rows = slice(g * 128, (g + 1) * 128)
        at[:, rows] = attn_ref[rows, :].T
        gw_ref[rows, :] = dot(attn_ref[rows, :], gp_ref[...])
    for c in range(8):
        for b in range(8):
            tmp[pl.ds(b, SLAB, stride=8), :] = dot(
                at[b * SLAB : (b + 1) * SLAB, :], w_ref[:, c * 128 : (c + 1) * 128]
            )
        out_ref[:, c * 128 : (c + 1) * 128] = tmp[...].astype(BF)


def project(attn, gp, w):
    return pl.pallas_call(
        project_kernel,
        out_shape=[
            jax.ShapeDtypeStruct((KEYS, 1024), BF),
            jax.ShapeDtypeStruct((512, 1024), F32),
        ],
        scratch_shapes=[pltpu.VMEM((KEYS, 512), BF), pltpu.VMEM((KEYS, 128), F32)],
        compiler_params=params(),
        cost_estimate=cost(7),
        name="project",
    )(attn, gp, w)


def finish_kernel(*refs):
    parts, (dk_ref, dv_ref, tmp) = refs[: 3 * GROUPS], refs[3 * GROUPS :]
    for g in range(GROUPS):
        own, kept, got = parts[3 * g : 3 * g + 3]
        for part, out in enumerate((dk_ref, dv_ref)):
            cols = slice(part * 128, (part + 1) * 128)
            for b in range(8):
                rows = slice(b * SLAB, (b + 1) * SLAB)
                half = slice(b // 2 * SLAB, (b // 2 + 1) * SLAB)
                tmp[pl.ds(b, SLAB, stride=8), :] = (
                    own[rows, cols] + 0.5 * kept[half, cols] + got[rows, cols].astype(F32)
                )
            out[:, g * 128 : (g + 1) * 128] = tmp[...].astype(BF)


def finish_keys(owns, kept, got):
    in_specs, args = [], []
    for (own, place), x, y in zip(owns, kept, got):
        in_specs.append(pl.BlockSpec((None, KEYS, 256), lambda i, place=place: (place, 0, 0)))
        in_specs += [pl.BlockSpec((512, 256), lambda i: (0, 0)), WHOLE]
        args += [own, x, y]
    return pl.pallas_call(
        finish_kernel,
        grid=(1,),
        in_specs=in_specs,
        out_specs=[pl.BlockSpec((KEYS, 512), lambda i: (0, 0))] * 2,
        out_shape=[jax.ShapeDtypeStruct((KEYS, 512), BF)] * 2,
        scratch_shapes=[pltpu.VMEM((KEYS, 128), F32)],
        compiler_params=params(),
        cost_estimate=cost(5),
        name="finish_keys",
    )(*args)


def partner(value, level):
    mask = MASKS[level]
    pairs = [(source, source ^ mask) for source in range(lax.axis_size("ctx"))]
    return lax.ppermute(value, "ctx", pairs)


def pool(x):
    y = x.astype(F32).reshape(4, 2, SLAB, 256)
    return (0.5 * (y[:, 0] + y[:, 1])).astype(BF).reshape(512, 256)


def spread(x):
    n = x.shape[0] // SLAB
    y = jnp.broadcast_to((0.5 * x).reshape(n, 1, SLAB, 256), (n, 2, SLAB, 256))
    return y.reshape(2 * x.shape[0], 256)


def after(values, done):
    out = lax.optimization_barrier((*values, *done))
    return list(out[: len(values)])


def on_device(queries, key_states, value_states, grad_out, out_weight):
    held = [[x] for x in prep_keys(key_states[0], value_states[0])]
    far = [[] for _ in held]

    def send(g):
        far[g].append(partner(held[g][-1], len(far[g])))

    def pool_and_send(which, done):
        for g, x in zip(which, after([far[g][-1] for g in which], done)):
            far[g][-1] = x
            held[g].append(jnp.concatenate([pool(held[g][-1]), pool(x)], 0))
        made = [held[g][-1] for g in which]
        for g in which:
            send(g)
        return made

    own = [h[0] for h in held]
    for g in range(GROUPS):
        send(g)
    qT, gaT, gp = prep_rows(queries[0], grad_out[0], out_weight)

    p_own0, w_own0, st_own0 = block_forward(0, qT, own[:1])
    made = pool_and_send([0], [st_own0])
    (qT,) = after([qT], made)
    p_own1, w_own1, st_own1 = block_forward(1, qT, own[1:])
    made = pool_and_send([0, 1], [st_own1])
    (qT,) = after([qT], made)
    p_far0, w_far0, st_far0 = block_forward(0, qT, [far[0][0], far[1][0]])
    made = pool_and_send([0, 1, 2], [st_far0])
    (qT,) = after([qT], made)
    p_far2, w_far2, st_far2 = block_forward(2, qT, [far[2][0]])
    made = pool_and_send([1, 2, 3], [st_far2])
    (qT,) = after([qT], made)

    owns = [(w_own0, st_own0, 0)] + [(w_own1, st_own1, i) for i in range(3)]
    fars = [(w_far0, st_far0, 0), (w_far0, st_far0, 1), (w_far2, st_far2, 0)]
    attn = None
    dqs, gls, scales, grads, pending, sent = [], [], [], [], [], []

    def level_3_to_1(g):
        nonlocal attn
        attn, dq, gl, gs, f1, f2, f3 = group(g, qT, gaT, far[g][1:], owns[g], fars[g], attn)
        dqs.append(dq)
        gls.append(gl)
        scales.append(gs)
        grads.append([None, f1, f2, f3])
        sent.append(partner(f3, 3))
        pending.append(None)

    def pass_on(steps, done):
        made = []
        for (g, level), x in zip(steps, after([sent[g] for g, _ in steps], done)):
            x = x.astype(F32)
            low, high = x[:512], x[512:]
            if pending[g] is not None:
                low = spread(pending[g][:256]) + low
                high = spread(pending[g][256:]) + high
            pending[g] = low
            outgoing = (grads[g][level].astype(F32) + spread(high)).astype(BF)
            made.append(outgoing)
            sent[g] = partner(outgoing, level)
        return made

    level_3_to_1(0)
    made = pool_and_send([2, 3], [dqs[0]])
    (qT,) = after([qT], made)
    p_far3, w_far3, st_far3 = block_forward(3, qT, [far[3][0]])
    fars.append((w_far3, st_far3, 0))
    (qT,) = after([qT], [st_far3])
    level_3_to_1(1)
    made = pool_and_send([3], [dqs[1]]) + pass_on([(0, 2)], [dqs[1]])
    (qT,) = after([qT], made)
    level_3_to_1(2)
    made = pass_on([(0, 1), (1, 2)], [dqs[2]])
    (qT,) = after([qT], made)
    level_3_to_1(3)
    made = pass_on([(1, 1), (2, 2)], [dqs[3]])
    (attn,) = after([attn], made)
    outputs, weight_part = project(attn, gp, out_weight)
    (qT,) = after([qT], [outputs])

    def far_backward(first, p, n):
        which = range(first, first + n)
        dq, o = block_backward(
            first, qT, p, [far[g][0] for g in which], [gls[g] for g in which],
            [scales[g] for g in which], 1,
        )
        for i, g in enumerate(which):
            grads[g][0] = o[i]
        return dq

    dq_far0 = far_backward(0, p_far0, 2)
    made = pass_on([(0, 0), (1, 0), (2, 1), (3, 2)], [dq_far0])
    (qT,) = after([qT], made)
    dq_far2 = far_backward(2, p_far2, 1)
    made = pass_on([(2, 0), (3, 1)], [dq_far2])

    me = lax.axis_index("ctx")

    def halve(rows, mask, done):
        (rows,) = after([rows], done)
        n = rows.shape[0] // 2
        upper = (me // mask) % 2 == 1
        give = jnp.where(upper, rows[:n], rows[n:])
        pairs = [(source, source ^ mask) for source in range(lax.axis_size("ctx"))]
        return jnp.where(upper, rows[n:], rows[:n]), give, lax.ppermute(give, "ctx", pairs)

    weight_cols = lax.psum_scatter(weight_part, "rep", scatter_dimension=1, tiled=True)
    keep, give, come = halve(weight_cols, 8, [dq_far2])
    (qT,) = after([qT], [*made, give])
    dq_far3 = far_backward(3, p_far3, 1)
    (come,) = after([come], [dq_far3])
    keep, give, come = halve(keep + come, 4, [dq_far3])
    (qT,) = after([qT], [give])
    other = [(dq_far0, 0), (dq_far0, 1), (dq_far2, 0), (dq_far3, 0)]
    dq, o_own0 = block_backward(
        0, qT, p_own0, own[:1], gls[:1], scales[:1], 0, dqs[:1], other[:1]
    )
    made = pass_on([(3, 0)], [o_own0])
    (come,) = after([come], [o_own0])
    keep, give, come = halve(keep + come, 2, [o_own0])
    (qT,) = after([qT], [*made, give])
    dq, o_own1 = block_backward(
        1, qT, p_own1, own[1:], gls[1:], scales[1:], 0, dqs[1:], other[1:], dq
    )
    (come,) = after([come], [o_own1])
    keep, give, come = halve(keep + come, 1, [o_own1])
    got = after(sent, [o_own1, give])
    grad_keys, grad_values = finish_keys(
        [(o_own0, 0)] + [(o_own1, i) for i in range(3)], pending, got
    )
    (come,) = after([come], [grad_keys])
    grad_weight = keep + come
    return outputs[None], dq[None], grad_keys[None], grad_values[None], grad_weight


def solution(mesh):
    rows = P("rep", "ctx", None)
    return jax.shard_map(
        on_device,
        mesh=mesh,
        in_specs=(rows, rows, rows, rows, P()),
        out_specs=(rows, rows, rows, rows, P("ctx", "rep")),
        check_vma=False,
    )
```

```python
import functools

import jax
import jax.numpy as jnp
from jax import lax
from jax.experimental import pallas as pl
from jax.experimental.pallas import tpu as pltpu
from jax.sharding import PartitionSpec as P

F32 = jnp.float32
BF = jnp.bfloat16
KEYS = 1024
SLAB = 128
TW = 256
GROUPS = 4
MASKS = (1, 3, 4, 12)
NT = (((1,), (1,)), ((), ()))
NN = (((1,), (0,)), ((), ()))
LOG2E = 1.4426950408889634
CHUNK = 512
BACK = 256


def dot(a, b, dims=NN):
    return lax.dot_general(a, b, dims, preferred_element_type=F32)


def cost(us):
    return pl.CostEstimate(flops=int(us * 1.15e9), bytes_accessed=2**20, transcendentals=0)


def params(mib=58):
    return pltpu.CompilerParams(vmem_limit_bytes=mib * 2**20)


def score_keys(kv):
    k0, k1 = kv[:, 0:64], kv[:, 64:128]
    return jnp.concatenate([k0, k0, k1, k1], 1)


def grad_values_operand(kv):
    ones3 = (lax.broadcasted_iota(jnp.int32, (KEYS, 64), 1) < 3).astype(F32).astype(BF)
    return jnp.concatenate([kv[:, 128:192], ones3, kv[:, 192:256], ones3], 1)


def put_value_rows(ref, kv):
    ref[0:128] = kv[:, 128:256].T
    ref[128:144] = (lax.broadcasted_iota(jnp.int32, (16, KEYS), 0) == 0).astype(F32).astype(BF)


def put_query(qw, t, q):
    zero = jnp.zeros((128, SLAB), BF)
    qs = q.astype(F32) * (0.125 * LOG2E)
    hi = qs.astype(BF)
    lo = (qs - hi.astype(F32)).astype(BF)
    qw[t, 0:64, 0:128] = hi[0:64]
    qw[t, 64:128, 0:128] = lo[0:64]
    qw[t, 128:256, 0:128] = zero
    qw[t, 0:128, 128:256] = zero
    qw[t, 128:192, 128:256] = hi[64:128]
    qw[t, 192:256, 128:256] = lo[64:128]


def put_pair(ref, t, first, second):
    zero = jnp.zeros((64, SLAB), BF)
    off = t * TW
    ref[0:64, off : off + 128] = first
    ref[64:128, off : off + 128] = zero
    ref[0:64, off + 128 : off + 256] = zero
    ref[64:128, off + 128 : off + 256] = second


def put_scaled(qk, t, q):
    qq = (q.astype(F32) * 0.125).astype(BF)
    put_pair(qk, t, qq[0:64], qq[64:128])


def put_grad(gw, gk, t, g, scale):
    n = -scale
    hi = n.astype(BF).astype(F32)
    rest = n - hi
    mid = rest.astype(BF).astype(F32)
    row = lax.broadcasted_iota(jnp.int32, (64, TW), 0)
    low = jnp.where(row == 0, hi, jnp.where(row == 1, mid, jnp.where(row == 2, rest - mid, 0.0)))
    low = low.astype(BF)
    zero = jnp.zeros((128, SLAB), BF)
    gw[t, 0:64, 0:128] = g[:, 0:128]
    gw[t, 64:128, 0:128] = low[:, 0:128]
    gw[t, 128:256, 0:128] = zero
    gw[t, 0:128, 128:256] = zero
    gw[t, 128:192, 128:256] = g[:, 128:256]
    gw[t, 192:256, 128:256] = low[:, 128:256]
    put_pair(gk, t, g[:, 0:128], g[:, 128:256])


def both_heads(x):
    return jnp.concatenate([x[0:64, 0:128], x[64:128, 128:256]], 1)


def forward_step(nxt, cur):
    if nxt is not None:
        keys, query, sn, mn = nxt
        top = None
    if cur is not None:
        values, p_ref, off, sc, mc, w_ref, st_ref, t = cur
        m = mc[0:1]
        w = None
    for c in range(KEYS // CHUNK):
        r = slice(c * CHUNK, (c + 1) * CHUNK)
        if nxt is not None:
            s = dot(keys(r), query())
            sn[r] = s
            x = jnp.max(s.reshape(CHUNK // 8, 8, TW), axis=0)
            top = x if top is None else jnp.maximum(top, x)
        if cur is not None:
            p = jnp.exp2(sc[r] - m).astype(BF)
            p_ref(r, off, p)
            y = dot(values(r), p)
            w = y if w is None else w + y
    if nxt is not None:
        mn[0:1] = jnp.max(top, axis=0, keepdims=True)
    if cur is not None:
        w_ref(t, both_heads(w))
        st_ref(t, m, w[128:129])


def forward_tiles(count, score, value, sa, sb, ma, mb):
    forward_step(score(jnp.int32(0), sa, ma), None)

    def body(i, c):
        t = 2 * i
        forward_step(score(t + 1, sb, mb), value(t, sa, ma))
        forward_step(score(t + 2, sa, ma), value(t + 1, sb, mb))
        return c

    steps = (count - 1) // 2
    lax.fori_loop(0, steps, body, 0)
    t = jnp.int32(2 * steps)
    if count % 2 == 0:
        forward_step(score(t + 1, sb, mb), value(t, sa, ma))
        forward_step(None, value(t + 1, sb, mb))
    else:
        forward_step(None, value(t, sa, ma))


def tile_cols(t):
    if isinstance(t, int):
        return slice(t * TW, (t + 1) * TW)
    return pl.ds(pl.multiple_of(t * TW, TW), TW)


def select(refs, use):
    for i, ref in enumerate(refs):
        pl.when(pl.program_id(0) == i)(functools.partial(use, ref))


def block_forward_kernel(n, q_ref, *refs):
    kvs, (p_ref, w_ref, st_ref, kk, vT, qw, sa, sb, ma, mb) = refs[:n], refs[n:]

    def prepare(kv_ref):
        kv = kv_ref[...]
        kk[...] = score_keys(kv)
        put_value_rows(vT, kv)

    select(kvs, prepare)
    for j in range(8):
        put_query(qw, j, q_ref[:, j * SLAB : (j + 1) * SLAB])

    def put_p(r, t, p):
        p_ref[r, tile_cols(t)] = p

    def put_w(t, w):
        w_ref[t] = w

    def put_st(t, m, total):
        st_ref[t, 0:1] = m
        st_ref[t, 1:2] = total

    def score(t, s, m):
        return (lambda r: kk[r], lambda: qw[t], s, m)

    def value(t, s, m):
        return (lambda r: vT[:, r], put_p, t, s, m, put_w, put_st, t)

    forward_tiles(8, score, value, sa, sb, ma, mb)


WHOLE = pl.BlockSpec((KEYS, 256), lambda i: (0, 0))


def block_forward(first, qT, kvs):
    n = len(kvs)
    return pl.pallas_call(
        functools.partial(block_forward_kernel, n),
        grid=(n,),
        in_specs=[pl.BlockSpec((128, KEYS), lambda i: (first + i, 0))] + [WHOLE] * n,
        out_specs=[
            pl.BlockSpec((None, KEYS, 8 * TW), lambda i: (i, 0, 0)),
            pl.BlockSpec((None, 8, 64, TW), lambda i: (i, 0, 0, 0)),
            pl.BlockSpec((None, 8, 8, TW), lambda i: (i, 0, 0, 0)),
        ],
        out_shape=[
            jax.ShapeDtypeStruct((n, KEYS, 8 * TW), BF),
            jax.ShapeDtypeStruct((n, 8, 64, TW), F32),
            jax.ShapeDtypeStruct((n, 8, 8, TW), F32),
        ],
        scratch_shapes=[
            pltpu.VMEM((KEYS, 256), BF),
            pltpu.VMEM((144, KEYS), BF),
            pltpu.VMEM((8, 256, TW), BF),
            pltpu.VMEM((KEYS, TW), F32),
            pltpu.VMEM((KEYS, TW), F32),
            pltpu.VMEM((8, TW), F32),
            pltpu.VMEM((8, TW), F32),
        ],
        compiler_params=params(),
        cost_estimate=cost(5 * n),
        name="block_forward",
    )(qT, *kvs)


def backward_tiles(blocks, va, kT, qk, gw, gk, p_ref, ds_ref, dqt, outs, pieces):
    rows_of = KEYS // BACK
    items = [(b, t, c) for b, first, n in blocks for t in range(first, first + n) for c in range(rows_of)]
    ends = {first + n - 1: (b, first, n) for b, first, n in blocks}
    grads, scores, dqs, fill = {}, {}, {}, []

    def sums(b, first, n, left, right, lanes, count):
        cols = slice(first * TW, (first + n) * TW)

        def piece(rows):
            outs[b][rows, lanes] = dot(left[rows, cols], right[:, cols], NT).astype(outs[b].dtype)

        step = KEYS // count
        return [functools.partial(piece, slice(i * step, (i + 1) * step)) for i in range(count)]

    def issue(n):
        if n < len(items):
            b, t, c = items[n]
            grads[n] = dot(va(b, slice(c * BACK, (c + 1) * BACK)), gw[t])

    for block in blocks:
        fill += sums(*block, p_ref, gk, slice(128, 256), pieces)
    issue(0)
    issue(1)
    for n, (b, t, c) in enumerate(items):
        issue(n + 2)
        r = slice(c * BACK, (c + 1) * BACK)
        ds = (p_ref[r, tile_cols(t)].astype(F32) * grads.pop(n)).astype(BF)
        ds_ref[r, tile_cols(t)] = ds
        if c == 0 and fill:
            fill.pop(0)()
        y = dot(kT(b, r), ds)
        dqs[t] = y if c == 0 else dqs[t] + y
        if c == rows_of - 1:
            dqt[t] = both_heads(dqs.pop(t))
            if t in ends:
                last = t == items[-1][1]
                fill += sums(*ends[t], ds_ref, qk, slice(0, 128), 1 if last else pieces)
    while fill:
        fill.pop(0)()


FAR_TILES = 7
FAR_BLOCKS = ((0, 0, 4), (1, 4, 2), (2, 6, 1))


def far_block(t):
    one = lambda at: (t >= at).astype(jnp.int32)
    return one(4) + one(6)


def group_kernel(
    chained, q_ref, ga_ref, kv1, kv2, kv3, wa_ref, sta_ref, wb_ref, stb_ref, *refs
):
    if chained:
        refs = refs[1:]
    (
        attn_ref, dq_ref, g_ref, gs_ref, o1, o2, o3,
        kk, va, kT, vT, qw, qk, gw, gk, p_ref, ds_ref, w_ref, st_ref, dqt, sa, sb, ma, mb,
    ) = refs
    kvs, outs = (kv1, kv2, kv3), (o1, o2, o3)
    for b in range(3):
        kv = kvs[b][...]
        kk[b] = score_keys(kv)
        va[b] = grad_values_operand(kv)
        kT[b] = kv[:, 0:128].T
        put_value_rows(vT.at[b], kv)
    level = [q_ref[:, j * SLAB : (j + 1) * SLAB] for j in range(8)]
    first = 0
    for _ in range(3):
        level = [
            (0.5 * (level[2 * c].astype(F32) + level[2 * c + 1].astype(F32))).astype(BF)
            for c in range(len(level) // 2)
        ]
        for c, x in enumerate(level):
            put_query(qw, first + c, x)
            put_scaled(qk, first + c, x)
        first += len(level)

    def put_p(r, t, p):
        p_ref[r, tile_cols(t)] = p

    def put_w(t, w):
        w_ref[t] = w

    def put_st(t, m, total):
        st_ref[t, 0:1] = m
        st_ref[t, 1:2] = total

    def score(t, s, m):
        b = far_block(t)
        return (lambda r: kk[b, r], lambda: qw[t], s, m)

    def value(t, s, m):
        b = far_block(t)
        return (lambda r: vT[b, :, r], put_p, t, s, m, put_w, put_st, t)

    forward_tiles(FAR_TILES, score, value, sa, sb, ma, mb)

    gl, gs = [None] * FAR_TILES, [None] * FAR_TILES
    for j in range(8):
        ts = [j // 2, 4 + j // 4, 6]
        ms = [sta_ref[j, 0:1], stb_ref[j, 0:1]] + [st_ref[t, 0:1] for t in ts]
        totals = [sta_ref[j, 1:2], stb_ref[j, 1:2]] + [st_ref[t, 1:2] for t in ts]
        ws = [wa_ref[j], wb_ref[j]] + [w_ref[t] for t in ts]
        top = functools.reduce(jnp.maximum, ms)
        factors = [jnp.exp2(m - top) * c for m, c in zip(ms, (1.0, 1.0, 2.0, 4.0, 8.0))]
        inv = 1.0 / functools.reduce(jnp.add, [f * x for f, x in zip(factors, totals)])
        shares = [f * inv for f in factors]
        at = functools.reduce(jnp.add, [s * w for s, w in zip(shares, ws)]).astype(BF)
        cols = slice(j * SLAB, (j + 1) * SLAB)
        attn_ref[0:64, cols] = at[:, 0:128]
        attn_ref[64:128, cols] = at[:, 128:256]
        ga = jnp.concatenate([ga_ref[0:64, cols], ga_ref[64:128, cols]], 1).astype(F32)
        delta = jnp.sum(ga * at.astype(F32), axis=0, keepdims=True)
        for side in range(2):
            g_ref[side, j] = (shares[side] * ga).astype(BF)
            gs_ref[side, j, 0:1] = shares[side] * delta
        for s, t in zip(shares[2:], ts):
            x, y = s * ga, s * delta
            gl[t] = x if gl[t] is None else gl[t] + x
            gs[t] = y if gs[t] is None else gs[t] + y
    for t in range(FAR_TILES):
        put_grad(gw, gk, t, gl[t].astype(BF), gs[t])

    backward_tiles(
        FAR_BLOCKS, lambda b, r: va[b, r], lambda b, r: kT[b, :, r],
        qk, gw, gk, p_ref, ds_ref, dqt, outs, 4,
    )
    for j in range(8):
        dq_ref[j] = 0.5 * dqt[j // 2] + 0.25 * dqt[4 + j // 4] + 0.125 * dqt[6]


def group(g, qT, gaT, kvs, own, far, attn):
    cols = pl.BlockSpec((128, KEYS), lambda i: (g, 0))
    tiles = lambda rows: pl.BlockSpec((2, 8, rows, TW), lambda i: (0, 0, 0, 0))
    at = lambda place, rows: pl.BlockSpec((None, 8, rows, TW), lambda i: (place, 0, 0, 0))
    chain = [] if attn is None else [attn]
    return pl.pallas_call(
        functools.partial(group_kernel, bool(chain)),
        grid=(1,),
        in_specs=[cols, cols]
        + [WHOLE] * 3
        + [at(own[2], 64), at(own[2], 8), at(far[2], 64), at(far[2], 8)]
        + [pl.BlockSpec(memory_space=pl.ANY) for _ in chain],
        out_specs=[cols, pl.BlockSpec((8, 64, TW), lambda i: (0, 0, 0)), tiles(64), tiles(8)]
        + [WHOLE] * 3,
        out_shape=[
            jax.ShapeDtypeStruct((512, KEYS), BF),
            jax.ShapeDtypeStruct((8, 64, TW), F32),
            jax.ShapeDtypeStruct((2, 8, 64, TW), BF),
            jax.ShapeDtypeStruct((2, 8, 8, TW), F32),
        ]
        + [jax.ShapeDtypeStruct((KEYS, 256), BF)] * 3,
        scratch_shapes=[
            pltpu.VMEM((3, KEYS, 256), BF),
            pltpu.VMEM((3, KEYS, 256), BF),
            pltpu.VMEM((3, 128, KEYS), BF),
            pltpu.VMEM((3, 144, KEYS), BF),
            pltpu.VMEM((FAR_TILES, 256, TW), BF),
            pltpu.VMEM((128, FAR_TILES * TW), BF),
            pltpu.VMEM((FAR_TILES, 256, TW), BF),
            pltpu.VMEM((128, FAR_TILES * TW), BF),
            pltpu.VMEM((KEYS, FAR_TILES * TW), BF),
            pltpu.VMEM((KEYS, FAR_TILES * TW), BF),
            pltpu.VMEM((FAR_TILES, 64, TW), F32),
            pltpu.VMEM((FAR_TILES, 8, TW), F32),
            pltpu.VMEM((FAR_TILES, 64, TW), F32),
            pltpu.VMEM((KEYS, TW), F32),
            pltpu.VMEM((KEYS, TW), F32),
            pltpu.VMEM((8, TW), F32),
            pltpu.VMEM((8, TW), F32),
        ],
        input_output_aliases={9: 0} if chain else {},
        compiler_params=params(),
        cost_estimate=cost(16),
        name="group",
    )(qT, gaT, *kvs, *own[:2], *far[:2], *chain)


def block_backward_kernel(n, last, chained, q_ref, p_ref, *refs):
    take = lambda: (refs[:n], refs[n:])
    kvs, refs = take()
    gls, refs = take()
    scales, refs = take()
    if last:
        upper, refs = take()
        other, refs = take()
    if chained:
        refs = refs[1:]
    dq_ref, o_ref, va, kT, qk, gw, gk, ds_ref, dqt, tmp = refs
    for i in range(n):

        @pl.when(pl.program_id(0) == i)
        def _(i=i):
            kv = kvs[i][...]
            va[...] = grad_values_operand(kv)
            kT[...] = kv[:, 0:128].T
            for j in range(8):
                put_grad(gw, gk, j, gls[i][j], scales[i][j, 0:1])

    for j in range(8):
        put_scaled(qk, j, q_ref[:, j * SLAB : (j + 1) * SLAB])

    backward_tiles(
        ((0, 0, 8),), lambda b, r: va[r], lambda b, r: kT[:, r],
        qk, gw, gk, p_ref, ds_ref, dqt, (o_ref,), 8,
    )
    if not last:
        dq_ref[...] = dqt[...]
        return
    for i in range(n):

        @pl.when(pl.program_id(0) == i)
        def _(i=i):
            for j in range(8):
                dqt[j] = dqt[j] + upper[i][j] + other[i][j]

    for j in range(8):
        d = 0.125 * dqt[j]
        tmp[pl.ds(j, SLAB, stride=8), :] = jnp.concatenate([d[:, 0:128], d[:, 128:256]], 0).T
    dq_ref[...] = tmp[...].astype(BF)


def block_backward(first, qT, p, kvs, gls, scales, side, upper=None, other=None, dq=None):
    n = len(kvs)
    last = upper is not None
    chain = [] if dq is None else [dq]
    of_side = lambda rows: pl.BlockSpec((None, 8, rows, TW), lambda i: (side, 0, 0, 0))
    at = lambda place: pl.BlockSpec((None, 8, 64, TW), lambda i: (place, 0, 0, 0))
    in_specs = [
        pl.BlockSpec((128, KEYS), lambda i: (first + i, 0)),
        pl.BlockSpec((None, KEYS, 8 * TW), lambda i: (i, 0, 0)),
    ]
    in_specs += [WHOLE] * n + [of_side(64)] * n + [of_side(8)] * n
    args = [qT, p, *kvs, *gls, *scales]
    if last:
        in_specs += [pl.BlockSpec((8, 64, TW), lambda i: (0, 0, 0))] * n
        in_specs += [at(place) for _, place in other]
        args += [*upper, *[part for part, _ in other]]
        dq_spec = pl.BlockSpec((KEYS, 128), lambda i: (0, first + i))
        dq_shape = jax.ShapeDtypeStruct((KEYS, 512), BF)
    else:
        dq_spec = pl.BlockSpec((None, 8, 64, TW), lambda i: (i, 0, 0, 0))
        dq_shape = jax.ShapeDtypeStruct((n, 8, 64, TW), F32)
    in_specs += [pl.BlockSpec(memory_space=pl.ANY) for _ in chain]
    return pl.pallas_call(
        functools.partial(block_backward_kernel, n, last, bool(chain)),
        grid=(n,),
        in_specs=in_specs,
        out_specs=[dq_spec, pl.BlockSpec((None, KEYS, 256), lambda i: (i, 0, 0))],
        out_shape=[dq_shape, jax.ShapeDtypeStruct((n, KEYS, 256), F32 if last else BF)],
        scratch_shapes=[
            pltpu.VMEM((KEYS, 256), BF),
            pltpu.VMEM((128, KEYS), BF),
            pltpu.VMEM((128, 8 * TW), BF),
            pltpu.VMEM((8, 256, TW), BF),
            pltpu.VMEM((128, 8 * TW), BF),
            pltpu.VMEM((KEYS, 8 * TW), BF),
            pltpu.VMEM((8, 64, TW), F32),
            pltpu.VMEM((KEYS, 128), F32),
        ],
        input_output_aliases={len(args): 0} if chain else {},
        compiler_params=params(),
        cost_estimate=cost(10 * n),
        name="block_backward",
    )(*args, *chain)


def keys_kernel(k_ref, v_ref, o0, o1, o2, o3, tmp):
    outs = (o0, o1, o2, o3)
    for part, src in enumerate((k_ref, v_ref)):
        for g in range(GROUPS):
            tmp[...] = src[:, g * 128 : (g + 1) * 128].astype(F32)
            for b in range(8):
                outs[g][b * SLAB : (b + 1) * SLAB, part * 128 : (part + 1) * 128] = tmp[
                    pl.ds(b, SLAB, stride=8), :
                ].astype(BF)


def prep_keys(k, v):
    return pl.pallas_call(
        keys_kernel,
        out_shape=[jax.ShapeDtypeStruct((KEYS, 256), BF)] * GROUPS,
        scratch_shapes=[pltpu.VMEM((KEYS, 128), F32)],
        compiler_params=params(),
        cost_estimate=cost(3),
        name="prep_keys",
    )(k, v)


def rows_kernel(q_ref, go_ref, w_ref, qT_ref, gaT_ref, gp_ref, tmp):
    for g in range(GROUPS):
        tmp[...] = q_ref[:, g * 128 : (g + 1) * 128].astype(F32)
        for b in range(8):
            x = tmp[pl.ds(b, SLAB, stride=8), :]
            qT_ref[g * 128 : (g + 1) * 128, b * SLAB : (b + 1) * SLAB] = x.T.astype(BF)
    for c in range(8):
        tmp[...] = go_ref[:, c * 128 : (c + 1) * 128].astype(F32)
        for b in range(8):
            gp_ref[b * SLAB : (b + 1) * SLAB, c * 128 : (c + 1) * 128] = tmp[
                pl.ds(b, SLAB, stride=8), :
            ].astype(BF)
    for c in range(4):
        rows = pl.ds(c * 256, 256)
        gaT_ref[:, c * 256 : (c + 1) * 256] = dot(w_ref[...], gp_ref[rows, :], NT).astype(BF)


def prep_rows(q, go, w):
    return pl.pallas_call(
        rows_kernel,
        out_shape=[
            jax.ShapeDtypeStruct((512, KEYS), BF),
            jax.ShapeDtypeStruct((512, KEYS), BF),
            jax.ShapeDtypeStruct((KEYS, 1024), BF),
        ],
        scratch_shapes=[pltpu.VMEM((KEYS, 128), F32)],
        compiler_params=params(),
        cost_estimate=cost(6),
        name="prep_rows",
    )(q, go, w)


def project_kernel(attn_ref, gp_ref, w_ref, out_ref, gw_ref, at, tmp):
    for g in range(GROUPS):
        rows = slice(g * 128, (g + 1) * 128)
        at[:, rows] = attn_ref[rows, :].T
        gw_ref[rows, :] = dot(attn_ref[rows, :], gp_ref[...])
    for c in range(8):
        for b in range(8):
            tmp[pl.ds(b, SLAB, stride=8), :] = dot(
                at[b * SLAB : (b + 1) * SLAB, :], w_ref[:, c * 128 : (c + 1) * 128]
            )
        out_ref[:, c * 128 : (c + 1) * 128] = tmp[...].astype(BF)


def project(attn, gp, w):
    return pl.pallas_call(
        project_kernel,
        out_shape=[
            jax.ShapeDtypeStruct((KEYS, 1024), BF),
            jax.ShapeDtypeStruct((512, 1024), F32),
        ],
        scratch_shapes=[pltpu.VMEM((KEYS, 512), BF), pltpu.VMEM((KEYS, 128), F32)],
        compiler_params=params(),
        cost_estimate=cost(7),
        name="project",
    )(attn, gp, w)


def finish_kernel(*refs):
    parts, (dk_ref, dv_ref, tmp) = refs[: 3 * GROUPS], refs[3 * GROUPS :]
    for g in range(GROUPS):
        own, kept, got = parts[3 * g : 3 * g + 3]
        for part, out in enumerate((dk_ref, dv_ref)):
            cols = slice(part * 128, (part + 1) * 128)
            for b in range(8):
                rows = slice(b * SLAB, (b + 1) * SLAB)
                half = slice(b // 2 * SLAB, (b // 2 + 1) * SLAB)
                tmp[pl.ds(b, SLAB, stride=8), :] = (
                    own[rows, cols] + 0.5 * kept[half, cols] + got[rows, cols].astype(F32)
                )
            out[:, g * 128 : (g + 1) * 128] = tmp[...].astype(BF)


def finish_keys(owns, kept, got):
    in_specs, args = [], []
    for (own, place), x, y in zip(owns, kept, got):
        in_specs.append(pl.BlockSpec((None, KEYS, 256), lambda i, place=place: (place, 0, 0)))
        in_specs += [pl.BlockSpec((512, 256), lambda i: (0, 0)), WHOLE]
        args += [own, x, y]
    return pl.pallas_call(
        finish_kernel,
        grid=(1,),
        in_specs=in_specs,
        out_specs=[pl.BlockSpec((KEYS, 512), lambda i: (0, 0))] * 2,
        out_shape=[jax.ShapeDtypeStruct((KEYS, 512), BF)] * 2,
        scratch_shapes=[pltpu.VMEM((KEYS, 128), F32)],
        compiler_params=params(),
        cost_estimate=cost(5),
        name="finish_keys",
    )(*args)


def partner(value, level):
    mask = MASKS[level]
    pairs = [(source, source ^ mask) for source in range(lax.axis_size("ctx"))]
    return lax.ppermute(value, "ctx", pairs)


def pool(x):
    y = x.astype(F32).reshape(4, 2, SLAB, 256)
    return (0.5 * (y[:, 0] + y[:, 1])).astype(BF).reshape(512, 256)


def spread(x):
    n = x.shape[0] // SLAB
    y = jnp.broadcast_to((0.5 * x).reshape(n, 1, SLAB, 256), (n, 2, SLAB, 256))
    return y.reshape(2 * x.shape[0], 256)


def after(values, done):
    out = lax.optimization_barrier((*values, *done))
    return list(out[: len(values)])


def on_device(queries, key_states, value_states, grad_out, out_weight):
    held = [[x] for x in prep_keys(key_states[0], value_states[0])]
    far = [[] for _ in held]

    def send(g):
        far[g].append(partner(held[g][-1], len(far[g])))

    def pool_and_send(which, done):
        for g, x in zip(which, after([far[g][-1] for g in which], done)):
            far[g][-1] = x
            held[g].append(jnp.concatenate([pool(held[g][-1]), pool(x)], 0))
        made = [held[g][-1] for g in which]
        for g in which:
            send(g)
        return made

    own = [h[0] for h in held]
    for g in range(GROUPS):
        send(g)
    qT, gaT, gp = prep_rows(queries[0], grad_out[0], out_weight)

    p_own0, w_own0, st_own0 = block_forward(0, qT, own[:1])
    made = pool_and_send([0], [st_own0])
    (qT,) = after([qT], made)
    p_own1, w_own1, st_own1 = block_forward(1, qT, own[1:])
    made = pool_and_send([0, 1], [st_own1])
    (qT,) = after([qT], made)
    p_far0, w_far0, st_far0 = block_forward(0, qT, [far[0][0], far[1][0]])
    made = pool_and_send([0, 1, 2], [st_far0])
    (qT,) = after([qT], made)
    p_far2, w_far2, st_far2 = block_forward(2, qT, [far[2][0]])
    made = pool_and_send([1, 2, 3], [st_far2])
    (qT,) = after([qT], made)

    owns = [(w_own0, st_own0, 0)] + [(w_own1, st_own1, i) for i in range(3)]
    fars = [(w_far0, st_far0, 0), (w_far0, st_far0, 1), (w_far2, st_far2, 0)]
    attn = None
    dqs, gls, scales, grads, pending, sent = [], [], [], [], [], []

    def level_3_to_1(g):
        nonlocal attn
        attn, dq, gl, gs, f1, f2, f3 = group(g, qT, gaT, far[g][1:], owns[g], fars[g], attn)
        dqs.append(dq)
        gls.append(gl)
        scales.append(gs)
        grads.append([None, f1, f2, f3])
        sent.append(partner(f3, 3))
        pending.append(None)

    def pass_on(steps, done):
        made = []
        for (g, level), x in zip(steps, after([sent[g] for g, _ in steps], done)):
            low, high = x[:512].astype(F32), x[512:].astype(F32)
            if pending[g] is not None:
                low = spread(pending[g][:256]) + low
                high = spread(pending[g][256:]) + high
            pending[g] = low
            outgoing = (grads[g][level].astype(F32) + spread(high)).astype(BF)
            made.append(outgoing)
            sent[g] = partner(outgoing, level)
        return made

    level_3_to_1(0)
    made = pool_and_send([2, 3], [dqs[0]])
    (qT,) = after([qT], made)
    level_3_to_1(1)
    made = pool_and_send([3], [dqs[1]])
    (qT,) = after([qT], made)
    p_far3, w_far3, st_far3 = block_forward(3, qT, [far[3][0]])
    fars.append((w_far3, st_far3, 0))
    made = pass_on([(0, 2)], [st_far3])
    (qT,) = after([qT], made)
    level_3_to_1(2)
    made = pass_on([(0, 1), (1, 2)], [dqs[2]])
    (qT,) = after([qT], made)
    level_3_to_1(3)
    made = pass_on([(1, 1), (2, 2)], [dqs[3]])
    (attn,) = after([attn], made)
    outputs, weight_part = project(attn, gp, out_weight)
    (qT,) = after([qT], [outputs])

    def far_backward(first, p, n):
        which = range(first, first + n)
        dq, o = block_backward(
            first, qT, p, [far[g][0] for g in which], [gls[g] for g in which],
            [scales[g] for g in which], 1,
        )
        for i, g in enumerate(which):
            grads[g][0] = o[i]
        return dq

    dq_far0 = far_backward(0, p_far0, 2)
    made = pass_on([(0, 0), (1, 0), (2, 1), (3, 2)], [dq_far0])
    (qT,) = after([qT], made)
    dq_far2 = far_backward(2, p_far2, 1)
    made = pass_on([(2, 0)], [dq_far2])

    me = lax.axis_index("ctx")

    def halve(rows, mask, done):
        (rows,) = after([rows], done)
        n = rows.shape[0] // 2
        upper = (me // mask) % 2 == 1
        give = jnp.where(upper, rows[:n], rows[n:])
        pairs = [(source, source ^ mask) for source in range(lax.axis_size("ctx"))]
        return jnp.where(upper, rows[n:], rows[:n]), give, lax.ppermute(give, "ctx", pairs)

    weight_cols = lax.psum_scatter(weight_part, "rep", scatter_dimension=1, tiled=True)
    keep, give, come = halve(weight_cols, 8, [dq_far2])
    (qT,) = after([qT], [*made, give])
    dq_far3 = far_backward(3, p_far3, 1)
    (come,) = after([come], [dq_far3])
    made = pass_on([(3, 1)], [dq_far3])
    keep, give, come = halve(keep + come, 4, [dq_far3])
    (qT,) = after([qT], [*made, give])
    other = [(dq_far0, 0), (dq_far0, 1), (dq_far2, 0), (dq_far3, 0)]
    dq, o_own0 = block_backward(
        0, qT, p_own0, own[:1], gls[:1], scales[:1], 0, dqs[:1], other[:1]
    )
    made = pass_on([(3, 0)], [o_own0])
    (come,) = after([come], [o_own0])
    keep, give, come = halve(keep + come, 2, [o_own0])
    (qT,) = after([qT], [*made, give])
    dq, o_own1 = block_backward(
        1, qT, p_own1, own[1:], gls[1:], scales[1:], 0, dqs[1:], other[1:], dq
    )
    (come,) = after([come], [o_own1])
    keep, give, come = halve(keep + come, 1, [o_own1])
    got = after(sent, [o_own1, give])
    grad_keys, grad_values = finish_keys(
        [(o_own0, 0)] + [(o_own1, i) for i in range(3)], pending, got
    )
    (come,) = after([come], [grad_keys])
    grad_weight = keep + come
    return outputs[None], dq[None], grad_keys[None], grad_values[None], grad_weight


def solution(mesh):
    rows = P("rep", "ctx", None)
    return jax.shard_map(
        on_device,
        mesh=mesh,
        in_specs=(rows, rows, rows, rows, P()),
        out_specs=(rows, rows, rows, rows, P("ctx", "rep")),
        check_vma=False,
    )
```
